32 devices in a mesh: dp: 8 (over y, x, core), tensor: 4 (over z).
Axes of the slice: x: 2, y: 2, z: 4, core: 2. Of those that a mesh axis runs over, the one named last changes fastest.
Arguments:
- tokens: bfloat16 [2048, 2560], P('dp'), may hold values from -6 to 6
- segments: int32 [2048], P('dp'), may hold values from 0 to 2047, as said below
- first_gain: float32 [2560], replicated, may hold values from 0.5 to 1.5
- x_weight: bfloat16 [2560, 10, 256], P('dp', None, 'tensor'), may hold values from -0.125 to 0.125
- y_weight: bfloat16 [2560, 10, 256], P('dp', None, 'tensor'), may hold values from -0.125 to 0.125
- conv_weight: float32 [4, 10, 256], P(None, None, 'tensor'), may hold values from -3 to 3
- conv_bias: float32 [10, 256], P(None, 'tensor'), may hold values from -3 to 3
- rate_weight: bfloat16 [10, 256, 256], P(None, None, 'tensor'), may hold values from -0.375 to 0.375
- input_weight: bfloat16 [10, 256, 256], P(None, None, 'tensor'), may hold values from -0.375 to 0.375
- rate_bias: float32 [10, 256], P(None, 'tensor'), may hold values from -4 to 4
- input_bias: float32 [10, 256], P(None, 'tensor'), may hold values from -4 to 4
- decay_logit: float32 [10, 256], P(None, 'tensor'), may hold values from 0.5 to 7
- out_weight: bfloat16 [10, 256, 2560], P(None, 'tensor', 'dp'), may hold values from -0.3125 to 0.3125
- second_gain: float32 [2560], replicated, may hold values from 0.5 to 1.5
- gate_weight: bfloat16 [2560, 7680], P('dp', 'tensor'), may hold values from -0.125 to 0.125
- up_weight: bfloat16 [2560, 7680], P('dp', 'tensor'), may hold values from -0.125 to 0.125
- down_weight: bfloat16 [7680, 2560], P('tensor', 'dp'), may hold values from -0.125 to 0.125
- cotangent: bfloat16 [2048, 2560], P('dp'), may hold values from -6 to 6
Outputs:
- block_out: bfloat16 [2048, 2560], P('dp')
- tokens_grad: float32 [2048, 2560], P('dp')
- first_gain_grad: float32 [2560], replicated
- x_weight_grad: float32 [2560, 10, 256], P('dp', None, 'tensor')
- y_weight_grad: float32 [2560, 10, 256], P('dp', None, 'tensor')
- conv_weight_grad: float32 [4, 10, 256], P(None, None, 'tensor')
- conv_bias_grad: float32 [10, 256], P(None, 'tensor')
- rate_weight_grad: float32 [10, 256, 256], P(None, None, 'tensor')
- input_weight_grad: float32 [10, 256, 256], P(None, None, 'tensor')
- rate_bias_grad: float32 [10, 256], P(None, 'tensor')
- input_bias_grad: float32 [10, 256], P(None, 'tensor')
- decay_logit_grad: float32 [10, 256], P(None, 'tensor')
- out_weight_grad: float32 [10, 256, 2560], P(None, 'tensor', 'dp')
- second_gain_grad: float32 [2560], replicated
- gate_weight_grad: float32 [2560, 7680], P('dp', 'tensor')
- up_weight_grad: float32 [2560, 7680], P('dp', 'tensor')
- down_weight_grad: float32 [7680, 2560], P('tensor', 'dp')
The draws below stay inside these ranges and needn't reach their ends.
Inputs may be any that keep to these rules, and one draw needn't show every extreme that they name: `segments`: each aligned block of 256 tokens holds whole sequences: a token's value is the index of the first token of its sequence, values never fall, a sequence begins at the first token of every block, the last token of all forms a sequence of its own, and in some block other than the last one sequence fills all 256 tokens.
All inputs are finite; a program needn't handle non-finite values.
Results may differ from the reference program's by a relative error of at most 0.01.
Values may be sent and summed in bfloat16 or wider, within the bound.
No kernel may reach another device: no remote copies, remote signals or barrier semaphores. Data moves between devices by JAX's collectives and lax.ppermute only.
A program may use at most 256 MiB of HBM per device.

```python
import jax
import jax.numpy as jnp
from jax import lax

D = 2560
HEADS = 10
HEAD_W = 256
FF = 7680
CONV = 4
TOK_DEV = 256
CH = 2560
TOKENS = 2048
N_DP = 8


def draw_segments(key, part):
    key = jax.random.fold_in(key, 7)
    first_key, second_key = jax.random.split(key)
    places = jnp.arange(TOKENS, dtype=jnp.int32)
    local = places % TOK_DEV
    owner = places // TOK_DEV
    whole_dev = jax.random.randint(first_key, (), 0, N_DP - 1)
    coins = jax.random.randint(second_key, (TOKENS,), 0, TOK_DEV)
    begins = (coins < 4) | (local == 0) | (places == TOKENS - 1)
    begins = jnp.where(owner == whole_dev, local == 0, begins)
    marks = jnp.where(begins, places, 0)
    return lax.cummax(marks, axis=0).astype(jnp.int32)


def spiked(entries, key, source, target, shards_of, factor):
    def block_of(position):
        return (jnp.arange(entries.shape[position]) // (entries.shape[position] // shards_of)).reshape((-1,) + (1,) * (entries.ndim - 1 - position))

    one_side = jax.random.permutation(key, shards_of)[block_of(target)]
    far = (block_of(target) + shards_of // 2) % shards_of
    return jnp.where((block_of(source) == one_side) | (block_of(source) == far), factor * entries, entries)


def level_of(stream_key, shape, cuts, smallest, high):
    gain, own = 1.0, jax.random.fold_in(stream_key, 6)
    for position, shards_of in cuts:
        steps = jnp.exp(jax.random.uniform(jax.random.fold_in(own, position), (shards_of,), jnp.float32, smallest / len(cuts), high / len(cuts)))
        gain = gain * jnp.repeat(steps, shape[position] // shards_of).reshape([-1 if axis == position else 1 for axis in range(len(shape))])
    return gain


def gaussian(key, shape, deviation, most, cuts=(), held_as=jnp.bfloat16):
    entries = deviation * jax.random.normal(key, shape, jnp.float32)
    if cuts:
        entries = entries * level_of(key, shape, cuts, -0.22, 0.18)
    return jnp.clip(entries, -most, most).astype(held_as)


def gaussian_with(rng, extent, spread, limit, pieces, heavy, kind=jnp.bfloat16):
    drawn = spread * jax.random.normal(rng, extent, jnp.float32)
    if pieces:
        drawn = drawn * level_of(rng, extent, pieces, -0.22, 0.18)
    return jnp.clip(spiked(drawn, jax.random.fold_in(rng, 3), *heavy), -limit, limit).astype(kind)


def setup_inputs(seed: int = 0) -> dict:
    key_of = jax.random.split(jax.random.key(seed), 19)
    tokens = gaussian(key_of[0], (TOKENS, D), 1.0, 6.0, ((0, 8),))
    segments = draw_segments(jax.random.fold_in(key_of[18], 71), 0)
    first_gain = jnp.clip(1.0 + 0.1 * jax.random.normal(key_of[2], (D,), jnp.float32), 0.5, 1.5)
    x_weight = gaussian(key_of[3], (D, HEADS, HEAD_W), D ** -0.5, 0.125, ((0, 8), (2, 4)))
    y_weight = gaussian(key_of[4], (D, HEADS, HEAD_W), D ** -0.5, 0.125, ((0, 8), (2, 4)))
    conv_weight = gaussian(key_of[5], (CONV, HEADS, HEAD_W), 0.5, 3.0, ((2, 4),), jnp.float32)
    conv_bias = gaussian(key_of[6], (HEADS, HEAD_W), 0.5, 3.0, ((1, 4),), jnp.float32)
    rate_weight = gaussian(key_of[7], (HEADS, HEAD_W, HEAD_W), HEAD_W ** -0.5, 0.375, ((2, 4),))
    input_weight = gaussian(key_of[8], (HEADS, HEAD_W, HEAD_W), HEAD_W ** -0.5, 0.375, ((2, 4),))
    rate_bias = gaussian(key_of[9], (HEADS, HEAD_W), 1.0, 4.0, ((1, 4),), jnp.float32)
    input_bias = gaussian(key_of[10], (HEADS, HEAD_W), 1.0, 4.0, ((1, 4),), jnp.float32)
    decay_logit = jnp.clip(0.5 + 6.5 * jax.random.uniform(key_of[11], (HEADS, HEAD_W), jnp.float32) ** level_of(key_of[11], (HEADS, HEAD_W), ((1, 4),), -0.2, 0.2), 0.5, 7.0)
    out_weight = gaussian(key_of[12], (HEADS, HEAD_W, D), (CH // 8) ** -0.5, 0.3125, ((1, 4), (2, 8)))
    second_gain = jnp.clip(1.0 + 0.1 * jax.random.normal(key_of[13], (D,), jnp.float32), 0.5, 1.5)
    gate_weight = gaussian(key_of[14], (D, FF), D ** -0.5, 0.125, ((0, 8), (1, 4)))
    up_weight = gaussian(key_of[15], (D, FF), D ** -0.5, 0.125, ((0, 8), (1, 4)))
    down_weight = gaussian(key_of[16], (FF, D), (FF // 4) ** -0.5, 0.125, ((0, 4), (1, 8)))
    cotangent = gaussian_with(key_of[17], (TOKENS, D), 1.0, 6.0, ((0, 8),), (0, 1, 8, 2.0))
    return dict(tokens=tokens, segments=segments, first_gain=first_gain, x_weight=x_weight, y_weight=y_weight, conv_weight=conv_weight, conv_bias=conv_bias, rate_weight=rate_weight, input_weight=input_weight, rate_bias=rate_bias, input_bias=input_bias, decay_logit=decay_logit, out_weight=out_weight, second_gain=second_gain, gate_weight=gate_weight, up_weight=up_weight, down_weight=down_weight, cotangent=cotangent)


eps = 1e-06
highest = lax.Precision.HIGHEST

@jax.custom_vjp
def low(v):
    return lax.optimization_barrier(v.astype(jnp.bfloat16)).astype(jnp.float32)

@jax.custom_vjp
def low_back(v):
    return v

def low_keep(v):
    return (low(v), None)

def low_pass(kept, grad):
    return (grad,)

def back_keep(v):
    return (v, None)

def back_low(kept, grad):
    return (low(grad),)
low.defvjp(low_keep, low_pass)
low_back.defvjp(back_keep, back_low)

def rms_norm(values, norm_gain):
    inv_root = lax.rsqrt(lax.optimization_barrier(jnp.mean(values * values, axis=-1, keepdims=True)) + eps)
    return values * inv_root * norm_gain

def pair_combine(earlier, later):
    return (earlier[0] * later[0], later[0] * earlier[1] + later[1])

def shift_down(values, steps):
    filler = jnp.zeros((steps,) + values.shape[1:], values.dtype)
    return jnp.concatenate([filler, values[:-steps]], axis=0)

def conv_apply(x_branch, conv_flat, bias_flat, same_masks):
    result = x_branch * conv_flat[0] + bias_flat
    for lag_step in range(1, conv_flat.shape[0]):
        result = result + shift_down(x_branch, lag_step) * same_masks[lag_step - 1] * conv_flat[lag_step]
    return result

def lru_inputs(conv_value, pre_rate, pre_entry, decay_flat, start_col):
    rate_gate = jax.nn.sigmoid(pre_rate)
    entry_gate = jax.nn.sigmoid(pre_entry)
    log_decay = -8.0 * rate_gate * jax.nn.softplus(-decay_flat)
    scaled = jnp.where(start_col, 1.0, jnp.sqrt(-jnp.expm1(2.0 * log_decay)))
    carried = jnp.where(start_col, 0.0, jnp.exp(log_decay))
    return (carried, conv_value * entry_gate * scaled)

def block_forward(x_rows, seg_rows, params):
    first_gain, x_weight, y_weight, conv_weight, conv_bias, rate_weight, input_weight, rate_bias, input_bias, decay_logit, out_weight, second_gain, gate_weight, up_weight, down_weight = params
    row_count = x_rows.shape[0]
    earlier_ids = [jnp.concatenate([jnp.full((lag_step,), -1, jnp.int32), seg_rows[:-lag_step]]) for lag_step in range(1, CONV)]
    same_masks = [(earlier == seg_rows).astype(jnp.float32)[:, None] for earlier in earlier_ids]
    start_col = (earlier_ids[0] != seg_rows)[:, None]
    normed_first = low(rms_norm(x_rows, first_gain))
    x_branch = low_back(jnp.dot(normed_first, x_weight.reshape(D, CH), precision=highest))
    y_branch = low_back(jnp.dot(normed_first, y_weight.reshape(D, CH), precision=highest))
    conv_out = low(conv_apply(x_branch, conv_weight.reshape(CONV, CH), conv_bias.reshape(CH), same_masks))
    block_heads = conv_out.reshape(row_count, HEADS, HEAD_W)
    pre_rate = low_back(jnp.einsum('thi,hij->thj', block_heads, rate_weight, precision=highest).reshape(row_count, CH) + rate_bias.reshape(CH))
    pre_entry = low_back(jnp.einsum('thi,hij->thj', block_heads, input_weight, precision=highest).reshape(row_count, CH) + input_bias.reshape(CH))
    carried, driven = lru_inputs(conv_out, pre_rate, pre_entry, decay_logit.reshape(CH), start_col)
    _, hidden = lax.associative_scan(pair_combine, (carried, driven), axis=0)
    mixed = low(hidden * jax.nn.gelu(y_branch))
    recurrent = low_back(jnp.dot(mixed, out_weight.reshape(CH, D), precision=highest))
    residual = x_rows + recurrent
    normed_second = low(rms_norm(residual, second_gain))
    gate_pre = low_back(jnp.dot(normed_second, gate_weight, precision=highest))
    up_pre = low_back(jnp.dot(normed_second, up_weight, precision=highest))
    ffn_mid = low(jax.nn.gelu(gate_pre) * up_pre)
    ffn_out = low_back(jnp.dot(ffn_mid, down_weight, precision=highest))
    return residual + ffn_out

def reference(tokens, segments, first_gain, x_weight, y_weight, conv_weight, conv_bias, rate_weight, input_weight, rate_bias, input_bias, decay_logit, out_weight, second_gain, gate_weight, up_weight, down_weight, cotangent):
    params = tuple((member.astype(jnp.float32) for member in (first_gain, x_weight, y_weight, conv_weight, conv_bias, rate_weight, input_weight, rate_bias, input_bias, decay_logit, out_weight, second_gain, gate_weight, up_weight, down_weight)))
    blocks = tokens.astype(jnp.float32).reshape(N_DP, TOK_DEV, D)
    seg_blocks = segments.reshape(N_DP, TOK_DEV)
    checked = jax.checkpoint(block_forward)

    def whole_pass(block_values, param_values):

        def one_block(packed):
            return checked(packed[0], packed[1], param_values)
        return lax.map(one_block, (block_values, seg_blocks))
    result, pull_back = jax.vjp(whole_pass, blocks, params)
    grad_blocks, grads = pull_back(cotangent.astype(jnp.float32).reshape(N_DP, TOK_DEV, D))
    return (result.reshape(TOKENS, D).astype(jnp.bfloat16), grad_blocks.reshape(TOKENS, D), grads[0], grads[1], grads[2], grads[3], grads[4], grads[5], grads[6], grads[7], grads[8], grads[9], grads[10], grads[11], grads[12], grads[13], grads[14])
```

```python
from functools import partial

import jax
import jax.numpy as jnp
from jax import lax
from jax.experimental import pallas as pl
from jax.experimental.pallas import tpu as pltpu
from jax.sharding import PartitionSpec as P

eps = 1e-06
f32 = jnp.float32
bf16 = jnp.bfloat16
vmem = pl.BlockSpec(memory_space=pltpu.VMEM)
smem = pl.BlockSpec(memory_space=pltpu.SMEM)
MIB = 1024 * 1024
chunk_count = 3


def nn(a, b):
    return lax.dot_general(a, b, (((1,), (0,)), ((), ())), preferred_element_type=f32)


def nt(a, b):
    return lax.dot_general(a, b, (((1,), (1,)), ((), ())), preferred_element_type=f32)


def tn(a, b):
    return lax.dot_general(a, b, (((0,), (0,)), ((), ())), preferred_element_type=f32)


def call(kernel, outs, *args, scalars=0, mem=48, flops=0, name=None):
    moved = sum(a.size * a.dtype.itemsize for a in args)
    moved += sum(s.size * jnp.dtype(s.dtype).itemsize for s in outs)
    return pl.pallas_call(
        kernel,
        out_shape=outs,
        in_specs=[smem] * scalars + [vmem] * (len(args) - scalars),
        out_specs=[vmem] * len(outs),
        compiler_params=pltpu.CompilerParams(vmem_limit_bytes=mem * MIB),
        cost_estimate=pl.CostEstimate(flops=flops, bytes_accessed=moved, transcendentals=0),
        name=name,
    )(*args)


def like(shape, dtype):
    return jax.ShapeDtypeStruct(shape, dtype)


def gelu_pair(v):
    c = 0.7978845608028654
    sq = v * v
    t = jnp.tanh(c * v * (1.0 + 0.044715 * sq))
    half = 0.5 * (1.0 + t)
    slope = half + 0.5 * v * (1.0 - t * t) * c * (1.0 + 3.0 * 0.044715 * sq)
    return v * half, slope


def one_less_exp(x):
    series = x * (
        1.0
        - x * (1 / 2) * (1.0 - x * (1 / 3) * (1.0 - x * (1 / 4) * (1.0 - x * (1 / 5) * (
            1.0 - x * (1 / 6) * (1.0 - x * (1 / 7) * (1.0 - x * (1 / 8)))))))
    )
    return jnp.where(x < 0.5, series, 1.0 - jnp.exp(-x))


def softplus(v):
    return jnp.maximum(v, 0.0) + jnp.log1p(jnp.exp(-jnp.abs(v)))


def sigmoid(v):
    return 1.0 / (1.0 + jnp.exp(-v))


def row_ids(shape):
    return lax.broadcasted_iota(jnp.int32, shape, 0)


def down_rows(v, steps, fill=0.0):
    return jnp.where(row_ids(v.shape) >= steps, pltpu.roll(v, steps, 0), fill)


def up_rows(v, steps, fill=0.0):
    rows = v.shape[0]
    return jnp.where(row_ids(v.shape) < rows - steps, pltpu.roll(v, rows - steps, 0), fill)


def scan_rows(decay, drive, shift):
    steps = 1
    while steps < decay.shape[0]:
        drive = decay * shift(drive, steps) + drive
        if steps * 2 < decay.shape[0]:
            decay = decay * shift(decay, steps, 1.0)
        steps *= 2
    return drive


def norm_first_kernel(x_ref, gain_ref, out_ref):
    x = x_ref[...].astype(f32)
    inv = lax.rsqrt(jnp.mean(x * x, axis=1, keepdims=True) + eps)
    out_ref[...] = (x * inv * gain_ref[...]).astype(bf16)


def branches_kernel(nf_ref, w0_ref, w1_ref, taps_ref, bias_ref, mask_ref, x_ref, y_ref, conv_ref):
    half, chan = w0_ref.shape[0], x_ref.shape[1]
    both = nn(nf_ref[:, :half], w0_ref[...]) + nn(nf_ref[:, half:], w1_ref[...])
    x_ref[...] = both[:, :chan]
    y_ref[...] = both[:, chan:]
    for c in range(0, chan, 128):
        cols = slice(c, c + 128)
        x = x_ref[:, cols]
        total = x * taps_ref[0:1, cols] + bias_ref[:, cols]
        for lag in range(1, taps_ref.shape[0]):
            total = total + down_rows(x, lag) * mask_ref[lag - 1] * taps_ref[lag : lag + 1, cols]
        conv_ref[:, cols] = total.astype(bf16)


def gates_of(rate, decay_logit, start):
    soft = softplus(-decay_logit)
    minus_log = 8.0 * rate * soft
    lost = one_less_exp(2.0 * minus_log)
    mult = jnp.where(start, 1.0, jnp.sqrt(lost))
    carried = jnp.where(start, 0.0, jnp.exp(-minus_log))
    return soft, mult, carried


def forward_scan_kernel(
    c0, c1, c2, c3, block_ref, rb_ref, ib_ref, dl_ref, y_ref, mask_ref,
    rate_ref, entry_ref, hidden_ref, mixed_ref,
):
    start = mask_ref[0] == 0.0
    pre = nn(jnp.concatenate([c0[...], c1[...], c2[...], c3[...]], axis=1), block_ref[0])
    rate = sigmoid(pre[:, :128] + rb_ref[...])
    entry = sigmoid(pre[:, 128:] + ib_ref[...])
    _, mult, carried = gates_of(rate, dl_ref[...], start)
    driven = c0[...].astype(f32) * entry * mult
    hidden = scan_rows(carried, driven, down_rows)
    rate_ref[...] = rate
    entry_ref[...] = entry
    hidden_ref[...] = hidden
    mixed_ref[...] = (hidden * gelu_pair(y_ref[...])[0]).astype(bf16)


def backward_scan_kernel(
    g_ref, w0_ref, w1_ref, c0, c1, c2, c3, block_ref, dl_ref, y_ref, mask_ref, rate_ref, entry_ref,
    hidden_ref,
    gy_ref, direct_ref, h1_ref, h2_ref, h3_ref, wg_ref, sums_ref,
):
    start = mask_ref[0] == 0.0
    half = w0_ref.shape[0]
    grad_mixed = nn(g_ref[:, :half], w0_ref[...]) + nn(g_ref[:, half:], w1_ref[...])
    hidden, rate, entry = hidden_ref[...], rate_ref[...], entry_ref[...]
    conv = c0[...].astype(f32)
    gelu_y, slope_y = gelu_pair(y_ref[...])
    gy_ref[...] = (grad_mixed * hidden * slope_y).astype(bf16)
    decay_logit = dl_ref[...]
    soft, mult, carried = gates_of(rate, decay_logit, start)
    state = scan_rows(up_rows(carried, 1), grad_mixed * gelu_y, up_rows)
    kept = carried * carried
    grad_log = jnp.where(
        start, 0.0, state * (down_rows(hidden, 1) * carried - conv * entry * kept / mult)
    )
    rate_low = (grad_log * (-8.0 * soft) * rate * (1.0 - rate)).astype(bf16)
    entry_low = (state * conv * mult * entry * (1.0 - entry)).astype(bf16)
    both = jnp.concatenate([rate_low, entry_low], axis=1)
    sums_ref[...] = jnp.concatenate(
        [
            jnp.sum(grad_log * rate, axis=0, keepdims=True) * (8.0 * sigmoid(-decay_logit)),
            jnp.sum(rate_low.astype(f32), axis=0, keepdims=True),
            jnp.sum(entry_low.astype(f32), axis=0, keepdims=True),
            jnp.zeros((5, 128), f32),
        ],
        axis=0,
    )
    heads = nt(both, block_ref[0])
    direct_ref[...] = state * entry * mult + heads[:, :128]
    h1_ref[...] = heads[:, 128:256].astype(bf16)
    h2_ref[...] = heads[:, 256:384].astype(bf16)
    h3_ref[...] = heads[:, 384:].astype(bf16)
    units = jnp.concatenate([c0[...], c1[...], c2[...], c3[...]], axis=1)
    grads = tn(units, both)
    first = jnp.concatenate([grads[:, 0:64], grads[:, 128:192]], axis=1)
    second = jnp.concatenate([grads[:, 64:128], grads[:, 192:256]], axis=1)
    for k in range(4):
        wg_ref[0, k] = first[k * 128 : k * 128 + 64]
        wg_ref[1, k] = second[k * 128 + 64 : k * 128 + 128]


def conv_back_kernel(direct_ref, r1, r2, r3, x_ref, taps_ref, mask_ref, gx_ref, sums_ref):
    total = direct_ref[...] + r1[...].astype(f32) + r2[...].astype(f32) + r3[...].astype(f32)
    x = x_ref[...]
    grad = total * taps_ref[0:1]
    sums = [jnp.sum(total * x, axis=0, keepdims=True)]
    for lag in range(1, taps_ref.shape[0]):
        kept = total * mask_ref[lag - 1]
        grad = grad + up_rows(kept, lag) * taps_ref[lag : lag + 1]
        sums.append(jnp.sum(kept * down_rows(x, lag), axis=0, keepdims=True))
    gx_ref[...] = grad.astype(bf16)
    sums.append(jnp.sum(total, axis=0, keepdims=True))
    sums.append(jnp.zeros((8 - len(sums), x.shape[1]), f32))
    sums_ref[...] = jnp.concatenate(sums, axis=0)


def split_rows(z_ref, total_ref, outs):
    rows = outs[0].shape[0]
    for k, out in enumerate(outs):
        at = pl.multiple_of((z_ref[0] ^ k) * rows, rows)
        out[...] = total_ref[pl.ds(at, rows), :].astype(out.dtype)


def product_split_kernel(z_ref, a_ref, w0_ref, w1_ref, o0, o1, o2, o3, total_ref):
    half = w0_ref.shape[0]
    total_ref[:, :half] = nt(a_ref[...], w0_ref[...])
    total_ref[:, half:] = nt(a_ref[...], w1_ref[...])
    split_rows(z_ref, total_ref, (o0, o1, o2, o3))


def assemble_kernel(z_ref, p0, p1, p2, p3, out_ref):
    rows = p0.shape[0]
    for k, piece in enumerate((p0, p1, p2, p3)):
        at = pl.multiple_of((z_ref[0] ^ k) * rows, rows)
        out_ref[pl.ds(at, rows), :] = piece[...].astype(out_ref.dtype)


def sum_pieces(pieces):
    total = pieces[0][...]
    for piece in pieces[1:]:
        total = total + piece[...].astype(f32)
    return total


def my_rows(z_ref, ref, rows):
    return ref[pl.ds(pl.multiple_of(z_ref[0] * rows, rows), rows), :].astype(f32)


def norm_second_kernel(z_ref, x_ref, gain_ref, o0, o1, o2, o3, res_ref, low_ref):
    residual = my_rows(z_ref, x_ref, res_ref.shape[0]) + sum_pieces((o0, o1, o2, o3))
    inv = lax.rsqrt(jnp.mean(residual * residual, axis=1, keepdims=True) + eps)
    res_ref[...] = residual
    low_ref[...] = (residual * inv * gain_ref[...]).astype(bf16)


def norm_back(x, gain, grad):
    inv = lax.rsqrt(jnp.mean(x * x, axis=1, keepdims=True) + eps)
    unit = x * inv
    scaled = grad * gain
    out = inv * (scaled - unit * jnp.mean(scaled * unit, axis=1, keepdims=True))
    return out, jnp.sum(grad * unit, axis=0, keepdims=True)


def second_back_kernel(z_ref, cot_ref, gain_ref, res_ref, o0, o1, o2, o3, gr_ref, low_ref, gain_out):
    grad, gain_grad = norm_back(res_ref[...], gain_ref[...], sum_pieces((o0, o1, o2, o3)))
    grad = grad + my_rows(z_ref, cot_ref, res_ref.shape[0])
    gr_ref[...] = grad
    low_ref[...] = grad.astype(bf16)
    gain_out[...] = gain_grad


def first_back_kernel(z_ref, x_ref, gain_ref, gr_ref, o0, o1, o2, o3, out_ref, gain_out):
    x = my_rows(z_ref, x_ref, gr_ref.shape[0])
    grad, gain_grad = norm_back(x, gain_ref[...], sum_pieces((o0, o1, o2, o3)))
    out_ref[...] = (gr_ref[...] + grad).astype(bf16)
    gain_out[...] = gain_grad


def block_out_kernel(res_ref, o0, o1, o2, o3, out_ref):
    out_ref[...] = (res_ref[...] + sum_pieces((o0, o1, o2, o3))).astype(bf16)


def ffn_kernel(first, last, *refs):
    refs = list(refs)
    z_ref = refs.pop(0)
    s_ref, cot_ref, w0_ref, w1_ref = refs[:4]
    refs = refs[4:]
    if not first:
        in_out, in_grad = refs[:2]
        refs = refs[2:]
    ggu_ref, mid_ref = refs[:2]
    refs = refs[2:]
    pre_ref, back_ref = refs[-2:]
    if last:
        out_pieces, grad_pieces = refs[:4], refs[4:8]
        acc_out, acc_grad = refs[8:10]
    else:
        acc_out, acc_grad = refs[:2]
    half, width = w0_ref.shape[0], mid_ref.shape[1]
    pre_ref[...] = nn(s_ref[:, :half], w0_ref[:, : 2 * width])
    pre_ref[...] += nn(s_ref[:, half:], w1_ref[:, : 2 * width])
    back_ref[...] = nn(cot_ref[:, :half], w0_ref[:, 2 * width :])
    back_ref[...] += nn(cot_ref[:, half:], w1_ref[:, 2 * width :])
    for c in range(0, width, 128):
        gate, up = pre_ref[:, c : c + 128], pre_ref[:, width + c : width + c + 128]
        back = back_ref[:, c : c + 128]
        gelu_gate, slope = gelu_pair(gate)
        mid_ref[:, c : c + 128] = (gelu_gate * up).astype(bf16)
        ggu_ref[:, c : c + 128] = (back * up * slope).astype(bf16)
        ggu_ref[:, width + c : width + c + 128] = (back * gelu_gate).astype(bf16)
    for lo, w_ref in ((0, w0_ref), (half, w1_ref)):
        cols = slice(lo, lo + half)
        out = nt(mid_ref[...], w_ref[:, 2 * width :])
        acc_out[:, cols] = out if first else in_out[:, cols] + out
        grad = nt(ggu_ref[...], w_ref[:, : 2 * width])
        acc_grad[:, cols] = grad if first else in_grad[:, cols] + grad
    if last:
        split_rows(z_ref, acc_out, out_pieces)
        split_rows(z_ref, acc_grad, grad_pieces)


def grads_out_kernel(sides, *refs):
    lefts, rights, out = refs[:sides], refs[sides : 2 * sides], refs[2 * sides]
    at = 0
    for left, right in zip(lefts, rights):
        half, width = left.shape[1] // 2, right.shape[1]
        out[:, at : at + width] = tn(left[:, half:], right[...]).astype(bf16)
        at += width


def grads_own_kernel(sides, *refs):
    lefts, rights = refs[:sides], refs[sides : 2 * sides]
    got, own, x_top, y_bot, send_x, send_y = refs[2 * sides :]
    at = 0
    q = x_top.shape[0]
    for left, right in zip(lefts, rights):
        half, width = left.shape[1] // 2, right.shape[1]
        cols = slice(at, at + width)
        at += width
        near = tn(left[:, : half // 2], right[...]) + got[: half // 2, cols].astype(f32)
        own[:, cols] = near[: 2 * q]
        x_top[:, cols] = near[2 * q : 3 * q]
        send_x[q:, cols] = near[3 * q :].astype(bf16)
        far = tn(left[:, half // 2 : half], right[...]) + got[half // 2 :, cols].astype(f32)
        send_y[q:, cols] = far[:q].astype(bf16)
        y_bot[:, cols] = far[q : 2 * q]
        send_y[:q, cols] = far[2 * q : 3 * q].astype(bf16)
        send_x[:q, cols] = far[3 * q :].astype(bf16)


def exchange(v, axis, size, bit):
    return lax.ppermute(v, axis, [(i, i ^ bit) for i in range(size)])


def after(v, *others):
    return lax.optimization_barrier((v,) + others)[0]


def gather_rows(shard, size, before):
    if before:
        shard = after(shard, *before)
    if size == 8:
        half = shard.shape[0] // 2
        by_x = exchange(shard, "dp", size, 2)
        by_y = exchange(shard, "dp", size, 4)
        top = exchange(by_x[:half], "dp", size, 4)
        bottom = exchange(by_y[half:], "dp", size, 2)
        mine = jnp.concatenate([shard, by_x, by_y, top, bottom], axis=0)
        marks = (by_x, by_y)
    else:
        mine, bit = shard, 2
        while bit < size:
            mine = jnp.concatenate([mine, exchange(mine, "dp", size, bit)], axis=0)
            bit *= 2
        marks = (mine,)
    return mine, exchange(mine, "dp", size, 1), marks


def scatter_grads(lefts, rights, size):
    sides, model = len(lefts), lefts[0].shape[1]
    tokens = lefts[0].shape[0]
    width = sum(r.shape[1] for r in rights)
    flops = tokens * model * width
    out = call(
        partial(grads_out_kernel, sides), [like((model // 2, width), bf16)], *lefts, *rights,
        flops=flops, name="grads_out",
    )[0]
    got = exchange(out, "dp", size, 1)
    q = model // 16
    own, x_top, y_bot, send_x, send_y = call(
        partial(grads_own_kernel, sides),
        [like((2 * q, width), f32), like((q, width), f32), like((q, width), f32),
         like((2 * q, width), bf16), like((2 * q, width), bf16)],
        *lefts, *rights, got, flops=flops, name="grads_own",
    )
    if size == 8:
        from_x = exchange(send_x, "dp", size, 2)
        from_y = exchange(send_y, "dp", size, 4)
        last_x = exchange((x_top + from_y[:q].astype(f32)).astype(bf16), "dp", size, 2)
        last_y = exchange((y_bot + from_x[:q].astype(f32)).astype(bf16), "dp", size, 4)
        return jnp.concatenate(
            [
                own[:q] + from_y[q:].astype(f32) + last_x.astype(f32),
                own[q:] + from_x[q:].astype(f32) + last_y.astype(f32),
            ],
            axis=0,
        )
    total = jnp.concatenate(
        [own, x_top, send_x[q:].astype(f32), send_y[q:].astype(f32), y_bot,
         send_y[:q].astype(f32), send_x[:q].astype(f32)],
        axis=0,
    )
    bit = size // 2
    while bit > 1:
        half = total.shape[0] // 2
        total = total[:half] + exchange(total[half:].astype(bf16), "dp", size, bit).astype(f32)
        bit //= 2
    return total


def send_rows(pieces):
    return [pieces[0]] + [exchange(pieces[k], "tensor", 4, k) for k in range(1, 4)]


def spread_rows(piece):
    return [piece] + [exchange(piece, "tensor", 4, k) for k in range(1, 4)]


def sum_over(v, axis, size):
    bit = 1
    while bit < size:
        v = v + exchange(v, axis, size, bit)
        bit *= 2
    return v


def body(
    tokens, segments, first_gain, x_weight, y_weight, conv_weight, conv_bias, rate_weight,
    input_weight, rate_bias, input_bias, decay_logit, out_weight, second_gain, gate_weight,
    up_weight, down_weight, cotangent, dp_size,
):
    count, model = tokens.shape
    heads, _, units = rate_weight.shape
    chan = heads * units
    pairs = heads // 2
    taps = conv_weight.shape[0]
    hidden_units = gate_weight.shape[1]
    width = hidden_units // chunk_count
    me = lax.axis_index("dp")
    z = lax.axis_index("tensor").astype(jnp.int32)
    z_arr = z.reshape(1)
    part = model // dp_size
    order = [2 * j + c for c in range(2) for j in range(dp_size // 2)]
    rows = count // 4

    def to_rel(v):
        return jnp.concatenate(
            [lax.dynamic_slice_in_dim(v, (me ^ r) * part, part, axis=-1) for r in order], axis=-1
        )

    def to_abs(v):
        places = []
        for s in range(dp_size):
            rel = me ^ s
            places.append((rel % 2) * (dp_size // 2) + rel // 2)
        return jnp.concatenate(
            [lax.dynamic_slice_in_dim(v, p * part, part, axis=-1) for p in places], axis=-1
        )

    xy_shard = jnp.concatenate([x_weight.reshape(part, chan), y_weight.reshape(part, chan)], axis=1)
    out_shard = out_weight.reshape(chan, part).T
    down_shard = down_weight.T
    ffn_shards = [
        jnp.concatenate(
            [v[:, c * width : (c + 1) * width] for v in (gate_weight, up_weight, down_shard)], axis=1
        )
        for c in range(chunk_count)
    ]
    xy0, xy1, marks = gather_rows(xy_shard, dp_size, None)
    out0, out1, marks = gather_rows(out_shard, dp_size, marks)
    ffn_weights = []
    for shard in ffn_shards:
        w0, w1, marks = gather_rows(shard, dp_size, marks)
        ffn_weights.append((w0, w1))

    x_rel = to_rel(tokens)
    cot_rel = to_rel(cotangent)
    gain_one = to_rel(first_gain).reshape(1, model)
    gain_two = to_rel(second_gain).reshape(1, model)
    masks = jnp.stack(
        [
            jnp.concatenate([jnp.full((lag,), -1, jnp.int32), segments[:-lag]]) == segments
            for lag in range(1, taps)
        ]
    ).astype(f32)
    masks = jnp.broadcast_to(masks[:, :, None], (taps - 1, count, 128))
    wide_masks = masks
    taps_flat = conv_weight.reshape(taps, chan)
    bias_flat = conv_bias.reshape(1, chan)
    rate_flat, input_flat = rate_bias.reshape(1, chan), input_bias.reshape(1, chan)
    decay_flat = decay_logit.reshape(1, chan)
    both = jnp.stack([rate_weight, input_weight], axis=2).reshape(pairs, 2, 4, units, 2, units)
    both = jnp.stack([lax.dynamic_index_in_dim(both, z ^ k, 2, False) for k in range(4)], axis=1)
    zero = jnp.zeros((pairs, 4, units, 2, units), bf16)
    blocks = jnp.stack(
        [jnp.stack([both[:, :, 0], zero], axis=4), jnp.stack([zero, both[:, :, 1]], axis=4)], axis=2
    ).reshape(pairs, 8 * units, 4 * units)

    nf = call(norm_first_kernel, [like((count, model), bf16)], x_rel, gain_one, name="norm_first")[0]
    x_branch, y_branch, conv_low = call(
        branches_kernel,
        [like((count, chan), f32), like((count, chan), f32), like((count, chan), bf16)],
        nf, xy0, xy1, taps_flat, bias_flat, masks, flops=4 * count * model * chan, name="branches",
    )
    conv = spread_rows(conv_low)
    lane = pl.BlockSpec((count, 128), lambda p: (0, p))
    line = pl.BlockSpec((1, 128), lambda p: (0, p))
    block_spec = pl.BlockSpec((1, 8 * units, 4 * units), lambda p: (p, 0, 0))
    mask_spec = pl.BlockSpec((taps - 1, count, 128), lambda p: (0, 0, 0))
    rate, entry, hidden, mixed = pl.pallas_call(
        forward_scan_kernel,
        grid=(pairs,),
        in_specs=[lane] * 4 + [block_spec] + [line] * 3 + [lane, mask_spec],
        out_specs=[lane] * 4,
        out_shape=[like((count, chan), f32)] * 3 + [like((count, chan), bf16)],
        compiler_params=pltpu.CompilerParams(vmem_limit_bytes=24 * MIB),
        cost_estimate=pl.CostEstimate(
            flops=pairs * count * 512 * 256 * 2, bytes_accessed=6 * MIB, transcendentals=0),
        name="forward_scan",
    )(*conv, blocks, rate_flat, input_flat, decay_flat, y_branch, masks)

    def product_split(a, w0, w1, name):
        return pl.pallas_call(
            product_split_kernel,
            out_shape=[like((rows, model), f32)] + [like((rows, model), bf16)] * 3,
            in_specs=[smem] + [vmem] * 3,
            out_specs=[vmem] * 4,
            scratch_shapes=[pltpu.VMEM((count, model), f32)],
            compiler_params=pltpu.CompilerParams(vmem_limit_bytes=32 * MIB),
            cost_estimate=pl.CostEstimate(
                flops=2 * count * model * a.shape[1], bytes_accessed=2 * w0.size * 2,
                transcendentals=0),
            name=name,
        )(z_arr, a, w0, w1)

    def assemble(pieces, dtype, name):
        return call(assemble_kernel, [like((count, model), dtype)], z_arr, *pieces, scalars=1, name=name)[0]

    pieces = send_rows(product_split(mixed, out0, out1, "recurrent"))
    residual, second_rows = call(
        norm_second_kernel, [like((rows, model), f32), like((rows, model), bf16)],
        z_arr, x_rel, gain_two, *pieces, scalars=1, name="norm_second",
    )
    second = assemble(spread_rows(second_rows), bf16, "second_all")

    ffn_grads = []
    sums = None
    for c, (w0, w1) in enumerate(ffn_weights):
        first, last = c == 0, c == chunk_count - 1
        outs = [like((count, 2 * width), bf16), like((count, width), bf16)]
        scratch = [pltpu.VMEM((count, 2 * width), f32), pltpu.VMEM((count, width), f32)]
        if last:
            outs += ([like((rows, model), f32)] + [like((rows, model), bf16)] * 3) * 2
            scratch = [pltpu.VMEM((count, model), f32)] * 2 + scratch
        else:
            outs += [like((count, model), f32)] * 2
        ins = [z_arr, second, cot_rel, w0, w1] + ([] if first else sums)
        res = pl.pallas_call(
            partial(ffn_kernel, first, last),
            out_shape=outs,
            in_specs=[smem] + [vmem] * (len(ins) - 1),
            out_specs=[vmem] * len(outs),
            scratch_shapes=scratch,
            compiler_params=pltpu.CompilerParams(vmem_limit_bytes=56 * MIB),
            cost_estimate=pl.CostEstimate(
                flops=12 * count * model * width, bytes_accessed=25 * MIB, transcendentals=0),
            name="ffn_%d" % c,
        )(*ins)
        ffn_grads.append((res[0], res[1]))
        sums = list(res[2:])
    out_pieces, grad_pieces = sums[:4], sums[4:]

    grad_pieces = send_rows(grad_pieces)
    grad_res, rec_rows, second_gain_part = call(
        second_back_kernel,
        [like((rows, model), f32), like((rows, model), bf16), like((1, model), f32)],
        z_arr, cot_rel, gain_two, residual, *grad_pieces, scalars=1, name="second_back",
    )
    grad_rec = assemble(spread_rows(rec_rows), bf16, "grad_rec_all")

    ffn_shares = [
        scatter_grads([second, cot_rel], [ggu, mid], dp_size) for ggu, mid in ffn_grads
    ]

    out_pieces = send_rows(out_pieces)
    block_rows = call(block_out_kernel, [like((rows, model), bf16)], residual, *out_pieces, name="block_out")[0]
    block_out = assemble(spread_rows(to_abs(block_rows)), bf16, "block_out_all")

    half_spec = pl.BlockSpec((model // 2, 128), lambda p: (0, p))
    whole = pl.BlockSpec((count, model), lambda p: (0, 0))
    gate_spec = pl.BlockSpec((2, 4, units, 2 * units), lambda p: (p, 0, 0, 0))
    grad_y, direct, h1, h2, h3, gate_grads, scan_sums = pl.pallas_call(
        backward_scan_kernel,
        grid=(pairs,),
        in_specs=[whole, half_spec, half_spec] + [lane] * 4 + [block_spec, line, lane, mask_spec]
        + [lane] * 3,
        out_specs=[lane, lane, lane, lane, lane, gate_spec, pl.BlockSpec((8, 128), lambda p: (0, p))],
        out_shape=[like((count, chan), bf16), like((count, chan), f32)]
        + [like((count, chan), bf16)] * 3
        + [like((heads, 4, units, 2 * units), f32), like((8, chan), f32)],
        compiler_params=pltpu.CompilerParams(vmem_limit_bytes=32 * MIB),
        cost_estimate=pl.CostEstimate(
            flops=2 * count * model * chan + pairs * count * 512 * 256 * 4, bytes_accessed=12 * MIB,
            transcendentals=0),
        name="backward_scan",
    )(grad_rec, out0, out1, *conv, blocks, decay_flat, y_branch, masks, rate, entry, hidden)
    out_share = scatter_grads([grad_rec], [mixed], dp_size)
    got = send_rows([direct, h1, h2, h3])
    grad_x, conv_sums = pl.pallas_call(
        conv_back_kernel,
        grid=(pairs,),
        in_specs=[lane] * 5 + [pl.BlockSpec((taps, 128), lambda p: (0, p)), mask_spec],
        out_specs=[lane, pl.BlockSpec((8, 128), lambda p: (0, p))],
        out_shape=[like((count, chan), bf16), like((8, chan), f32)],
        compiler_params=pltpu.CompilerParams(vmem_limit_bytes=24 * MIB),
        cost_estimate=pl.CostEstimate(flops=0, bytes_accessed=4 * MIB, transcendentals=0),
        name="conv_back",
    )(*got, x_branch, taps_flat, masks)

    grad_xy = jnp.concatenate([grad_x, grad_y], axis=1)
    first_pieces = send_rows(product_split(grad_xy, xy0, xy1, "grad_first"))
    tokens_rows, first_gain_part = call(
        first_back_kernel, [like((rows, model), bf16), like((1, model), f32)],
        z_arr, x_rel, gain_one, grad_res, *first_pieces, scalars=1, name="first_back",
    )
    tokens_grad = assemble(spread_rows(to_abs(tokens_rows)), f32, "tokens_grad_all")
    xy_share = scatter_grads([nf], [grad_xy], dp_size)

    small = jnp.concatenate([scan_sums, conv_sums], axis=0)
    small = sum_over(small, "dp", dp_size)
    gains = to_abs(jnp.concatenate([first_gain_part, second_gain_part], axis=0))
    gains = sum_over(sum_over(gains, "tensor", 4), "dp", dp_size)
    gate_low = gate_grads.astype(bf16)
    bit = 1
    while bit < dp_size:
        gate_low = gate_low.astype(bf16)
        gate_low = gate_low.astype(f32) + exchange(gate_low, "dp", dp_size, bit).astype(f32)
        bit *= 2
    gate_sum = jnp.concatenate(
        [lax.dynamic_index_in_dim(gate_low, z ^ k, 1, False) for k in range(4)], axis=1
    )

    ffn_cat = [
        jnp.concatenate([s[:, k * width : (k + 1) * width] for s in ffn_shares], axis=1)
        for k in range(3)
    ]
    return (
        block_out,
        tokens_grad,
        gains[0],
        xy_share[:, :chan].reshape(part, heads, units),
        xy_share[:, chan:].reshape(part, heads, units),
        small[8 : 8 + taps].reshape(taps, heads, units),
        small[8 + taps].reshape(heads, units),
        gate_sum[:, :, :units],
        gate_sum[:, :, units:],
        small[1].reshape(heads, units),
        small[2].reshape(heads, units),
        small[0].reshape(heads, units),
        out_share.T.reshape(heads, units, part),
        gains[1],
        ffn_cat[0],
        ffn_cat[1],
        ffn_cat[2].T,
    )


def solution(mesh):
    return jax.shard_map(
        partial(body, dp_size=mesh.shape["dp"]),
        mesh=mesh,
        in_specs=(
            P("dp", None),
            P("dp"),
            P(),
            P("dp", None, "tensor"),
            P("dp", None, "tensor"),
            P(None, None, "tensor"),
            P(None, "tensor"),
            P(None, None, "tensor"),
            P(None, None, "tensor"),
            P(None, "tensor"),
            P(None, "tensor"),
            P(None, "tensor"),
            P(None, "tensor", "dp"),
            P(),
            P("dp", "tensor"),
            P("dp", "tensor"),
            P("tensor", "dp"),
            P("dp", None),
        ),
        out_specs=(
            P("dp", None),
            P("dp", None),
            P(),
            P("dp", None, "tensor"),
            P("dp", None, "tensor"),
            P(None, None, "tensor"),
            P(None, "tensor"),
            P(None, None, "tensor"),
            P(None, None, "tensor"),
            P(None, "tensor"),
            P(None, "tensor"),
            P(None, "tensor"),
            P(None, "tensor", "dp"),
            P(),
            P("dp", "tensor"),
            P("dp", "tensor"),
            P("tensor", "dp"),
        ),
        check_vma=False,
    )
```

```python
from functools import partial

import jax
import jax.numpy as jnp
from jax import lax
from jax.experimental import pallas as pl
from jax.experimental.pallas import tpu as pltpu
from jax.sharding import PartitionSpec as P

eps = 1e-06
f32 = jnp.float32
bf16 = jnp.bfloat16
vmem = pl.BlockSpec(memory_space=pltpu.VMEM)
smem = pl.BlockSpec(memory_space=pltpu.SMEM)
MIB = 1024 * 1024
chunk_count = 3


def nn(a, b):
    return lax.dot_general(a, b, (((1,), (0,)), ((), ())), preferred_element_type=f32)


def nt(a, b):
    return lax.dot_general(a, b, (((1,), (1,)), ((), ())), preferred_element_type=f32)


def tn(a, b):
    return lax.dot_general(a, b, (((0,), (0,)), ((), ())), preferred_element_type=f32)


def full(v):
    zeros = (0,) * len(v.shape)
    return pl.BlockSpec(v.shape, lambda i: zeros, pipeline_mode=pl.Buffered(1))


def call(kernel, outs, *args, scalars=0, mem=60, flops=0, scratch=(), name=None):
    moved = sum(a.size * a.dtype.itemsize for a in args)
    moved += sum(s.size * jnp.dtype(s.dtype).itemsize for s in outs)
    return pl.pallas_call(
        kernel,
        grid=(1,),
        out_shape=outs,
        in_specs=[smem] * scalars + [full(a) for a in args[scalars:]],
        out_specs=[full(s) for s in outs],
        scratch_shapes=scratch,
        compiler_params=pltpu.CompilerParams(vmem_limit_bytes=mem * MIB),
        cost_estimate=pl.CostEstimate(flops=flops, bytes_accessed=moved, transcendentals=0),
        name=name,
    )(*args)


def like(shape, dtype):
    return jax.ShapeDtypeStruct(shape, dtype)


def gelu_pair(v):
    c = 0.7978845608028654
    sq = v * v
    t = jnp.tanh(c * v * (1.0 + 0.044715 * sq))
    half = 0.5 * (1.0 + t)
    slope = half + 0.5 * v * (1.0 - t * t) * c * (1.0 + 3.0 * 0.044715 * sq)
    return v * half, slope


def one_less_exp(x):
    series = x * (
        1.0
        - x * (1 / 2) * (1.0 - x * (1 / 3) * (1.0 - x * (1 / 4) * (1.0 - x * (1 / 5) * (
            1.0 - x * (1 / 6) * (1.0 - x * (1 / 7) * (1.0 - x * (1 / 8)))))))
    )
    return jnp.where(x < 0.5, series, 1.0 - jnp.exp(-x))


def softplus(v):
    return jnp.maximum(v, 0.0) + jnp.log1p(jnp.exp(-jnp.abs(v)))


def sigmoid(v):
    return 1.0 / (1.0 + jnp.exp(-v))


def row_ids(shape):
    return lax.broadcasted_iota(jnp.int32, shape, 0)


def down_rows(v, steps, fill=0.0):
    return jnp.where(row_ids(v.shape) >= steps, pltpu.roll(v, steps, 0), fill)


def up_rows(v, steps, fill=0.0):
    rows = v.shape[0]
    return jnp.where(row_ids(v.shape) < rows - steps, pltpu.roll(v, rows - steps, 0), fill)


def scan_rows(decay, drive, shift):
    steps = 1
    while steps < decay.shape[0]:
        drive = decay * shift(drive, steps) + drive
        if steps * 2 < decay.shape[0]:
            decay = decay * shift(decay, steps, 1.0)
        steps *= 2
    return drive


def norm_first_kernel(x_ref, gain_ref, out_ref):
    x = x_ref[...].astype(f32)
    inv = lax.rsqrt(jnp.mean(x * x, axis=1, keepdims=True) + eps)
    out_ref[...] = (x * inv * gain_ref[...]).astype(bf16)


def branches_kernel(nf_ref, w0_ref, w1_ref, taps_ref, bias_ref, mask_ref, x_ref, y_ref, conv_ref):
    half, chan = w0_ref.shape[0], x_ref.shape[1]
    both = nn(nf_ref[:, :half], w0_ref[:, : 2 * chan]) + nn(nf_ref[:, half:], w1_ref[:, : 2 * chan])
    x_ref[...] = both[:, :chan]
    y_ref[...] = both[:, chan:]
    for c in range(0, chan, 128):
        cols = slice(c, c + 128)
        x = x_ref[:, cols]
        total = x * taps_ref[0:1, cols] + bias_ref[:, cols]
        for lag in range(1, taps_ref.shape[0]):
            total = total + down_rows(x, lag) * mask_ref[lag - 1] * taps_ref[lag : lag + 1, cols]
        conv_ref[:, cols] = total.astype(bf16)


def gates_of(rate, decay_logit, start):
    soft = softplus(-decay_logit)
    minus_log = 8.0 * rate * soft
    lost = one_less_exp(2.0 * minus_log)
    mult = jnp.where(start, 1.0, jnp.sqrt(lost))
    carried = jnp.where(start, 0.0, jnp.exp(-minus_log))
    return soft, mult, carried


def forward_scan_kernel(
    c0, c1, c2, c3, block_ref, rb_ref, ib_ref, dl_ref, y_ref, mask_ref,
    rate_ref, entry_ref, hidden_ref, mixed_ref,
):
    start = mask_ref[0] == 0.0
    pre = nn(jnp.concatenate([c0[...], c1[...], c2[...], c3[...]], axis=1), block_ref[0])
    rate = sigmoid(pre[:, :128] + rb_ref[...])
    entry = sigmoid(pre[:, 128:] + ib_ref[...])
    _, mult, carried = gates_of(rate, dl_ref[...], start)
    driven = c0[...].astype(f32) * entry * mult
    hidden = scan_rows(carried, driven, down_rows)
    rate_ref[...] = rate
    entry_ref[...] = entry
    hidden_ref[...] = hidden
    mixed_ref[...] = (hidden * gelu_pair(y_ref[...])[0]).astype(bf16)


def backward_scan_kernel(
    g_ref, w0_ref, w1_ref, c0, c1, c2, c3, block_ref, dl_ref, y_ref, mask_ref, rate_ref, entry_ref,
    hidden_ref,
    gy_ref, direct_ref, h1_ref, h2_ref, h3_ref, wg_ref, sums_ref,
):
    start = mask_ref[0] == 0.0
    half = w0_ref.shape[0]
    grad_mixed = nn(g_ref[:, :half], w0_ref[...]) + nn(g_ref[:, half:], w1_ref[...])
    hidden, rate, entry = hidden_ref[...], rate_ref[...], entry_ref[...]
    conv = c0[...].astype(f32)
    gelu_y, slope_y = gelu_pair(y_ref[...])
    gy_ref[...] = (grad_mixed * hidden * slope_y).astype(bf16)
    decay_logit = dl_ref[...]
    soft, mult, carried = gates_of(rate, decay_logit, start)
    state = scan_rows(up_rows(carried, 1), grad_mixed * gelu_y, up_rows)
    kept = carried * carried
    grad_log = jnp.where(
        start, 0.0, state * (down_rows(hidden, 1) * carried - conv * entry * kept / mult)
    )
    rate_low = (grad_log * (-8.0 * soft) * rate * (1.0 - rate)).astype(bf16)
    entry_low = (state * conv * mult * entry * (1.0 - entry)).astype(bf16)
    both = jnp.concatenate([rate_low, entry_low], axis=1)
    sums_ref[...] = jnp.concatenate(
        [
            jnp.sum(grad_log * rate, axis=0, keepdims=True) * (8.0 * sigmoid(-decay_logit)),
            jnp.sum(rate_low.astype(f32), axis=0, keepdims=True),
            jnp.sum(entry_low.astype(f32), axis=0, keepdims=True),
            jnp.zeros((5, 128), f32),
        ],
        axis=0,
    )
    heads = nt(both, block_ref[0])
    direct_ref[...] = state * entry * mult + heads[:, :128]
    h1_ref[...] = heads[:, 128:256].astype(bf16)
    h2_ref[...] = heads[:, 256:384]
    h3_ref[...] = heads[:, 384:].astype(bf16)
    units = jnp.concatenate([c0[...], c1[...], c2[...], c3[...]], axis=1)
    grads = tn(units, both)
    first = jnp.concatenate([grads[:, 0:64], grads[:, 128:192]], axis=1)
    second = jnp.concatenate([grads[:, 64:128], grads[:, 192:256]], axis=1)
    for k in range(4):
        wg_ref[0, k] = first[k * 128 : k * 128 + 64]
        wg_ref[1, k] = second[k * 128 + 64 : k * 128 + 128]


def conv_back_kernel(direct_ref, r1, r2, x_ref, taps_ref, mask_ref, gx_ref, sums_ref):
    total = direct_ref[...] + r1[...].astype(f32) + r2[...].astype(f32)
    x = x_ref[...]
    grad = total * taps_ref[0:1]
    sums = [jnp.sum(total * x, axis=0, keepdims=True)]
    for lag in range(1, taps_ref.shape[0]):
        kept = total * mask_ref[lag - 1]
        grad = grad + up_rows(kept, lag) * taps_ref[lag : lag + 1]
        sums.append(jnp.sum(kept * down_rows(x, lag), axis=0, keepdims=True))
    gx_ref[...] = grad.astype(bf16)
    sums.append(jnp.sum(total, axis=0, keepdims=True))
    sums.append(jnp.zeros((8 - len(sums), x.shape[1]), f32))
    sums_ref[...] = jnp.concatenate(sums, axis=0)


def split_rows(z_ref, total_ref, outs):
    rows = outs[0].shape[0]
    for k, out in enumerate(outs):
        at = pl.multiple_of((z_ref[0] ^ k) * rows, rows)
        out[...] = total_ref[pl.ds(at, rows), :].astype(out.dtype)


def product_split_kernel(at, z_ref, a_ref, w0_ref, w1_ref, o0, o1, o2, o3, total_ref):
    half, cols = w0_ref.shape[0], slice(at, at + a_ref.shape[1])
    total_ref[:, :half] = nt(a_ref[...], w0_ref[:, cols])
    total_ref[:, half:] = nt(a_ref[...], w1_ref[:, cols])
    split_rows(z_ref, total_ref, (o0, o1, o2, o3))


def assemble_kernel(z_ref, p0, p1, p2, p3, out_ref):
    rows = p0.shape[0]
    for k, piece in enumerate((p0, p1, p2, p3)):
        at = pl.multiple_of((z_ref[0] ^ k) * rows, rows)
        out_ref[pl.ds(at, rows), :] = piece[...].astype(out_ref.dtype)


def sum_pieces(pieces):
    total = pieces[0][...]
    for piece in pieces[1:]:
        total = total + piece[...].astype(f32)
    return total


def my_rows(z_ref, ref, rows):
    return ref[pl.ds(pl.multiple_of(z_ref[0] * rows, rows), rows), :].astype(f32)


def norm_second_kernel(z_ref, x_ref, gain_ref, o0, o1, o2, res_ref, low_ref):
    residual = my_rows(z_ref, x_ref, res_ref.shape[0]) + sum_pieces((o0, o1, o2))
    inv = lax.rsqrt(jnp.mean(residual * residual, axis=1, keepdims=True) + eps)
    res_ref[...] = residual
    low_ref[...] = (residual * inv * gain_ref[...]).astype(bf16)


def norm_back(x, gain, grad):
    inv = lax.rsqrt(jnp.mean(x * x, axis=1, keepdims=True) + eps)
    unit = x * inv
    scaled = grad * gain
    out = inv * (scaled - unit * jnp.mean(scaled * unit, axis=1, keepdims=True))
    return out, jnp.sum(grad * unit, axis=0, keepdims=True)


def second_back_kernel(z_ref, cot_ref, gain_ref, res_ref, o0, o1, o2, gr_ref, low_ref, gain_out):
    grad, gain_grad = norm_back(res_ref[...], gain_ref[...], sum_pieces((o0, o1, o2)))
    grad = grad + my_rows(z_ref, cot_ref, res_ref.shape[0])
    gr_ref[...] = grad
    low_ref[...] = grad.astype(bf16)
    gain_out[...] = gain_grad


def first_back_kernel(z_ref, x_ref, gain_ref, gr_ref, o0, o1, o2, out_ref, gain_out):
    x = my_rows(z_ref, x_ref, gr_ref.shape[0])
    grad, gain_grad = norm_back(x, gain_ref[...], sum_pieces((o0, o1, o2)))
    out_ref[...] = (gr_ref[...] + grad).astype(bf16)
    gain_out[...] = gain_grad


def block_out_kernel(res_ref, o0, o1, o2, out_ref):
    out_ref[...] = (res_ref[...] + sum_pieces((o0, o1, o2))).astype(bf16)


def ffn_kernel(first, last, *refs):
    refs = list(refs)
    z_ref = refs.pop(0)
    s_ref, cot_ref, w0_ref, w1_ref = refs[:4]
    refs = refs[4:]
    if not first:
        in_out, in_grad = refs[:2]
        refs = refs[2:]
    ggu_ref, mid_ref = refs[:2]
    refs = refs[2:]
    pre_ref, back_ref = refs[-2:]
    if last:
        out_pieces, grad_pieces = refs[:4], refs[4:8]
        acc_out, acc_grad = refs[8:10]
    else:
        acc_out, acc_grad = refs[:2]
    half, width = w0_ref.shape[0], mid_ref.shape[1]
    pre_ref[...] = nn(s_ref[:, :half], w0_ref[:, : 2 * width])
    pre_ref[...] += nn(s_ref[:, half:], w1_ref[:, : 2 * width])
    back_ref[...] = nn(cot_ref[:, :half], w0_ref[:, 2 * width :])
    back_ref[...] += nn(cot_ref[:, half:], w1_ref[:, 2 * width :])
    for c in range(0, width, 128):
        gate, up = pre_ref[:, c : c + 128], pre_ref[:, width + c : width + c + 128]
        back = back_ref[:, c : c + 128]
        gelu_gate, slope = gelu_pair(gate)
        mid_ref[:, c : c + 128] = (gelu_gate * up).astype(bf16)
        ggu_ref[:, c : c + 128] = (back * up * slope).astype(bf16)
        ggu_ref[:, width + c : width + c + 128] = (back * gelu_gate).astype(bf16)
    for lo, w_ref in ((0, w0_ref), (half, w1_ref)):
        cols = slice(lo, lo + half)
        out = nt(mid_ref[...], w_ref[:, 2 * width :])
        acc_out[:, cols] = out if first else in_out[:, cols] + out
        grad = nt(ggu_ref[...], w_ref[:, : 2 * width])
        acc_grad[:, cols] = grad if first else in_grad[:, cols] + grad
    if last:
        split_rows(z_ref, acc_out, out_pieces)
        split_rows(z_ref, acc_grad, grad_pieces)


def grads_out_kernel(sides, *refs):
    lefts, rights, out = refs[:sides], refs[sides : 2 * sides], refs[2 * sides]
    at = 0
    for left, right in zip(lefts, rights):
        half, width = left.shape[1] // 2, right.shape[1]
        out[:, at : at + width] = tn(left[:, half:], right[...]).astype(bf16)
        at += width


def grads_own_kernel(sides, *refs):
    lefts, rights = refs[:sides], refs[sides : 2 * sides]
    got, own, x_top, y_bot, send_x, send_y = refs[2 * sides :]
    at = 0
    q = x_top.shape[0]
    for left, right in zip(lefts, rights):
        half, width = left.shape[1] // 2, right.shape[1]
        cols = slice(at, at + width)
        at += width
        near = tn(left[:, : half // 2], right[...]) + got[: half // 2, cols].astype(f32)
        own[:, cols] = near[: 2 * q]
        x_top[:, cols] = near[2 * q : 3 * q]
        send_x[q:, cols] = near[3 * q :].astype(bf16)
        far = tn(left[:, half // 2 : half], right[...]) + got[half // 2 :, cols].astype(f32)
        send_y[q:, cols] = far[:q].astype(bf16)
        y_bot[:, cols] = far[q : 2 * q]
        send_y[:q, cols] = far[2 * q : 3 * q].astype(bf16)
        send_x[:q, cols] = far[3 * q :].astype(bf16)


def exchange(v, axis, size, bit):
    return lax.ppermute(v, axis, [(i, i ^ bit) for i in range(size)])


def tie(*values):
    return lax.optimization_barrier(values)


def move(size, send_x, send_y):
    if size != 8:
        return send_x, send_y
    return exchange(send_x, "dp", 8, 2), exchange(send_y, "dp", 8, 4)


def stack_sends(parts, more):
    return tuple(jnp.concatenate([a, b], axis=0) for a, b in zip(parts, more))


def cut_sends(got, rows):
    return tuple(v[:rows] for v in got), tuple(v[rows:] for v in got)


class Gather:
    def __init__(self, size):
        self.size = size

    def second(self, by_x, by_y):
        half = by_x.shape[0] // 2
        return by_y[half:], by_x[:half]

    def join(self, shard, first, second):
        if self.size == 8:
            return jnp.concatenate([shard, *first, second[1], second[0]], axis=0)
        mine, bit = shard, 2
        while bit < self.size:
            mine = jnp.concatenate([mine, exchange(mine, "dp", self.size, bit)], axis=0)
            bit *= 2
        return mine

    def other(self, mine):
        return exchange(mine, "dp", self.size, 1)


class Scatter:
    def __init__(self, size, lefts, rights, name):
        self.size, self.name = size, name
        self.lefts, self.rights = lefts, rights
        self.model = lefts[0].shape[1]
        self.width = sum(r.shape[1] for r in rights)
        self.flops = lefts[0].shape[0] * self.model * self.width

    def sibling(self):
        return call(
            partial(grads_out_kernel, len(self.lefts)),
            [like((self.model // 2, self.width), bf16)],
            *self.lefts, *self.rights, flops=self.flops, name="grads_out_" + self.name,
        )[0]

    def swap(self, out):
        return exchange(out, "dp", self.size, 1)

    def own(self, got):
        q, w = self.model // 16, self.width
        return call(
            partial(grads_own_kernel, len(self.lefts)),
            [like((2 * q, w), f32), like((q, w), f32), like((q, w), f32),
             like((2 * q, w), bf16), like((2 * q, w), bf16)],
            *self.lefts, *self.rights, got, flops=self.flops, name="grads_own_" + self.name,
        )

    def second(self, cut, got):
        _, x_top, y_bot, _, _ = cut
        if self.size != 8:
            return x_top.astype(bf16), y_bot.astype(bf16)
        q = x_top.shape[0]
        return (
            (x_top + got[1][:q].astype(f32)).astype(bf16),
            (y_bot + got[0][:q].astype(f32)).astype(bf16),
        )

    def join(self, cut, got, last):
        own, x_top, y_bot, _, _ = cut
        (from_x, from_y), (last_x, last_y) = got, last
        q = x_top.shape[0]
        if self.size == 8:
            return jnp.concatenate(
                [
                    own[:q] + from_y[q:].astype(f32) + last_x.astype(f32),
                    own[q:] + from_x[q:].astype(f32) + last_y.astype(f32),
                ],
                axis=0,
            )
        total = jnp.concatenate(
            [own, x_top, from_x[q:].astype(f32), from_y[q:].astype(f32), y_bot,
             from_y[:q].astype(f32), from_x[:q].astype(f32)],
            axis=0,
        )
        bit = self.size // 2
        while bit > 1:
            half = total.shape[0] // 2
            total = total[:half] + exchange(total[half:].astype(bf16), "dp", self.size, bit).astype(f32)
            bit //= 2
        return total


def to_owner(parts):
    return exchange(parts[3], "tensor", 4, 1), exchange(parts[1], "tensor", 4, 1)


def pass_on(part, got):
    return exchange((part + got.astype(f32)).astype(bf16), "tensor", 4, 2)


def spread(piece):
    return exchange(piece, "tensor", 4, 2), exchange(piece, "tensor", 4, 1)


def neighbour(v):
    return exchange(v, "tensor", 4, 1)


def sum_over(v, axis, size, first=1, until=None):
    bit = first
    while bit < (until or size):
        v = v + exchange(v, axis, size, bit)
        bit *= 2
    return v


def sum_low(v, axis, size, first=1, until=None):
    bit = first
    while bit < (until or size):
        low = v.astype(bf16)
        v = low.astype(f32) + exchange(low, axis, size, bit).astype(f32)
        bit *= 2
    return v


def body(
    tokens, segments, first_gain, x_weight, y_weight, conv_weight, conv_bias, rate_weight,
    input_weight, rate_bias, input_bias, decay_logit, out_weight, second_gain, gate_weight,
    up_weight, down_weight, cotangent, dp_size,
):
    count, model = tokens.shape
    heads, _, units = rate_weight.shape
    chan = heads * units
    pairs = heads // 2
    taps = conv_weight.shape[0]
    hidden_units = gate_weight.shape[1]
    width = hidden_units // chunk_count
    me = lax.axis_index("dp")
    z = lax.axis_index("tensor").astype(jnp.int32)
    z_arr = z.reshape(1)
    part = model // dp_size
    order = [2 * j + c for c in range(2) for j in range(dp_size // 2)]
    rows = count // 4

    def to_rel(v):
        return jnp.concatenate(
            [lax.dynamic_slice_in_dim(v, (me ^ r) * part, part, axis=-1) for r in order], axis=-1
        )

    def to_abs(v):
        places = []
        for s in range(dp_size):
            rel = me ^ s
            places.append((rel % 2) * (dp_size // 2) + rel // 2)
        return jnp.concatenate(
            [lax.dynamic_slice_in_dim(v, p * part, part, axis=-1) for p in places], axis=-1
        )

    gat = Gather(dp_size)
    lane = pl.BlockSpec((count, 128), lambda p: (0, p))
    line = pl.BlockSpec((1, 128), lambda p: (0, p))
    sums_spec = pl.BlockSpec((8, 128), lambda p: (0, p))
    block_spec = pl.BlockSpec((1, 8 * units, 4 * units), lambda p: (p, 0, 0))
    mask_spec = pl.BlockSpec((taps - 1, count, 128), lambda p: (0, 0, 0))

    def product_split(a, w0, w1, at, name):
        return call(
            partial(product_split_kernel, at), [like((rows, model), t) for t in (f32, bf16, f32, bf16)],
            z_arr, a, w0, w1, scalars=1, flops=2 * count * model * a.shape[1],
            scratch=[pltpu.VMEM((count, model), f32)], name=name,
        )

    def assemble(pieces, dtype, name):
        return call(assemble_kernel, [like((count, model), dtype)], z_arr, *pieces, scalars=1, name=name)[0]

    hold = lax.optimization_barrier
    x_flat, y_flat = x_weight.reshape(part, chan), y_weight.reshape(part, chan)
    xyo = jnp.concatenate([x_flat, y_flat, out_weight.reshape(chan, part).T], axis=1)
    xyo_first = move(dp_size, xyo, xyo)
    down_shard = down_weight.T

    def ffn_shard(c):
        cols = slice(c * width, (c + 1) * width)
        return jnp.concatenate([v[:, cols] for v in (gate_weight, up_weight, down_shard)], axis=1)

    x_rel = to_rel(tokens)
    gain_one = to_rel(first_gain).reshape(1, model)
    gain_two = to_rel(second_gain).reshape(1, model)
    nf = call(norm_first_kernel, [like((count, model), bf16)], x_rel, gain_one, name="norm_first")[0]
    f0 = ffn_shard(0)
    xyo_first, x_rel, gain_one, gain_two, nf, f0 = hold((xyo_first, x_rel, gain_one, gain_two, nf, f0))

    xyo_second = move(dp_size, *gat.second(*xyo_first))
    masks = jnp.stack(
        [
            jnp.concatenate([jnp.full((lag,), -1, jnp.int32), segments[:-lag]]) == segments
            for lag in range(1, taps)
        ]
    ).astype(f32)
    masks = jnp.broadcast_to(masks[:, :, None], (taps - 1, count, 128))
    taps_flat = conv_weight.reshape(taps, chan)
    bias_flat = conv_bias.reshape(1, chan)
    rate_flat, input_flat = rate_bias.reshape(1, chan), input_bias.reshape(1, chan)
    decay_flat = decay_logit.reshape(1, chan)
    lines = (masks, taps_flat, bias_flat, rate_flat, input_flat, decay_flat)
    xyo_second, lines = hold((xyo_second, lines))
    masks, taps_flat, bias_flat, rate_flat, input_flat, decay_flat = lines

    f0_first = move(dp_size, f0, f0)
    xyo0 = gat.join(xyo, xyo_first, xyo_second)
    xyo1 = gat.other(xyo0)
    x_branch, y_branch, conv_low = call(
        branches_kernel,
        [like((count, chan), f32), like((count, chan), f32), like((count, chan), bf16)],
        nf, xyo0, xyo1, taps_flat, bias_flat, masks, flops=4 * count * model * chan, name="branches",
    )
    conv2, conv1 = spread(conv_low)
    both = jnp.stack([rate_weight, input_weight], axis=2).reshape(pairs, 2, 4, units, 2, units)
    both = jnp.stack([lax.dynamic_index_in_dim(both, z ^ k, 2, False) for k in range(4)], axis=1)
    zero = jnp.zeros((pairs, 4, units, 2, units), bf16)
    blocks = jnp.stack(
        [jnp.stack([both[:, :, 0], zero], axis=4), jnp.stack([zero, both[:, :, 1]], axis=4)], axis=2
    ).reshape(pairs, 8 * units, 4 * units)
    f1 = ffn_shard(1)
    conv2, conv1, f0_first, blocks, f1 = hold((conv2, conv1, f0_first, blocks, f1))
    conv3 = neighbour(conv2)
    slot = move(dp_size, *stack_sends(gat.second(*f0_first), (f1, f1)))
    cot_rel = to_rel(cotangent)
    f2 = ffn_shard(2)
    conv3, cot_rel, f2 = hold((conv3, cot_rel, f2))
    conv = [conv_low, conv1, conv2, conv3]
    rate, entry, hidden, mixed = pl.pallas_call(
        forward_scan_kernel,
        grid=(pairs,),
        in_specs=[lane] * 4 + [block_spec] + [line] * 3 + [lane, mask_spec],
        out_specs=[lane] * 4,
        out_shape=[like((count, chan), f32)] * 3 + [like((count, chan), bf16)],
        compiler_params=pltpu.CompilerParams(vmem_limit_bytes=60 * MIB),
        cost_estimate=pl.CostEstimate(
            flops=pairs * count * 512 * 256 * 2, bytes_accessed=6 * MIB, transcendentals=0),
        name="forward_scan",
    )(*conv, blocks, rate_flat, input_flat, decay_flat, y_branch, masks)
    parts = product_split(mixed, xyo0, xyo1, 2 * chan, "recurrent")
    got3, got1 = to_owner(parts)
    got2 = pass_on(parts[2], got3)
    got1, got2, slot = hold((got1, got2, slot))

    f0_second, f1_first = cut_sends(slot, part // 2)
    residual, second_rows = call(
        norm_second_kernel, [like((rows, model), f32), like((rows, model), bf16)],
        z_arr, x_rel, gain_two, parts[0], got1, got2, scalars=1, name="norm_second",
    )
    sec2, sec1 = spread(second_rows)
    slot = move(dp_size, *stack_sends(gat.second(*f1_first), (f2, f2)))
    f0_w0 = gat.join(f0, f0_first, f0_second)
    f0_w1 = gat.other(f0_w0)
    sec2, f0_w1 = hold((sec2, f0_w1))
    sec3 = neighbour(sec2)
    second = assemble([second_rows, sec1, sec2, sec3], bf16, "second_all")

    def ffn(c, w0, w1, sums):
        first, last = c == 0, c == chunk_count - 1
        outs = [like((count, 2 * width), bf16), like((count, width), bf16)]
        scratch = [pltpu.VMEM((count, 2 * width), f32), pltpu.VMEM((count, width), f32)]
        if last:
            outs += [like((rows, model), t) for t in (f32, bf16, f32, bf16)] * 2
            scratch = [pltpu.VMEM((count, model), f32)] * 2 + scratch
        else:
            outs += [like((count, model), f32)] * 2
        res = call(
            partial(ffn_kernel, first, last), outs, z_arr, second, cot_rel, w0, w1, *sums,
            scalars=1, flops=12 * count * model * width, scratch=scratch, name="ffn_%d" % c,
        )
        return Scatter(dp_size, [second, cot_rel], res[:2], "ffn_%d" % c), res[2:]

    s0, sums = ffn(0, f0_w0, f0_w1, [])
    s0_out = s0.sibling()
    sums, slot, s0_out = hold((sums, slot, s0_out))
    f1_second, f2_first = cut_sends(slot, part // 2)
    f2_second = move(dp_size, *gat.second(*f2_first))
    f1_w0 = gat.join(f1, f1_first, f1_second)
    f1_w1 = gat.other(f1_w0)
    s0_cut = s0.own(s0.swap(s0_out))
    f1_w1, s0_cut = hold((f1_w1, s0_cut))
    s1, sums = ffn(1, f1_w0, f1_w1, sums)
    sums, f2_second = hold((sums, f2_second))
    f2_w0 = gat.join(f2, f2_first, f2_second)
    f2_w1 = gat.other(f2_w0)
    s0_got = move(dp_size, *s0_cut[3:])
    s1_out = s1.sibling()
    f2_w1, s1_out = hold((f2_w1, s1_out))
    s2, sums = ffn(2, f2_w0, f2_w1, sums)
    out_parts, grad_parts = sums[:4], sums[4:]

    got3, got1 = to_owner(grad_parts)
    s1_cut = s1.own(s1.swap(s1_out))
    got3, s1_cut = hold((got3, s1_cut))
    got2 = pass_on(grad_parts[2], got3)
    s2_out = s2.sibling()
    got1, got2, s0_got, s2_out = hold((got1, got2, s0_got, s2_out))
    slot = move(dp_size, *stack_sends(s0.second(s0_cut, s0_got), s1_cut[3:]))
    grad_res, rec_rows, second_gain_part = call(
        second_back_kernel,
        [like((rows, model), f32), like((rows, model), bf16), like((1, model), f32)],
        z_arr, cot_rel, gain_two, residual, grad_parts[0], got1, got2, scalars=1, name="second_back",
    )
    rec2, rec1 = spread(rec_rows)
    s2_cut = s2.own(s2.swap(s2_out))
    rec2, s2_cut = hold((rec2, s2_cut))
    rec3 = neighbour(rec2)
    out_got = neighbour(jnp.concatenate([out_parts[3], out_parts[1]], axis=0))
    grad_rec = assemble([rec_rows, rec1, rec2, rec3], bf16, "grad_rec_all")

    half_spec = pl.BlockSpec((model // 2, 128), lambda p: (0, 2 * pairs + p))
    whole = pl.BlockSpec((count, model), lambda p: (0, 0))
    gate_spec = pl.BlockSpec((2, 4, units, 2 * units), lambda p: (p, 0, 0, 0))
    grad_y, direct, h1, h2, h3, gate_grads, scan_sums = pl.pallas_call(
        backward_scan_kernel,
        grid=(pairs,),
        in_specs=[whole, half_spec, half_spec] + [lane] * 4 + [block_spec, line, lane, mask_spec]
        + [lane] * 3,
        out_specs=[lane, lane, lane, lane, lane, gate_spec, sums_spec],
        out_shape=[like((count, chan), t) for t in (bf16, f32, bf16, f32, bf16)]
        + [like((heads, 4, units, 2 * units), f32), like((8, chan), f32)],
        compiler_params=pltpu.CompilerParams(vmem_limit_bytes=60 * MIB),
        cost_estimate=pl.CostEstimate(
            flops=2 * count * model * chan + pairs * count * 512 * 256 * 4, bytes_accessed=12 * MIB,
            transcendentals=0),
        name="backward_scan",
    )(grad_rec, xyo0, xyo1, *conv, blocks, decay_flat, y_branch, masks, rate, entry, hidden)
    got3, got1 = to_owner([None, h1, None, h3])
    out_got, slot, got3 = hold((out_got, slot, got3))
    got2 = pass_on(h2, got3)
    s0_last, s1_got = cut_sends(slot, model // 16)
    slot = move(dp_size, *stack_sends(s1.second(s1_cut, s1_got), s2_cut[3:]))
    out_got2 = pass_on(out_parts[2], out_got[:rows])
    gate_sum = sum_low(gate_grads, "dp", dp_size, 1, 2)
    got1, got2, out_got2, gate_sum = hold((got1, got2, out_got2, gate_sum))
    grad_x, conv_sums = pl.pallas_call(
        conv_back_kernel,
        grid=(pairs,),
        in_specs=[lane] * 4 + [pl.BlockSpec((taps, 128), lambda p: (0, p)), mask_spec],
        out_specs=[lane, sums_spec],
        out_shape=[like((count, chan), bf16), like((8, chan), f32)],
        compiler_params=pltpu.CompilerParams(vmem_limit_bytes=60 * MIB),
        cost_estimate=pl.CostEstimate(flops=0, bytes_accessed=4 * MIB, transcendentals=0),
        name="conv_back",
    )(direct, got1, got2, x_branch, taps_flat, masks)
    grad_xy = jnp.concatenate([grad_x, grad_y], axis=1)
    first_parts = product_split(grad_xy, xyo0, xyo1, 0, "grad_first")
    got3, got1 = to_owner(first_parts)
    sxyo = Scatter(dp_size, [nf, grad_rec], [grad_xy, mixed], "xyo")
    sxyo_out = sxyo.sibling()
    block_rows = call(
        block_out_kernel, [like((rows, model), bf16)], residual, out_parts[0], out_got[rows:], out_got2,
        name="block_out",
    )[0]
    block_rows = to_abs(block_rows)
    gate_sum = sum_low(gate_sum, "dp", dp_size, 2, 4)
    got3, slot, sxyo_out, block_rows, gate_sum = hold((got3, slot, sxyo_out, block_rows, gate_sum))
    got2 = pass_on(first_parts[2], got3)
    s1_last, s2_got = cut_sends(slot, model // 16)
    s2_last = move(dp_size, *s2.second(s2_cut, s2_got))
    sxyo_cut = sxyo.own(sxyo.swap(sxyo_out))
    block2 = exchange(block_rows, "tensor", 4, 2)
    small = jnp.concatenate([scan_sums, conv_sums], axis=0)
    small = sum_over(small, "dp", dp_size, 1, 2)
    got1, got2, s2_last, sxyo_cut, block2, small, gate_sum = hold(
        (got1, got2, s2_last, sxyo_cut, block2, small, gate_sum)
    )
    sxyo_got = move(dp_size, *sxyo_cut[3:])
    tokens_rows, first_gain_part = call(
        first_back_kernel, [like((rows, model), bf16), like((1, model), f32)],
        z_arr, x_rel, gain_one, grad_res, first_parts[0], got1, got2, scalars=1, name="first_back",
    )
    tokens_rows = to_abs(tokens_rows)
    tok2, tok1 = spread(tokens_rows)
    block_more = neighbour(jnp.concatenate([block_rows, block2], axis=0))
    ffn_shares = [
        s0.join(s0_cut, s0_got, s0_last),
        s1.join(s1_cut, s1_got, s1_last),
        s2.join(s2_cut, s2_got, s2_last),
    ]
    gate_share, up_share, down_share = [
        jnp.concatenate([s[:, k * width : (k + 1) * width] for s in ffn_shares], axis=1)
        for k in range(3)
    ]
    down_share = down_share.T
    gate_sum = sum_low(gate_sum, "dp", dp_size, 4)
    gate_sum = jnp.concatenate(
        [lax.dynamic_index_in_dim(gate_sum, z ^ k, 1, False) for k in range(4)], axis=1
    )
    small = sum_over(small, "dp", dp_size, 2, 4)
    gains = to_abs(jnp.concatenate([first_gain_part, second_gain_part], axis=0))
    gains = sum_over(gains, "tensor", 4)
    tok2, gate_share, up_share, down_share, gate_sum, small, gains, block_more = hold(
        (tok2, gate_share, up_share, down_share, gate_sum, small, gains, block_more)
    )
    tok3 = neighbour(tok2)
    gains = sum_over(gains, "dp", dp_size, 1, 4)
    small = sum_over(small, "dp", dp_size, 4)
    block_out = assemble(
        [block_rows, block_more[:rows], block2, block_more[rows:]], bf16, "block_out_all"
    )
    tok3, sxyo_got, gains, block_out = hold((tok3, sxyo_got, gains, block_out))
    sxyo_last = move(dp_size, *sxyo.second(sxyo_cut, sxyo_got))
    tokens_grad = assemble([tokens_rows, tok1, tok2, tok3], f32, "tokens_grad_all")
    gains = sum_over(gains, "dp", dp_size, 4)
    xyo_share = sxyo.join(sxyo_cut, sxyo_got, sxyo_last)
    return (
        block_out,
        tokens_grad,
        gains[0],
        xyo_share[:, :chan].reshape(part, heads, units),
        xyo_share[:, chan : 2 * chan].reshape(part, heads, units),
        small[8 : 8 + taps].reshape(taps, heads, units),
        small[8 + taps].reshape(heads, units),
        gate_sum[:, :, :units],
        gate_sum[:, :, units:],
        small[1].reshape(heads, units),
        small[2].reshape(heads, units),
        small[0].reshape(heads, units),
        xyo_share[:, 2 * chan :].T.reshape(heads, units, part),
        gains[1],
        gate_share,
        up_share,
        down_share,
    )


def solution(mesh):
    return jax.shard_map(
        partial(body, dp_size=mesh.shape["dp"]),
        mesh=mesh,
        in_specs=(
            P("dp", None),
            P("dp"),
            P(),
            P("dp", None, "tensor"),
            P("dp", None, "tensor"),
            P(None, None, "tensor"),
            P(None, "tensor"),
            P(None, None, "tensor"),
            P(None, None, "tensor"),
            P(None, "tensor"),
            P(None, "tensor"),
            P(None, "tensor"),
            P(None, "tensor", "dp"),
            P(),
            P("dp", "tensor"),
            P("dp", "tensor"),
            P("tensor", "dp"),
            P("dp", None),
        ),
        out_specs=(
            P("dp", None),
            P("dp", None),
            P(),
            P("dp", None, "tensor"),
            P("dp", None, "tensor"),
            P(None, None, "tensor"),
            P(None, "tensor"),
            P(None, None, "tensor"),
            P(None, None, "tensor"),
            P(None, "tensor"),
            P(None, "tensor"),
            P(None, "tensor"),
            P(None, "tensor", "dp"),
            P(),
            P("dp", "tensor"),
            P("dp", "tensor"),
            P("tensor", "dp"),
        ),
        check_vma=False,
    )
```

```python
from functools import partial

import jax
import jax.numpy as jnp
from jax import lax
from jax.experimental import pallas as pl
from jax.experimental.pallas import tpu as pltpu
from jax.sharding import PartitionSpec as P

eps = 1e-06
f32 = jnp.float32
bf16 = jnp.bfloat16
vmem = pl.BlockSpec(memory_space=pltpu.VMEM)
smem = pl.BlockSpec(memory_space=pltpu.SMEM)
MIB = 1024 * 1024
chunk_count = 3


def nn(a, b):
    return lax.dot_general(a, b, (((1,), (0,)), ((), ())), preferred_element_type=f32)


def nt(a, b):
    return lax.dot_general(a, b, (((1,), (1,)), ((), ())), preferred_element_type=f32)


def tn(a, b):
    return lax.dot_general(a, b, (((0,), (0,)), ((), ())), preferred_element_type=f32)


def full(v):
    zeros = (0,) * len(v.shape)
    return pl.BlockSpec(v.shape, lambda i: zeros, pipeline_mode=pl.Buffered(1))


def block(shape, *index):
    return pl.BlockSpec(shape, lambda i: index)


def hint_of(micros):
    return pl.CostEstimate(
        flops=1, bytes_accessed=max(1, int(micros * 3.0e6)), transcendentals=0
    )


hint = hint_of(0)


def call(kernel, outs, *args, scalars=0, mem=60, specs=None, out_specs=None, alias=None, scratch=(), micros=0, name=None):
    specs = specs or {}
    return pl.pallas_call(
        kernel,
        grid=(1,),
        out_shape=outs,
        in_specs=[smem] * scalars
        + [specs.get(i) or full(a) for i, a in enumerate(args) if i >= scalars],
        out_specs=out_specs or [full(s) for s in outs],
        scratch_shapes=scratch,
        input_output_aliases=alias or {},
        compiler_params=pltpu.CompilerParams(vmem_limit_bytes=mem * MIB),
        cost_estimate=hint_of(micros),
        name=name,
    )(*args)


def like(shape, dtype):
    return jax.ShapeDtypeStruct(shape, dtype)


def gelu_pair(v):
    c = 0.7978845608028654
    sq = v * v
    t = jnp.tanh(c * v * (1.0 + 0.044715 * sq))
    half = 0.5 * (1.0 + t)
    slope = half + 0.5 * v * (1.0 - t * t) * c * (1.0 + 3.0 * 0.044715 * sq)
    return v * half, slope


def one_less_exp(x):
    series = x * (
        1.0
        - x * (1 / 2) * (1.0 - x * (1 / 3) * (1.0 - x * (1 / 4) * (1.0 - x * (1 / 5) * (
            1.0 - x * (1 / 6) * (1.0 - x * (1 / 7) * (1.0 - x * (1 / 8)))))))
    )
    return jnp.where(x < 0.5, series, 1.0 - jnp.exp(-x))


def softplus(v):
    return jnp.maximum(v, 0.0) + jnp.log1p(jnp.exp(-jnp.abs(v)))


def sigmoid(v):
    return 1.0 / (1.0 + jnp.exp(-v))


def row_ids(shape):
    return lax.broadcasted_iota(jnp.int32, shape, 0)


def down_rows(v, steps, fill=0.0):
    return jnp.where(row_ids(v.shape) >= steps, pltpu.roll(v, steps, 0), fill)


def up_rows(v, steps, fill=0.0):
    rows = v.shape[0]
    return jnp.where(row_ids(v.shape) < rows - steps, pltpu.roll(v, rows - steps, 0), fill)


def scan_rows(decay, drive, shift):
    steps = 1
    while steps < decay.shape[0]:
        drive = decay * shift(drive, steps) + drive
        if steps * 2 < decay.shape[0]:
            decay = decay * shift(decay, steps, 1.0)
        steps *= 2
    return drive


def norm_first_kernel(size, z_ref, x_ref, one_ref, two_ref, rel_ref, out_ref, one_out, two_out):
    me = z_ref[1]
    gain = to_rel(me, size, one_ref[...])
    rel = to_rel(me, size, x_ref[...].astype(f32))
    rel_ref[...] = rel.astype(bf16)
    inv = lax.rsqrt(jnp.mean(rel * rel, axis=1, keepdims=True) + eps)
    out_ref[...] = (rel * inv * gain).astype(bf16)
    one_out[...] = gain
    two_out[...] = to_rel(me, size, two_ref[...])


def to_rel_kernel(size, z_ref, x_ref, rel_ref):
    rel_ref[...] = to_rel(z_ref[1], size, x_ref[...].astype(f32)).astype(bf16)


def shard_kernel(gate_ref, up_ref, down_ref, out_ref):
    width = gate_ref.shape[1]
    out_ref[:, :width] = gate_ref[...]
    out_ref[:, width : 2 * width] = up_ref[...]
    out_ref[:, 2 * width :] = down_ref[...]


def blocks_kernel(z_ref, rate_ref, input_ref, out_ref):
    units = rate_ref.shape[1]
    zero = jnp.zeros((units, units), bf16)
    for p in range(out_ref.shape[0]):
        for a in range(2):
            parts = [ref[2 * p + a].T for ref in (rate_ref, input_ref)]
            rows = []
            for k in range(4):
                row = []
                for part in parts:
                    one = jnp.zeros_like(zero)
                    for owner in range(4):
                        one = jnp.where(
                            (z_ref[0] ^ k) == owner, part[owner * units : (owner + 1) * units], one
                        )
                    row += [zero, one] if a else [one, zero]
                at = slice((2 * k + a) * units, (2 * k + a + 1) * units)
                out_ref[p, at, :] = jnp.concatenate(row, axis=1)


def land(pieces, w_ref, sems, first=0):
    copies, at = [], 0
    for n, piece in enumerate(pieces):
        rows = piece.shape[0]
        copy = pltpu.make_async_copy(piece, w_ref.at[pl.ds(at, rows)], sems.at[first + n])
        copy.start()
        copies.append((at, copy))
        at += rows
    return copies


def await_rows(copies, until):
    while copies and copies[0][0] < until:
        copies.pop(0)[1].wait()


def join_kernel(count, *refs):
    pieces, (first, second, sems) = refs[:-3], refs[-3:]
    copies = land(pieces[:count], first, sems) + land(pieces[count:], second, sems, count)
    for _, copy in copies:
        copy.wait()


def branches_kernel(nf_ref, taps_ref, bias_ref, mask_ref, *refs):
    pieces, (x_ref, y_ref, conv_ref, total_ref, w_ref, sems) = refs[:-6], refs[-6:]
    chan = x_ref.shape[1]
    step = w_ref.shape[0] // 4
    copies = land(pieces, w_ref, sems)
    for i in range(4):
        rows = slice(i * step, (i + 1) * step)
        await_rows(copies, (i + 1) * step)
        part = nn(nf_ref[:, rows], w_ref[rows, :])
        total_ref[...] = part if i == 0 else total_ref[...] + part
    both = total_ref[...]
    x_ref[...] = both[:, :chan]
    y_ref[...] = both[:, chan:]
    for c in range(0, chan, 128):
        cols = slice(c, c + 128)
        x = x_ref[:, cols]
        total = x * taps_ref[0:1, cols] + bias_ref[:, cols]
        for lag in range(1, taps_ref.shape[0]):
            total = total + down_rows(x, lag) * mask_ref[lag - 1] * taps_ref[lag : lag + 1, cols]
        conv_ref[:, cols] = total.astype(bf16)


def gates_of(rate, decay_logit, start):
    soft = softplus(-decay_logit)
    minus_log = 8.0 * rate * soft
    lost = one_less_exp(2.0 * minus_log)
    mult = jnp.where(start, 1.0, jnp.sqrt(lost))
    carried = jnp.where(start, 0.0, jnp.exp(-minus_log))
    return soft, mult, carried


def forward_scan_kernel(
    z_ref, c0, c1, c2, c3, block_ref, rb_ref, ib_ref, dl_ref, y_ref, mask_ref, w0, w1, w2, w3,
    rate_ref, entry_ref, hidden_ref, mixed_ref, o0, o1, o2, o3, total_ref,
):
    step, part = pl.program_id(0), w0.shape[0]
    start = mask_ref[0] == 0.0
    pre = nn(jnp.concatenate([c0[...], c1[...], c2[...], c3[...]], axis=1), block_ref[0])
    rate = sigmoid(pre[:, :128] + rb_ref[...])
    entry = sigmoid(pre[:, 128:] + ib_ref[...])
    _, mult, carried = gates_of(rate, dl_ref[...], start)
    driven = c0[...].astype(f32) * entry * mult
    hidden = scan_rows(carried, driven, down_rows)
    rate_ref[...] = rate
    entry_ref[...] = entry
    hidden_ref[...] = hidden
    mixed = (hidden * gelu_pair(y_ref[...])[0]).astype(bf16)
    mixed_ref[...] = mixed
    add_product(step, total_ref, mixed, [(k * part, w[...]) for k, w in enumerate((w0, w1, w2, w3))])

    @pl.when(step == pl.num_programs(0) - 1)
    def _():
        split_rows(z_ref, total_ref, (o0, o1, o2, o3))


def add_product(step, total_ref, left, sides):
    @pl.when(step == 0)
    def _():
        total_ref[...] = jnp.zeros_like(total_ref)

    for at, right in sides:
        total_ref[:, at : at + right.shape[0]] += nt(left, right)


def backward_scan_kernel(
    z_ref, p0, p1, p2, p3, w0, w1, w2, w3, c0, c1, c2, c3, block_ref, dl_ref, y_ref, mask_ref, rate_ref, entry_ref,
    hidden_ref,
    g_ref, gy_ref, direct_ref, h1_ref, h2_ref, h3_ref, mine_ref, theirs_ref, sums_ref,
):
    @pl.when(pl.program_id(0) == 0)
    def _():
        assemble_kernel(z_ref, p0, p1, p2, p3, g_ref)

    start = mask_ref[0] == 0.0
    part = w0.shape[0]
    grad_mixed = nn(g_ref[:, :part], w0[...])
    for k, w in enumerate((w1, w2, w3)):
        grad_mixed += nn(g_ref[:, (k + 1) * part : (k + 2) * part], w[...])
    hidden, rate, entry = hidden_ref[...], rate_ref[...], entry_ref[...]
    conv = c0[...].astype(f32)
    gelu_y, slope_y = gelu_pair(y_ref[...])
    gy_ref[...] = (grad_mixed * hidden * slope_y).astype(bf16)
    decay_logit = dl_ref[...]
    soft, mult, carried = gates_of(rate, decay_logit, start)
    state = scan_rows(up_rows(carried, 1), grad_mixed * gelu_y, up_rows)
    kept = carried * carried
    grad_log = jnp.where(
        start, 0.0, state * (down_rows(hidden, 1) * carried - conv * entry * kept / mult)
    )
    rate_low = (grad_log * (-8.0 * soft) * rate * (1.0 - rate)).astype(bf16)
    entry_low = (state * conv * mult * entry * (1.0 - entry)).astype(bf16)
    both = jnp.concatenate([rate_low, entry_low], axis=1)
    sums_ref[...] = jnp.concatenate(
        [
            jnp.sum(grad_log * rate, axis=0, keepdims=True) * (8.0 * sigmoid(-decay_logit)),
            jnp.sum(rate_low.astype(f32), axis=0, keepdims=True),
            jnp.sum(entry_low.astype(f32), axis=0, keepdims=True),
            jnp.zeros((5, 128), f32),
        ],
        axis=0,
    )
    heads = nt(both, block_ref[0])
    direct_ref[...] = state * entry * mult + heads[:, :128]
    h1_ref[...] = heads[:, 128:256].astype(bf16)
    h2_ref[...] = heads[:, 256:384]
    h3_ref[...] = heads[:, 384:].astype(bf16)
    units = jnp.concatenate([c0[...], c1[...], c2[...], c3[...]], axis=1)
    grads = tn(units, both)
    first = jnp.concatenate([grads[:, 0:64], grads[:, 128:192]], axis=1)
    second = jnp.concatenate([grads[:, 64:128], grads[:, 192:256]], axis=1)
    for k in range(4):
        even, odd = first[k * 128 : k * 128 + 64], second[k * 128 + 64 : k * 128 + 128]
        own = z_ref[1] % 2 == 0
        mine_ref[0, k] = jnp.where(own, even, odd).astype(bf16)
        theirs_ref[0, k] = jnp.where(own, odd, even).astype(bf16)


def conv_back_kernel(
    z_ref, direct_ref, r1, r2, x_ref, taps_ref, mask_ref, gy_ref, wx0, wx1, wy0, wy1,
    gx_ref, sums_ref, o0, o1, o2, o3, total_ref,
):
    step, half = pl.program_id(0), wx0.shape[0]
    total = direct_ref[...] + r1[...].astype(f32) + r2[...].astype(f32)
    x = x_ref[...]
    grad = total * taps_ref[0:1]
    sums = [jnp.sum(total * x, axis=0, keepdims=True)]
    for lag in range(1, taps_ref.shape[0]):
        kept = total * mask_ref[lag - 1]
        grad = grad + up_rows(kept, lag) * taps_ref[lag : lag + 1]
        sums.append(jnp.sum(kept * down_rows(x, lag), axis=0, keepdims=True))
    low = grad.astype(bf16)
    gx_ref[...] = low
    sums.append(jnp.sum(total, axis=0, keepdims=True))
    sums.append(jnp.zeros((8 - len(sums), x.shape[1]), f32))
    sums_ref[...] = jnp.concatenate(sums, axis=0)
    left = jnp.concatenate([low, gy_ref[...]], axis=1)
    first = jnp.concatenate([wx0[...], wy0[...]], axis=1)
    second = jnp.concatenate([wx1[...], wy1[...]], axis=1)
    add_product(step, total_ref, left, ((0, first), (half, second)))

    @pl.when(step == pl.num_programs(0) - 1)
    def _():
        split_rows(z_ref, total_ref, (o0, o1, o2, o3))


def split_rows(z_ref, total_ref, outs):
    rows = next(out for out in outs if out is not None).shape[0]
    for k, out in enumerate(outs):
        if out is None:
            continue
        at = pl.multiple_of((z_ref[0] ^ k) * rows, rows)
        out[...] = total_ref[pl.ds(at, rows), :].astype(out.dtype)


def assemble_kernel(z_ref, p0, p1, p2, p3, out_ref):
    rows = p0.shape[0]
    for k, piece in enumerate((p0, p1, p2, p3)):
        at = pl.multiple_of((z_ref[0] ^ k) * rows, rows)
        out_ref[pl.ds(at, rows), :] = piece[...].astype(out_ref.dtype)


def to_abs(me, size, v):
    part = v.shape[1] // size

    def picked(v, places):
        return jnp.concatenate([v[:, p * part : (p + 1) * part] for p in places], axis=1)

    v = picked(v, [(s % 2) * (size // 2) + s // 2 for s in range(size)])
    bit = 1
    while bit < size:
        v = jnp.where((me // bit) % 2 == 1, picked(v, [s ^ bit for s in range(size)]), v)
        bit *= 2
    return v


def to_rel(me, size, v):
    part = v.shape[1] // size

    def picked(v, places):
        return jnp.concatenate([v[:, p * part : (p + 1) * part] for p in places], axis=1)

    bit = 1
    while bit < size:
        v = jnp.where((me // bit) % 2 == 1, picked(v, [s ^ bit for s in range(size)]), v)
        bit *= 2
    return picked(v, [2 * j + c for c in range(2) for j in range(size // 2)])


def sum_pieces(pieces):
    total = pieces[0][...]
    for piece in pieces[1:]:
        total = total + piece[...].astype(f32)
    return total


def my_rows(z_ref, ref, rows):
    return ref[pl.ds(pl.multiple_of(z_ref[0] * rows, rows), rows), :].astype(f32)


def norm_second_kernel(z_ref, x_ref, gain_ref, o0, o1, o2, res_ref, low_ref):
    residual = my_rows(z_ref, x_ref, res_ref.shape[0]) + sum_pieces((o0, o1, o2))
    inv = lax.rsqrt(jnp.mean(residual * residual, axis=1, keepdims=True) + eps)
    res_ref[...] = residual
    low_ref[...] = (residual * inv * gain_ref[...]).astype(bf16)


def norm_back(x, gain, grad):
    inv = lax.rsqrt(jnp.mean(x * x, axis=1, keepdims=True) + eps)
    unit = x * inv
    scaled = grad * gain
    out = inv * (scaled - unit * jnp.mean(scaled * unit, axis=1, keepdims=True))
    return out, jnp.sum(grad * unit, axis=0, keepdims=True)


def second_back_kernel(size, z_ref, cot_ref, gain_ref, res_ref, o0, o1, o2, gr_ref, low_ref, gain_out):
    grad, gain_grad = norm_back(res_ref[...], gain_ref[...], sum_pieces((o0, o1, o2)))
    grad = grad + my_rows(z_ref, cot_ref, res_ref.shape[0])
    gr_ref[...] = grad
    low_ref[...] = grad.astype(bf16)
    gain_out[...] = to_abs(z_ref[1], size, gain_grad)


def first_back_kernel(size, z_ref, x_ref, gain_ref, gr_ref, o0, o1, o2, out_ref, gain_out):
    x = my_rows(z_ref, x_ref, gr_ref.shape[0])
    grad, gain_grad = norm_back(x, gain_ref[...], sum_pieces((o0, o1, o2)))
    out_ref[...] = to_abs(z_ref[1], size, gr_ref[...] + grad).astype(bf16)
    gain_out[...] = to_abs(z_ref[1], size, gain_grad)


def block_out_kernel(size, z_ref, res_ref, o0, o1, o2, out_ref):
    out_ref[...] = to_abs(z_ref[1], size, res_ref[...] + sum_pieces((o0, o1, o2))).astype(bf16)


def ffn_kernel(groups, first, last, *refs):
    refs = list(refs)

    def take(n):
        taken = refs[:n]
        del refs[:n]
        return taken

    (z_ref,) = take(1)
    if first:
        pieces = take(4)
    else:
        s_any, in_out, in_grad = take(3)
    (cot_any,) = take(1)
    s_ref, cot_ref, pre_ref, back_ref, w_ref, acc_out, acc_grad, sems, out_sems = refs[-9:]
    del refs[-9:]
    n_outs = 2 * groups + (7 if last else 2 + first)
    outs = refs[-n_outs:]
    del refs[-n_outs:]
    per = len(refs) // groups
    rows, width = w_ref.shape[1] // 4, back_ref.shape[1]
    copies = []

    def load(src, dst):
        copy = pltpu.make_async_copy(src, dst, sems.at[len(copies)])
        copy.start()
        copies.append(copy)
        return copy

    held = []
    if not first:
        held.append(load(s_any, s_ref))
    held.append(load(cot_any, cot_ref))
    landing = []
    for g in range(groups):
        at, marks = 0, []
        for piece in refs[g * per : (g + 1) * per]:
            marks.append((at, load(piece, w_ref.at[g, pl.ds(at, piece.shape[0])])))
            at += piece.shape[0]
        landing.append(marks)
    if not first:
        sums = [load(in_out, acc_out), load(in_grad, acc_grad)]
    if first:
        assemble_kernel(z_ref, *pieces, s_ref)
    for copy in held:
        copy.wait()
    stores = []

    def store(src, dst):
        copy = pltpu.make_async_copy(src, dst, out_sems.at[len(stores)])
        copy.start()
        stores.append(copy)

    if first:
        store(s_ref, outs[2 * groups])
    for g in range(groups):
        ggu_ref, mid_ref = outs[2 * g : 2 * g + 2]
        for i in range(4):
            at = slice(i * rows, (i + 1) * rows)
            await_rows(landing[g], (i + 1) * rows)
            pre = nn(s_ref[:, at], w_ref[g, at, : 2 * width])
            back = nn(cot_ref[:, at], w_ref[g, at, 2 * width :])
            if i == 0:
                pre_ref[...] = pre
                back_ref[...] = back
            else:
                pre_ref[...] += pre
                back_ref[...] += back
        for c in range(0, width, 128):
            gate, up = pre_ref[:, c : c + 128], pre_ref[:, width + c : width + c + 128]
            back = back_ref[:, c : c + 128]
            gelu_gate, slope = gelu_pair(gate)
            mid_ref[:, c : c + 128] = (gelu_gate * up).astype(bf16)
            ggu_ref[:, c : c + 128] = (back * up * slope).astype(bf16)
            ggu_ref[:, width + c : width + c + 128] = (back * gelu_gate).astype(bf16)
        if g == 0 and not first:
            for copy in sums:
                copy.wait()
        for i in range(4):
            at = slice(i * rows, (i + 1) * rows)
            grad = nt(ggu_ref[...], w_ref[g, at, : 2 * width])
            out = nt(mid_ref[...], w_ref[g, at, 2 * width :])
            if first and g == 0:
                acc_out[:, at] = out
                acc_grad[:, at] = grad
            else:
                acc_out[:, at] += out
                acc_grad[:, at] += grad
            if g == groups - 1 and not last:
                cols = pl.ds(i * rows, rows)
                store(acc_out.at[:, cols], outs[-2].at[:, cols])
                store(acc_grad.at[:, cols], outs[-1].at[:, cols])
    if last:
        out_parts, grad_parts = outs[2:5], outs[5:9]
        split_rows(z_ref, acc_grad, grad_parts)
        split_rows(z_ref, acc_out, [out_parts[0], None, out_parts[1], None])
        count = out_parts[0].shape[0]
        both = [out_parts[2].at[pl.ds(count, count)], out_parts[2].at[pl.ds(0, count)]]
        split_rows(z_ref, acc_out, [None, both[0], None, both[1]])
    for copy in stores:
        copy.wait()


def grads_out_kernel(sides, *refs):
    lefts, rights, out = refs[:sides], refs[sides : 2 * sides], refs[2 * sides]
    at = 0
    for left, right in zip(lefts, rights):
        width = right.shape[1]
        out[:, at : at + width] = tn(left[...], right[...]).astype(bf16)
        at += width


def grads_own_kernel(sides, room, *refs):
    lefts, rights = refs[:sides], refs[sides : 2 * sides]
    got, own, x_top, y_bot, send_x, send_y = refs[2 * sides :]
    at = 0
    q = x_top.shape[0]
    one, two = [slice((room + k) * q, (room + k + 1) * q) for k in range(2)]
    for left, right in zip(lefts, rights):
        half, width = left.shape[1], right.shape[1]
        cols = slice(at, at + width)
        at += width
        near = tn(left[:, : half // 2], right[...]) + got[: half // 2, cols].astype(f32)
        own[:, cols] = near[: 2 * q]
        x_top[:, cols] = near[2 * q : 3 * q]
        send_x[two, cols] = near[3 * q :].astype(bf16)
        far = tn(left[:, half // 2 :], right[...]) + got[half // 2 :, cols].astype(f32)
        send_y[two, cols] = far[:q].astype(bf16)
        y_bot[:, cols] = far[q : 2 * q]
        send_y[one, cols] = far[2 * q : 3 * q].astype(bf16)
        send_x[one, cols] = far[3 * q :].astype(bf16)


def relay_kernel(groups, has_next, *refs):
    refs = list(refs)
    out_x, out_y = refs[-2:]
    at = 0
    for _ in range(groups):
        x_top, y_bot, got_x, got_y = refs[:4]
        del refs[:4]
        q, cols = x_top.shape[0], slice(at, at + x_top.shape[1])
        out_x[:q, cols] = (x_top[...] + got_y[:, cols].astype(f32)).astype(bf16)
        out_y[:q, cols] = (y_bot[...] + got_x[:, cols].astype(f32)).astype(bf16)
        at += x_top.shape[1]
    at = 0
    for _ in range(has_next):
        send_x, send_y = refs[:2]
        del refs[:2]
        cols = slice(at, at + send_x.shape[1])
        out_x[q:, cols] = send_x[...]
        out_y[q:, cols] = send_y[...]
        at += send_x.shape[1]


def joined(own, got_x, got_y, last_x, last_y, at, cols):
    q = last_x.shape[0]
    top = own[:q, at] + got_y[:, cols].astype(f32) + last_x[:, cols].astype(f32)
    bottom = own[q:, at] + got_x[:, cols].astype(f32) + last_y[:, cols].astype(f32)
    return jnp.concatenate([top, bottom], axis=0)


def join_ffn_kernel(*refs):
    gate_ref, up_ref, down_ref = refs[-3:]
    for c in range(chunk_count):
        parts = refs[5 * c : 5 * c + 5]
        width = parts[0].shape[1] // 3
        at = slice(c * width, (c + 1) * width)
        gate, up, down = [slice(k * width, (k + 1) * width) for k in range(3)]
        gate_ref[:, at] = joined(*parts, gate, gate)
        up_ref[:, at] = joined(*parts, up, up)
        down_ref[:, at] = joined(*parts, down, down)


def add_kernel(a_ref, b_ref, out_ref):
    out_ref[...] = (a_ref[...].astype(f32) + b_ref[...].astype(f32)).astype(out_ref.dtype)


def gate_join_kernel(z_ref, mine_ref, other_ref, rate_ref, input_ref):
    pairs, _, units, _ = mine_ref.shape
    core = z_ref[1] % 2
    for src, head in ((mine_ref, core), (other_ref, 1 - core)):
        for p in range(pairs):
            whole = jnp.concatenate([src[p, z_ref[0] ^ owner] for owner in range(4)], axis=0)
            rate_ref[2 * p + head] = whole[:, :units].T
            input_ref[2 * p + head] = whole[:, units:].T


def relay_mixed_kernel(x_top, y_bot, got_x, got_y, send_x, send_y, out_x, out_y):
    q, width = x_top.shape[0], out_x.shape[1]
    for k in range(x_top.shape[1] // width):
        rows, cols = slice(k * q, (k + 1) * q), slice(k * width, (k + 1) * width)
        out_x[rows, :] = (x_top[:, cols] + got_y[:, cols].astype(f32)).astype(bf16)
        out_y[rows, :] = (y_bot[:, cols] + got_x[:, cols].astype(f32)).astype(bf16)
    out_x[(k + 1) * q :, :] = send_x[...]
    out_y[(k + 1) * q :, :] = send_y[...]


def join_yox_kernel(yo_own, x_own, yo_got_x, yo_got_y, y_x, y_y, o_x, o_y, x_got_x, x_got_y, x_x, x_y,
                    x_ref, y_ref, out_ref):
    width = x_ref.shape[0]
    first, second = slice(0, width), slice(width, 2 * width)
    y_ref[...] = joined(yo_own, yo_got_x[:, first], yo_got_y[:, first], y_x, y_y, first, first).T
    out_ref[...] = joined(
        yo_own, yo_got_x[:, second], yo_got_y[:, second], o_x, o_y, second, first
    ).T
    x_ref[...] = joined(x_own, x_got_x, x_got_y, x_x, x_y, first, first).T


def exchange(v, axis, size, bit):
    return lax.ppermute(v, axis, [(i, i ^ bit) for i in range(size)])


def tie(*values):
    return lax.optimization_barrier(values)


def along(size, bit, v):
    return exchange(v, "dp", 8, bit) if size == 8 else v


def move(size, send_x, send_y):
    return along(size, 2, send_x), along(size, 4, send_y)


def gather_all(shard, size):
    mine, bit = shard, 2
    while bit < size:
        mine = jnp.concatenate([mine, exchange(mine, "dp", size, bit)], axis=0)
        bit *= 2
    return [mine], [exchange(mine, "dp", size, 1)]


class Scatter:
    def __init__(self, size, lefts, rights, name):
        self.size, self.name = size, name
        self.lefts, self.rights = lefts, rights
        self.model = lefts[0].shape[1]
        self.width = sum(r.shape[1] for r in rights)

    def halves(self, side):
        tokens = self.lefts[0].shape[0]
        return {i: block((tokens, self.model // 2), 0, side) for i in range(len(self.lefts))}

    def sibling(self, run, micros=0):
        return run(
            partial(grads_out_kernel, len(self.lefts)),
            [like((self.model // 2, self.width), bf16)],
            *self.lefts, *self.rights, specs=self.halves(1), micros=micros,
            name="grads_out_" + self.name,
        )[0]

    def swap(self, out):
        return exchange(out, "dp", self.size, 1)

    def own(self, run, got, room=0):
        q, w = self.model // 16, self.width
        sends = [like(((2 + room) * q, w), bf16)] * 2
        return run(
            partial(grads_own_kernel, len(self.lefts), room),
            [like((2 * q, w), f32), like((q, w), f32), like((q, w), f32)] + sends,
            *self.lefts, *self.rights, got, specs=self.halves(0), name="grads_own_" + self.name,
        )

    def join(self, cut):
        own, x_top, y_bot, from_x, from_y = cut
        q = x_top.shape[0]
        from_x, from_y = from_x[-2 * q :], from_y[-2 * q :]
        total = jnp.concatenate(
            [own, x_top, from_x[q:].astype(f32), from_y[q:].astype(f32), y_bot,
             from_y[:q].astype(f32), from_x[:q].astype(f32)],
            axis=0,
        )
        bit = self.size // 2
        while bit > 1:
            half = total.shape[0] // 2
            total = total[:half] + exchange(total[half:].astype(bf16), "dp", self.size, bit).astype(f32)
            bit //= 2
        return total


def relay(run, cuts, got, base, nexts, name):
    q = cuts[0][1].shape[0]
    width = sum(cut[1].shape[1] for cut in cuts)
    ins, specs, options = [], {}, {}
    for cut in cuts:
        ins += [cut[1], cut[2]]
        for v in got:
            specs[len(ins)] = block((q, v.shape[1]), base, 0)
            ins.append(v)
    if len(nexts) == 1:
        options = dict(
            alias={len(ins): 0, len(ins) + 1: 1}, out_specs=[block((q, width), 0, 0)] * 2
        )
        specs[len(ins)] = specs[len(ins) + 1] = pl.BlockSpec(memory_space=pl.ANY)
    for cut in nexts:
        ins += [cut[3], cut[4]]
    return run(
        partial(relay_kernel, len(cuts), 0 if len(nexts) == 1 else len(nexts)),
        [like((3 * q if nexts else q, width), bf16)] * 2, *ins, specs=specs, name=name, **options,
    )


def to_owner(part):
    return exchange(part, "tensor", 4, 1)


def pass_on(part, got):
    return exchange((part + got.astype(f32)).astype(bf16), "tensor", 4, 2)


class Order:
    def __init__(self):
        self.last = None

    def after(self, *values):
        if self.last is not None:
            values, _ = lax.optimization_barrier((values, self.last))
        return values if len(values) > 1 else values[0]

    def wait(self, *values):
        values = self.after(*values)
        self.last = jax.tree.leaves(values)[0]
        return values

    def run(self, kernel, outs, *args, **options):
        results = call(kernel, outs, *self.after(*args), **options)
        self.last = results[0]
        return results


def spread(piece):
    return exchange(piece, "tensor", 4, 2), exchange(piece, "tensor", 4, 1)


def neighbour(v):
    return exchange(v, "tensor", 4, 1)


def sum_over(v, axis, size, first=1, until=None):
    bit = first
    while bit < (until or size):
        v = v + exchange(v, axis, size, bit)
        bit *= 2
    return v


def sum_low(v, axis, size, first=1, until=None):
    bit = first
    while bit < (until or size):
        low = v.astype(bf16)
        v = low.astype(f32) + exchange(low, axis, size, bit).astype(f32)
        bit *= 2
    return v


def body(
    tokens, segments, first_gain, x_weight, y_weight, conv_weight, conv_bias, rate_weight,
    input_weight, rate_bias, input_bias, decay_logit, out_weight, second_gain, gate_weight,
    up_weight, down_weight, cotangent, dp_size,
):
    count, model = tokens.shape
    heads, _, units = rate_weight.shape
    chan = heads * units
    pairs = heads // 2
    taps = conv_weight.shape[0]
    hidden_units = gate_weight.shape[1]
    width = hidden_units // chunk_count
    me = lax.axis_index("dp")
    z = lax.axis_index("tensor").astype(jnp.int32)
    ids = jnp.stack([z, me.astype(jnp.int32)])
    part = model // dp_size
    q = model // 16
    rows = count // 4
    size = dp_size
    order = Order()
    after, wait, run = order.after, order.wait, order.run
    anywhere = pl.BlockSpec(memory_space=pl.ANY)
    lane = pl.BlockSpec((count, 128), lambda p: (0, p))
    line = pl.BlockSpec((1, 128), lambda p: (0, p))
    sums_spec = pl.BlockSpec((8, 128), lambda p: (0, p))
    block_spec = pl.BlockSpec((1, 8 * units, 4 * units), lambda p: (p, 0, 0))
    mask_spec = pl.BlockSpec((taps - 1, count, 128), lambda p: (0, 0, 0))
    pair_grid = dict(
        grid=(pairs,), cost_estimate=hint,
        compiler_params=pltpu.CompilerParams(vmem_limit_bytes=60 * MIB),
    )
    split_shapes = [like((rows, model), t) for t in (f32, bf16, f32, bf16)]
    split_specs = [pl.BlockSpec((rows, model), lambda p: (0, 0))] * 4
    total_scratch = [pltpu.VMEM((count, model), f32)]

    out_block = pl.BlockSpec((model // 4, 128), lambda p: (0, p))

    def weight_block(at):
        return pl.BlockSpec((model // 2, 128), lambda p: (0, at * pairs + p))

    def sibling(v):
        return exchange(v, "dp", size, 1)

    def halves(by_x, by_y):
        half = by_x.shape[0] // 2
        lower, upper = move(size, by_y[half:], by_x[:half])
        return upper, lower

    def pieces_of(shard, *got):
        if size == 8:
            return [shard, *got[: len(got) // 2]], list(got[len(got) // 2 :])
        return gather_all(shard, size)

    def assemble(pieces, dtype, name):
        return run(
            assemble_kernel, [like((count, model), dtype)], ids, *pieces, scalars=1, name=name
        )[0]

    x_flat, y_flat = x_weight.reshape(part, chan), y_weight.reshape(part, chan)
    out_shard = out_weight.reshape(chan, part).T
    half = part // 2
    xy_t = jnp.concatenate([x_flat[:half], y_flat[:half]], axis=1)
    xy_b = jnp.concatenate([x_flat[half:], y_flat[half:]], axis=1)
    xt, yt = move(size, xy_t, xy_t)
    xb, yb = move(size, xy_b, xy_b)

    def ffn_shard(c):
        cols = block((part, width), 0, c)
        return run(
            shard_kernel, [like((part, 3 * width), bf16)], gate_weight, up_weight, down_weight.T,
            specs={0: cols, 1: cols, 2: cols}, name="shard",
        )[0]

    x_rel, nf, gain_one, gain_two = run(
        partial(norm_first_kernel, size),
        [like((count, model), bf16)] * 2 + [like((1, model), f32)] * 2,
        ids, tokens, first_gain.reshape(1, model), second_gain.reshape(1, model), scalars=1,
        name="norm_first",
    )
    f0, f1 = ffn_shard(0), ffn_shard(1)
    xt, xb, yt, yb, out_shard = wait(xt, xb, yt, yb, out_shard)

    top, bot = along(size, 4, xt), along(size, 2, yb)
    st, sb, sxt = sibling(xy_t), sibling(xy_b), sibling(xt)
    (cot_rel,) = run(
        partial(to_rel_kernel, size), [like((count, model), bf16)], ids, cotangent, scalars=1,
        name="cotangent",
    )
    segs = after(segments)
    masks = jnp.stack(
        [
            jnp.concatenate([jnp.full((lag,), -1, jnp.int32), segs[:-lag]]) == segs
            for lag in range(1, taps)
        ]
    ).astype(f32)
    masks = jnp.broadcast_to(masks[:, :, None], (taps - 1, count, 128))
    taps_flat = conv_weight.reshape(taps, chan)
    bias_flat = conv_bias.reshape(1, chan)
    rate_flat, input_flat = rate_bias.reshape(1, chan), input_bias.reshape(1, chan)
    decay_flat = decay_logit.reshape(1, chan)
    masks, taps_flat, bias_flat, rate_flat, input_flat, decay_flat, top, bot, st, sb, sxt = wait(
        masks, taps_flat, bias_flat, rate_flat, input_flat, decay_flat, top, bot, st, sb, sxt
    )
    sxb, syt, syb = sibling(after(xb)), sibling(after(yt)), sibling(after(yb))
    s_top, s_bot = sibling(top), sibling(bot)
    sxb, syt, syb, s_top, s_bot = wait(sxb, syt, syb, s_top, s_bot)
    out_x, out_y = move(size, out_shard, out_shard)
    if size == 8:
        own_w = [xy_t, xy_b, xt, xb, yt, yb, top, bot]
        sib_w = [st, sb, sxt, sxb, syt, syb, s_top, s_bot]
    else:
        own_w, sib_w = gather_all(jnp.concatenate([xy_t, xy_b], axis=0), size)
    all_w = own_w + sib_w
    x_branch, y_branch, conv_low = run(
        branches_kernel,
        [like((count, chan), f32), like((count, chan), f32), like((count, chan), bf16)],
        nf, taps_flat, bias_flat, masks, *all_w,
        specs={4 + i: anywhere for i in range(len(all_w))},
        scratch=[
            pltpu.VMEM((count, 2 * chan), f32),
            pltpu.VMEM((model, 2 * chan), bf16),
            pltpu.SemaphoreType.DMA((len(all_w),)),
        ],
        name="branches",
    )
    conv_low, out_x, out_y = wait(conv_low, out_x, out_y)
    conv2, conv1 = spread(conv_low)
    out_far = along(size, 2, out_y)
    f0_x, f0_y = move(size, *after(f0, f0))
    xy0, xy1 = run(
        partial(join_kernel, len(own_w)), [like((model // 2, 2 * chan), bf16)] * 2, *all_w,
        specs={i: anywhere for i in range(len(all_w))},
        scratch=[pltpu.SemaphoreType.DMA((len(all_w),))], name="join_xy",
    )
    (blocks,) = run(
        blocks_kernel, [like((pairs, 8 * units, 4 * units), bf16)], ids,
        rate_weight.transpose(0, 2, 1), input_weight.transpose(0, 2, 1),
        scalars=1, name="gate_blocks",
    )
    conv2, conv1, out_far = wait(conv2, conv1, out_far)
    conv3 = neighbour(conv2)
    if size == 8:
        pieces = [out_shard, out_x, out_y, out_far]
        outs = run(
            partial(join_kernel, 2), [like((model // 4, chan), bf16)] * 2, *pieces,
            specs={i: anywhere for i in range(4)}, scratch=[pltpu.SemaphoreType.DMA((4,))],
            name="join_out",
        )
    else:
        whole_out = gather_all(out_shard, size)[0][0]
        outs = [whole_out[: model // 4], whole_out[model // 4 :]]
    outs = [*outs, *[sibling(v) for v in outs]]
    conv3, f0_x, f0_y, outs = wait(conv3, f0_x, f0_y, outs)
    conv = [conv_low, conv1, conv2, conv3]
    f0_s, f1_s = [sibling(v) for v in after(f0, f1)]
    f1_x, f1_y = move(size, f1, after(f1))
    f0_sx = sibling(f0_x)
    rate, entry, hidden, mixed, *parts = pl.pallas_call(
        forward_scan_kernel,
        in_specs=[smem] + [lane] * 4 + [block_spec] + [line] * 3 + [lane, mask_spec]
        + [out_block] * 4,
        out_specs=[lane] * 4 + split_specs,
        out_shape=[like((count, chan), t) for t in (f32, f32, f32, bf16)] + split_shapes,
        scratch_shapes=total_scratch,
        name="forward_scan",
        **pair_grid,
    )(ids, *conv, blocks, rate_flat, input_flat, decay_flat, y_branch, masks, *outs)
    order.last = rate
    parts, f0_s, f1_s, f0_sx = wait(tuple(parts), f0_s, f1_s, f0_sx)
    got3 = to_owner(parts[3])
    f0_sy = sibling(after(f0_y))
    got3, f0_sy = wait(got3, f0_sy)
    got2, got1 = pass_on(parts[2], got3), to_owner(after(parts[1]))
    got2, got1, f1_x, f1_y = wait(got2, got1, f1_x, f1_y)
    f0_far, f1_far = along(size, 2, after(f0_y)), along(size, 4, f1_x)
    f1_sx, f1_sy = sibling(f1_x), sibling(f1_y)
    residual, second_rows = run(
        norm_second_kernel, [like((rows, model), f32), like((rows, model), bf16)],
        ids, x_rel, gain_two, parts[0], got1, got2, scalars=1, name="norm_second",
    )
    second_rows, f1_sx, f1_sy = wait(second_rows, f1_sx, f1_sy)
    sec2, sec1 = spread(second_rows)
    f2 = ffn_shard(2)
    sec2, sec1 = wait(sec2, sec1)
    sec3 = neighbour(sec2)
    sec3, f0_far, f1_far = wait(sec3, f0_far, f1_far)
    f2_x, f2_y = move(size, *after(f2, f2))
    f0_sf, f1_sf, f2_s = sibling(f0_far), sibling(f1_far), sibling(after(f2))
    f0_sf, f1_sf, f2_s = wait(f0_sf, f1_sf, f2_s)

    def ffn(left, groups, sums, first, last, name):
        outs = [like((count, 2 * width), bf16), like((count, width), bf16)] * len(groups)
        out_specs = [full(v) for v in outs]
        if first:
            outs.append(like((count, model), bf16))
            out_specs.append(anywhere)
        if last:
            more = [like((rows, model), f32)] * 2 + [like((2 * rows, model), bf16)] + split_shapes
            outs += more
            out_specs += [full(v) for v in more]
        else:
            outs += [like((count, model), f32)] * 2
            out_specs += [anywhere] * 2
        weights = sum([own + sib for own, sib in groups], [])
        scratch = [
            pltpu.VMEM((count, model), bf16),
            pltpu.VMEM((count, model), bf16),
            pltpu.VMEM((count, 2 * width), f32),
            pltpu.VMEM((count, width), f32),
            pltpu.VMEM((len(groups), model, 3 * width), bf16),
            pltpu.VMEM((count, model), f32),
            pltpu.VMEM((count, model), f32),
            pltpu.SemaphoreType.DMA((len(weights) + 4,)),
            pltpu.SemaphoreType.DMA((9,)),
        ]
        ins = [ids, *left, *sums, cot_rel, *weights]
        at = 1 + len(left) * first
        return run(
            partial(ffn_kernel, len(groups), first, last), outs, *ins, scalars=1, scratch=scratch,
            specs={i: anywhere for i in range(at, len(ins))}, out_specs=out_specs, name=name,
        )

    a, b, c, d, second, *sums = ffn(
        [second_rows, sec1, sec2, sec3],
        [
            pieces_of(f0, f0_x, f0_y, f0_far, f0_s, f0_sx, f0_sy, f0_sf),
            pieces_of(f1, f1_x, f1_y, f1_far, f1_s, f1_sx, f1_sy, f1_sf),
        ],
        [], True, False, "ffn_01",
    )
    s0 = Scatter(size, [second, cot_rel], [a, b], "ffn_0")
    s1 = Scatter(size, [second, cot_rel], [c, d], "ffn_1")
    s0_out = s0.sibling(run)
    s0_out, f2_x, f2_y = wait(s0_out, f2_x, f2_y)
    f2_top, f2_bot = halves(f2_x, f2_y)
    f2_sx, f2_sy = sibling(f2_x), sibling(f2_y)
    s0_swap = s0.swap(s0_out)
    s1_out = s1.sibling(run)
    f2_sx, f2_sy, s0_swap = wait(f2_sx, f2_sy, s0_swap)
    s0_cut = s0.own(run, s0_swap)
    f2_top, f2_bot, s0_send = wait(f2_top, f2_bot, tuple(s0_cut[3:]))
    f2_st, f2_sb = sibling(f2_top), sibling(f2_bot)
    f2_st, f2_sb = wait(f2_st, f2_sb)
    s0_got = move(size, *after(*s0_send))
    s1_swap = s1.swap(after(s1_out))
    a, b, *sums = ffn(
        [second],
        [pieces_of(f2, f2_x, f2_y, f2_top, f2_bot, f2_s, f2_sx, f2_sy, f2_st, f2_sb)], sums, False,
        True, "ffn_2",
    )
    s2 = Scatter(size, [second, cot_rel], [a, b], "ffn_2")
    out_parts, grad_parts, s1_swap = wait(tuple(sums[:3]), tuple(sums[3:]), s1_swap)

    got3, got1 = to_owner(grad_parts[3]), to_owner(grad_parts[1])
    s1_cut = s1.own(run, s1_swap, 1)
    s2_out = s2.sibling(run)
    got3, s0_got, s2_out = wait(got3, s0_got, s2_out)
    got2 = pass_on(grad_parts[2], got3)
    slot1 = move(size, *relay(run, [s0_cut], s0_got, 0, [s1_cut], "relay_0"))
    s2_swap = s2.swap(s2_out)
    got2, got1, s2_swap = wait(got2, got1, s2_swap)
    grad_res, rec_rows, second_gain = run(
        partial(second_back_kernel, size),
        [like((rows, model), f32), like((rows, model), bf16), like((1, model), f32)],
        ids, cot_rel, gain_two, residual, grad_parts[0], got1, got2, scalars=1, micros=6, name="second_back",
    )
    rec2, rec1 = spread(rec_rows)
    s2_cut = s2.own(run, s2_swap, 1)
    rec2, rec1 = wait(rec2, rec1)
    rec3 = neighbour(rec2)
    rec3, slot1 = wait(rec3, slot1)
    out_got = neighbour(after(out_parts[2]))
    slot2 = move(size, *relay(run, [s1_cut], slot1, 1, [s2_cut], "relay_1"))

    whole = pl.BlockSpec((count, model), lambda p: (0, 0))
    piece = pl.BlockSpec((rows, model), lambda p: (0, 0))
    gate_spec = pl.BlockSpec((1, 4, units, 2 * units), lambda p: (p, 0, 0, 0))
    gate_half = like((pairs, 4, units, 2 * units), bf16)
    grad_rec, grad_y, direct, h1, h2, h3, gate_mine, gate_theirs, scan_sums = pl.pallas_call(
        backward_scan_kernel,
        in_specs=[smem] + [piece] * 4 + [out_block] * 4 + [lane] * 4
        + [block_spec, line, lane, mask_spec] + [lane] * 3,
        out_specs=[whole, lane, lane, lane, lane, lane, gate_spec, gate_spec, sums_spec],
        out_shape=[like((count, model), bf16)]
        + [like((count, chan), t) for t in (bf16, f32, bf16, f32, bf16)]
        + [gate_half, gate_half, like((8, chan), f32)],
        name="backward_scan",
        **pair_grid,
    )(
        *after(ids, rec_rows, rec1, rec2, rec3, *outs, *conv, blocks, decay_flat, y_branch, masks),
        rate, entry, hidden,
    )
    order.last = grad_rec
    out_got, h1, h2, h3 = wait(out_got, h1, h2, h3)
    got3 = to_owner(h3)
    out_got2 = pass_on(out_parts[1], out_got[:rows])
    gate_got = sibling(gate_theirs)
    syo = Scatter(size, [nf, grad_rec], [grad_y, mixed], "yo")
    syo_out = syo.sibling(run)
    got3, syo_out, gate_got = wait(got3, syo_out, gate_got)
    got2, got1 = pass_on(h2, got3), to_owner(after(h1))
    (gate_sum,) = run(add_kernel, [gate_half], gate_mine, gate_got, name="gate_add")
    got2, got1, slot2, out_got2 = wait(got2, got1, slot2, out_got2)
    syo_swap = syo.swap(after(syo_out))
    gate_got = along(size, 2, after(gate_sum))
    grad_x, conv_sums, *first_parts = pl.pallas_call(
        conv_back_kernel,
        in_specs=[smem] + [lane] * 4 + [pl.BlockSpec((taps, 128), lambda p: (0, p)), mask_spec, lane]
        + [weight_block(0)] * 2 + [weight_block(1)] * 2,
        out_specs=[lane, sums_spec] + split_specs,
        out_shape=[like((count, chan), bf16), like((8, chan), f32)] + split_shapes,
        scratch_shapes=total_scratch,
        name="conv_back",
        **pair_grid,
    )(*after(ids, direct, got1, got2, x_branch, taps_flat, masks, grad_y, xy0, xy1, xy0, xy1))
    order.last = grad_x
    first_parts, syo_swap, gate_got = wait(tuple(first_parts), syo_swap, gate_got)
    got3 = to_owner(first_parts[3])
    sx = Scatter(size, [nf], [grad_x], "x")
    sx_out = sx.sibling(run)
    syo_cut = syo.own(run, syo_swap)
    got3, sx_out, yo_send = wait(got3, sx_out, tuple(syo_cut[3:]))
    got2, got1 = pass_on(first_parts[2], got3), to_owner(after(first_parts[1]))
    sx_swap = sx.swap(sx_out)
    yo_got = move(size, *yo_send)
    s2_send = relay(run, [s2_cut], slot2, 1, [], "relay_2")
    (block_rows,) = run(
        partial(block_out_kernel, size), [like((rows, model), bf16)],
        ids, residual, out_parts[0], out_got[rows:], out_got2, scalars=1, name="block_out",
    )
    (gate_sum2,) = run(add_kernel, [gate_half], gate_sum, gate_got, name="gate_add")
    got2, got1, sx_swap, yo_got = wait(got2, got1, sx_swap, yo_got)
    tokens_rows, first_gain_part = run(
        partial(first_back_kernel, size), [like((rows, model), bf16), like((1, model), f32)],
        ids, x_rel, gain_one, grad_res, first_parts[0], got1, got2, scalars=1, name="first_back",
    )
    tok2, tok1 = spread(tokens_rows)
    s2_last = move(size, *after(*s2_send))
    sx_cut = sx.own(run, sx_swap)
    specs = {k: block((q, 2 * chan), 0, 0) for k in (2, 3)}
    mixed_sends = run(
        relay_mixed_kernel, [like((4 * q, chan), bf16)] * 2, syo_cut[1], syo_cut[2], *yo_got,
        *sx_cut[3:], specs=specs, name="relay_3",
    )
    tok2, tok1, s2_last, mixed_sends = wait(tok2, tok1, s2_last, tuple(mixed_sends))
    tok3 = neighbour(tok2)
    slot3 = move(size, *mixed_sends)
    block2 = exchange(after(block_rows), "tensor", 4, 2)
    gains = jnp.concatenate([first_gain_part, second_gain], axis=0)
    gains = sum_over(after(gains), "tensor", 4, 1, 2)
    if size == 8:
        ins, specs = [], {}
        for cut, (got, base), last in (
            (s0_cut, (s0_got, 0), slot1), (s1_cut, (slot1, 1), slot2), (s2_cut, (slot2, 1), s2_last)
        ):
            ins.append(cut[0])
            for v, at in ((got[0], base + 1), (got[1], base + 1), (last[0], 0), (last[1], 0)):
                specs[len(ins)] = block((q, v.shape[1]), at, 0)
                ins.append(v)
        gate_share, up_share, down_share = run(
            join_ffn_kernel,
            [like((part, hidden_units), f32)] * 3,
            *ins, specs=specs, name="join_ffn",
        )
    else:
        shares = [s0.join(s0_cut), s1.join(s1_cut), s2.join(s2_cut)]
        gate_share, up_share, down_share = [
            jnp.concatenate([v[:, k * width : (k + 1) * width] for v in shares], axis=1)
            for k in range(3)
        ]
    tok3, gains, slot3, block2 = wait(tok3, gains, slot3, block2)
    x_last = move(size, *relay(run, [sx_cut], slot3, 2, [], "relay_4"))
    block1, block3 = neighbour(after(block_rows)), neighbour(block2)
    gains = sum_over(gains, "tensor", 4, 2)
    tokens_grad = assemble([tokens_rows, tok1, tok2, tok3], f32, "tokens_grad_all")
    gains, x_last = wait(gains, x_last)
    gate_got = along(size, 4, after(gate_sum2))
    small = jnp.concatenate([scan_sums, conv_sums, gains.reshape(8, chan)], axis=0)
    small = sum_over(small, "dp", size, 1, 2)
    small, gate_got = wait(small, gate_got)
    (gate_sum,) = run(
        add_kernel, [like(gate_half.shape, f32)], gate_sum2, gate_got, name="gate_add"
    )
    gate_got = sibling(gate_sum)
    if size == 8:
        by_x, by_y, across = [exchange(small, "dp", size, bit) for bit in (2, 4, 6)]
        ins = [syo_cut[0], sx_cut[0], *yo_got, *slot3, *slot3, *slot3, *x_last]
        specs = {2: block((q, 2 * chan), 1, 0), 3: block((q, 2 * chan), 1, 0)}
        for k, at in enumerate((0, 0, 1, 1, 3, 3, 0, 0)):
            specs[4 + k] = block((q, chan), at, 0)
        x_share, y_share, out_share = run(
            join_yox_kernel, [like((chan, part), f32)] * 3, *ins,
            specs=specs, name="join_yox",
        )
        gate_got = wait(gate_got)
        rate_grad, input_grad = run(
            gate_join_kernel, [like((heads, units, 4 * units), f32)] * 2, ids, gate_sum, gate_got,
            scalars=1, name="gate_join",
        )
        rate_grad, input_grad = rate_grad.transpose(0, 2, 1), input_grad.transpose(0, 2, 1)
        by_x, by_y, across = wait(by_x, by_y, across)
        small = (small + by_x) + (by_y + across)
    else:
        small = sum_over(small, "dp", size, 2)
        yo_share, x_share = syo.join(syo_cut), sx.join(sx_cut)
        x_share, y_share, out_share = x_share.T, yo_share[:, :chan].T, yo_share[:, chan:].T
        mine = sum_low(gate_mine + sibling(gate_theirs), "dp", size, 2)
        other, core = sibling(mine), me % 2
        gate_sum = jnp.stack(
            [jnp.where(core == 0, mine, other), jnp.where(core == 0, other, mine)], axis=1
        ).reshape(heads, 4, units, 2 * units)
        gate_sum = jnp.concatenate(
            [lax.dynamic_index_in_dim(gate_sum, z ^ k, 1, False) for k in range(4)], axis=1
        )
        rate_grad, input_grad = gate_sum[:, :, :units], gate_sum[:, :, units:]
    block1, block3 = wait(block1, block3)
    block_out = assemble([block_rows, block1, block2, block3], bf16, "block_out_all")
    x_share = x_share.reshape(heads, units, part).transpose(2, 0, 1)
    y_share = y_share.reshape(heads, units, part).transpose(2, 0, 1)
    gains = small[16:].reshape(2, model)
    return (
        block_out,
        tokens_grad,
        gains[0],
        x_share,
        y_share,
        small[8 : 8 + taps].reshape(taps, heads, units),
        small[8 + taps].reshape(heads, units),
        rate_grad,
        input_grad,
        small[1].reshape(heads, units),
        small[2].reshape(heads, units),
        small[0].reshape(heads, units),
        out_share.reshape(heads, units, part),
        gains[1],
        gate_share,
        up_share,
        down_share.T,
    )


def solution(mesh):
    return jax.shard_map(
        partial(body, dp_size=mesh.shape["dp"]),
        mesh=mesh,
        in_specs=(
            P("dp", None),
            P("dp"),
            P(),
            P("dp", None, "tensor"),
            P("dp", None, "tensor"),
            P(None, None, "tensor"),
            P(None, "tensor"),
            P(None, None, "tensor"),
            P(None, None, "tensor"),
            P(None, "tensor"),
            P(None, "tensor"),
            P(None, "tensor"),
            P(None, "tensor", "dp"),
            P(),
            P("dp", "tensor"),
            P("dp", "tensor"),
            P("tensor", "dp"),
            P("dp", None),
        ),
        out_specs=(
            P("dp", None),
            P("dp", None),
            P(),
            P("dp", None, "tensor"),
            P("dp", None, "tensor"),
            P(None, None, "tensor"),
            P(None, "tensor"),
            P(None, None, "tensor"),
            P(None, None, "tensor"),
            P(None, "tensor"),
            P(None, "tensor"),
            P(None, "tensor"),
            P(None, "tensor", "dp"),
            P(),
            P("dp", "tensor"),
            P("dp", "tensor"),
            P("tensor", "dp"),
        ),
        check_vma=False,
    )
```

```python
from functools import partial

import jax
import jax.numpy as jnp
from jax import lax
from jax.experimental import pallas as pl
from jax.experimental.pallas import tpu as pltpu
from jax.sharding import PartitionSpec as P

eps = 1e-06
f32 = jnp.float32
bf16 = jnp.bfloat16
vmem = pl.BlockSpec(memory_space=pltpu.VMEM)
smem = pl.BlockSpec(memory_space=pltpu.SMEM)
MIB = 1024 * 1024
chunk_count = 3


def nn(a, b):
    return lax.dot_general(a, b, (((1,), (0,)), ((), ())), preferred_element_type=f32)


def nt(a, b):
    return lax.dot_general(a, b, (((1,), (1,)), ((), ())), preferred_element_type=f32)


def tn(a, b):
    return lax.dot_general(a, b, (((0,), (0,)), ((), ())), preferred_element_type=f32)


def full(v):
    zeros = (0,) * len(v.shape)
    return pl.BlockSpec(v.shape, lambda i: zeros, pipeline_mode=pl.Buffered(1))


def block(shape, *index):
    return pl.BlockSpec(shape, lambda i: index)


def hint_of(micros):
    return pl.CostEstimate(
        flops=1, bytes_accessed=max(1, int(micros * 3.0e6)), transcendentals=0
    )


hint = hint_of(0)


def call(kernel, outs, *args, scalars=0, mem=60, specs=None, out_specs=None, alias=None, scratch=(), micros=0, name=None):
    specs = specs or {}
    return pl.pallas_call(
        kernel,
        grid=(1,),
        out_shape=outs,
        in_specs=[smem] * scalars
        + [specs.get(i) or full(a) for i, a in enumerate(args) if i >= scalars],
        out_specs=out_specs or [full(s) for s in outs],
        scratch_shapes=scratch,
        input_output_aliases=alias or {},
        compiler_params=pltpu.CompilerParams(vmem_limit_bytes=mem * MIB),
        cost_estimate=hint_of(micros),
        name=name,
    )(*args)


def like(shape, dtype):
    return jax.ShapeDtypeStruct(shape, dtype)


def gelu_pair(v):
    c = 0.7978845608028654
    sq = v * v
    t = jnp.tanh(c * v * (1.0 + 0.044715 * sq))
    half = 0.5 * (1.0 + t)
    slope = half + 0.5 * v * (1.0 - t * t) * c * (1.0 + 3.0 * 0.044715 * sq)
    return v * half, slope


def one_less_exp(x):
    series = x * (
        1.0
        - x * (1 / 2) * (1.0 - x * (1 / 3) * (1.0 - x * (1 / 4) * (1.0 - x * (1 / 5) * (
            1.0 - x * (1 / 6) * (1.0 - x * (1 / 7) * (1.0 - x * (1 / 8)))))))
    )
    return jnp.where(x < 0.5, series, 1.0 - jnp.exp(-x))


def softplus(v):
    return jnp.maximum(v, 0.0) + jnp.log1p(jnp.exp(-jnp.abs(v)))


def sigmoid(v):
    return 1.0 / (1.0 + jnp.exp(-v))


def row_ids(shape):
    return lax.broadcasted_iota(jnp.int32, shape, 0)


def down_rows(v, steps, fill=0.0):
    return jnp.where(row_ids(v.shape) >= steps, pltpu.roll(v, steps, 0), fill)


def up_rows(v, steps, fill=0.0):
    rows = v.shape[0]
    return jnp.where(row_ids(v.shape) < rows - steps, pltpu.roll(v, rows - steps, 0), fill)


def scan_rows(decay, drive, shift):
    steps = 1
    while steps < decay.shape[0]:
        drive = decay * shift(drive, steps) + drive
        if steps * 2 < decay.shape[0]:
            decay = decay * shift(decay, steps, 1.0)
        steps *= 2
    return drive


def norm_first_kernel(size, z_ref, x_ref, one_ref, two_ref, rel_ref, out_ref, one_out, two_out):
    me = z_ref[1]
    gain = to_rel(me, size, one_ref[...])
    rel = to_rel(me, size, x_ref[...].astype(f32))
    rel_ref[...] = rel.astype(bf16)
    inv = lax.rsqrt(jnp.mean(rel * rel, axis=1, keepdims=True) + eps)
    out_ref[...] = (rel * inv * gain).astype(bf16)
    one_out[...] = gain
    two_out[...] = to_rel(me, size, two_ref[...])


def to_rel_kernel(size, z_ref, x_ref, rel_ref):
    rel_ref[...] = to_rel(z_ref[1], size, x_ref[...].astype(f32)).astype(bf16)


def shard_kernel(gate_ref, up_ref, down_ref, out_ref):
    width = gate_ref.shape[1]
    out_ref[:, :width] = gate_ref[...]
    out_ref[:, width : 2 * width] = up_ref[...]
    out_ref[:, 2 * width :] = down_ref[...]


def blocks_kernel(z_ref, rate_ref, input_ref, out_ref):
    units = rate_ref.shape[1]
    zero = jnp.zeros((units, units), bf16)
    for p in range(out_ref.shape[0]):
        for a in range(2):
            parts = [ref[2 * p + a].T for ref in (rate_ref, input_ref)]
            rows = []
            for k in range(4):
                row = []
                for part in parts:
                    one = jnp.zeros_like(zero)
                    for owner in range(4):
                        one = jnp.where(
                            (z_ref[0] ^ k) == owner, part[owner * units : (owner + 1) * units], one
                        )
                    row += [zero, one] if a else [one, zero]
                at = slice((2 * k + a) * units, (2 * k + a + 1) * units)
                out_ref[p, at, :] = jnp.concatenate(row, axis=1)


def land(pieces, w_ref, sems, first=0):
    copies, at = [], 0
    for n, piece in enumerate(pieces):
        rows = piece.shape[0]
        copy = pltpu.make_async_copy(piece, w_ref.at[pl.ds(at, rows)], sems.at[first + n])
        copy.start()
        copies.append((at, copy))
        at += rows
    return copies


def await_rows(copies, until):
    while copies and copies[0][0] < until:
        copies.pop(0)[1].wait()


def join_kernel(count, *refs):
    pieces, (first, second, sems) = refs[:-3], refs[-3:]
    copies = land(pieces[:count], first, sems) + land(pieces[count:], second, sems, count)
    for _, copy in copies:
        copy.wait()


def branches_kernel(nf_ref, taps_ref, bias_ref, mask_ref, *refs):
    pieces, (x_ref, y_ref, conv_ref, total_ref, w_ref, sems) = refs[:-6], refs[-6:]
    chan = x_ref.shape[1]
    step = w_ref.shape[0] // 4
    copies = land(pieces, w_ref, sems)
    for i in range(4):
        rows = slice(i * step, (i + 1) * step)
        await_rows(copies, (i + 1) * step)
        part = nn(nf_ref[:, rows], w_ref[rows, :])
        total_ref[...] = part if i == 0 else total_ref[...] + part
    both = total_ref[...]
    x_ref[...] = both[:, :chan]
    y_ref[...] = both[:, chan:]
    for c in range(0, chan, 128):
        cols = slice(c, c + 128)
        x = x_ref[:, cols]
        total = x * taps_ref[0:1, cols] + bias_ref[:, cols]
        for lag in range(1, taps_ref.shape[0]):
            total = total + down_rows(x, lag) * mask_ref[lag - 1] * taps_ref[lag : lag + 1, cols]
        conv_ref[:, cols] = total.astype(bf16)


def gates_of(rate, decay_logit, start):
    soft = softplus(-decay_logit)
    minus_log = 8.0 * rate * soft
    lost = one_less_exp(2.0 * minus_log)
    mult = jnp.where(start, 1.0, jnp.sqrt(lost))
    carried = jnp.where(start, 0.0, jnp.exp(-minus_log))
    return soft, mult, carried


def forward_scan_kernel(
    z_ref, c0, c1, c2, c3, block_ref, rb_ref, ib_ref, dl_ref, y_ref, mask_ref, w0, w1, w2, w3,
    rate_ref, entry_ref, hidden_ref, mixed_ref, o0, o1, o2, o3, total_ref, w_ref, left_ref, sems,
):
    step = pl.program_id(0)
    landing = fetch(step, (w0, w1, w2, w3), w_ref, sems)
    start = mask_ref[0] == 0.0
    pre = nn(jnp.concatenate([c0[...], c1[...], c2[...], c3[...]], axis=1), block_ref[0])
    rate = sigmoid(pre[:, :128] + rb_ref[...])
    entry = sigmoid(pre[:, 128:] + ib_ref[...])
    _, mult, carried = gates_of(rate, dl_ref[...], start)
    driven = c0[...].astype(f32) * entry * mult
    hidden = scan_rows(carried, driven, down_rows)
    rate_ref[...] = rate
    entry_ref[...] = entry
    hidden_ref[...] = hidden
    mixed = (hidden * gelu_pair(y_ref[...])[0]).astype(bf16)
    mixed_ref[...] = mixed
    left_ref[:, pl.ds(pl.multiple_of(step * 128, 128), 128)] = mixed

    @pl.when(step == pl.num_programs(0) - 1)
    def _():
        product(landing, left_ref, w_ref, total_ref)
        split_rows(z_ref, total_ref, (o0, o1, o2, o3))


def fetch(step, pieces, w_ref, sems):
    copies, at = [], 0
    for n, piece in enumerate(pieces):
        rows = piece.shape[0]
        copies.append(pltpu.make_async_copy(piece, w_ref.at[pl.ds(at, rows)], sems.at[n]))
        at += rows

    @pl.when(step == 0)
    def _():
        for copy in copies:
            copy.start()

    return copies


def product(landing, left_ref, w_ref, total_ref):
    for copy in landing:
        copy.wait()
    rows = w_ref.shape[0] // 4
    for i in range(4):
        at = slice(i * rows, (i + 1) * rows)
        total_ref[:, at] = nt(left_ref[...], w_ref[at, :])


def backward_scan_kernel(
    z_ref, p0, p1, p2, p3, w0, w1, w2, w3, c0, c1, c2, c3, block_ref, dl_ref, y_ref, mask_ref, rate_ref, entry_ref,
    hidden_ref,
    g_ref, gy_ref, direct_ref, h1_ref, h2_ref, h3_ref, mine_ref, theirs_ref, sums_ref,
):
    @pl.when(pl.program_id(0) == 0)
    def _():
        assemble_kernel(z_ref, p0, p1, p2, p3, g_ref)

    start = mask_ref[0] == 0.0
    part = w0.shape[0]
    grad_mixed = nn(g_ref[:, :part], w0[...])
    for k, w in enumerate((w1, w2, w3)):
        grad_mixed += nn(g_ref[:, (k + 1) * part : (k + 2) * part], w[...])
    hidden, rate, entry = hidden_ref[...], rate_ref[...], entry_ref[...]
    conv = c0[...].astype(f32)
    gelu_y, slope_y = gelu_pair(y_ref[...])
    gy_ref[...] = (grad_mixed * hidden * slope_y).astype(bf16)
    decay_logit = dl_ref[...]
    soft, mult, carried = gates_of(rate, decay_logit, start)
    state = scan_rows(up_rows(carried, 1), grad_mixed * gelu_y, up_rows)
    kept = carried * carried
    grad_log = jnp.where(
        start, 0.0, state * (down_rows(hidden, 1) * carried - conv * entry * kept / mult)
    )
    rate_low = (grad_log * (-8.0 * soft) * rate * (1.0 - rate)).astype(bf16)
    entry_low = (state * conv * mult * entry * (1.0 - entry)).astype(bf16)
    both = jnp.concatenate([rate_low, entry_low], axis=1)
    sums_ref[...] = jnp.concatenate(
        [
            jnp.sum(grad_log * rate, axis=0, keepdims=True) * (8.0 * sigmoid(-decay_logit)),
            jnp.sum(rate_low.astype(f32), axis=0, keepdims=True),
            jnp.sum(entry_low.astype(f32), axis=0, keepdims=True),
            jnp.zeros((5, 128), f32),
        ],
        axis=0,
    )
    heads = nt(both, block_ref[0])
    direct_ref[...] = state * entry * mult + heads[:, :128]
    h1_ref[...] = heads[:, 128:256].astype(bf16)
    h2_ref[...] = heads[:, 256:384]
    h3_ref[...] = heads[:, 384:].astype(bf16)
    units = jnp.concatenate([c0[...], c1[...], c2[...], c3[...]], axis=1)
    grads = tn(units, both)
    first = jnp.concatenate([grads[:, 0:64], grads[:, 128:192]], axis=1)
    second = jnp.concatenate([grads[:, 64:128], grads[:, 192:256]], axis=1)
    for k in range(4):
        even, odd = first[k * 128 : k * 128 + 64], second[k * 128 + 64 : k * 128 + 128]
        own = z_ref[1] % 2 == 0
        mine_ref[0, k] = jnp.where(own, even, odd).astype(bf16)
        theirs_ref[0, k] = jnp.where(own, odd, even).astype(bf16)


def conv_back_kernel(
    size, z_ref, direct_ref, r1, r2, x_ref, taps_ref, mask_ref, gy_ref, rel_ref, w0, w1,
    gx_ref, sums_ref, gain_ref, o0, o1, o2, o3, total_ref, w_ref, left_ref, sems,
):
    step = pl.program_id(0)
    landing = fetch(step, (w0, w1), w_ref, sems)
    chan = left_ref.shape[1] // 2
    total = direct_ref[...] + r1[...].astype(f32) + r2[...].astype(f32)
    x = x_ref[...]
    grad = total * taps_ref[0:1]
    sums = [jnp.sum(total * x, axis=0, keepdims=True)]
    for lag in range(1, taps_ref.shape[0]):
        kept = total * mask_ref[lag - 1]
        grad = grad + up_rows(kept, lag) * taps_ref[lag : lag + 1]
        sums.append(jnp.sum(kept * down_rows(x, lag), axis=0, keepdims=True))
    low = grad.astype(bf16)
    gx_ref[...] = low
    sums.append(jnp.sum(total, axis=0, keepdims=True))
    sums.append(jnp.zeros((8 - len(sums), x.shape[1]), f32))
    sums_ref[...] = jnp.concatenate(sums, axis=0)
    left_ref[:, pl.ds(pl.multiple_of(step * 128, 128), 128)] = low
    left_ref[:, pl.ds(pl.multiple_of(chan + step * 128, 128), 128)] = gy_ref[...]

    @pl.when(step == pl.num_programs(0) - 1)
    def _():
        product(landing, left_ref, w_ref, total_ref)
        split_rows(z_ref, total_ref, (o0, o1, o2, o3))
        rel = rel_ref[...].astype(f32)
        inv = lax.rsqrt(jnp.mean(rel * rel, axis=1, keepdims=True) + eps)
        gain = jnp.sum(total_ref[...] * (rel * inv), axis=0, keepdims=True)
        gain_ref[...] = to_abs(z_ref[1], size, gain)


def split_rows(z_ref, total_ref, outs):
    rows = outs[0].shape[0]
    for k, out in enumerate(outs):
        at = pl.multiple_of((z_ref[0] ^ k) * rows, rows)
        out[...] = total_ref[pl.ds(at, rows), :].astype(out.dtype)


def assemble_kernel(z_ref, *refs):
    pieces, out_ref = refs[:-1], refs[-1]
    rows = pieces[0].shape[0]
    for k, piece in enumerate(pieces):
        at = pl.multiple_of((z_ref[0] ^ k) * rows, rows)
        out_ref[pl.ds(at, rows), :] = piece[...].astype(out_ref.dtype)


def to_abs(me, size, v):
    part = v.shape[1] // size

    def picked(v, places):
        return jnp.concatenate([v[:, p * part : (p + 1) * part] for p in places], axis=1)

    v = picked(v, [(s % 2) * (size // 2) + s // 2 for s in range(size)])
    bit = 1
    while bit < size:
        v = jnp.where((me // bit) % 2 == 1, picked(v, [s ^ bit for s in range(size)]), v)
        bit *= 2
    return v


def to_rel(me, size, v):
    part = v.shape[1] // size

    def picked(v, places):
        return jnp.concatenate([v[:, p * part : (p + 1) * part] for p in places], axis=1)

    bit = 1
    while bit < size:
        v = jnp.where((me // bit) % 2 == 1, picked(v, [s ^ bit for s in range(size)]), v)
        bit *= 2
    return picked(v, [2 * j + c for c in range(2) for j in range(size // 2)])


def sum_pieces(pieces):
    total = pieces[0][...]
    for piece in pieces[1:]:
        total = total + piece[...].astype(f32)
    return total


def my_rows(z_ref, ref, rows):
    return ref[pl.ds(pl.multiple_of(z_ref[0] * rows, rows), rows), :].astype(f32)


def norm_second_kernel(z_ref, x_ref, gain_ref, o0, o1, o2, res_ref, low_ref):
    residual = my_rows(z_ref, x_ref, res_ref.shape[0]) + sum_pieces((o0, o1, o2))
    inv = lax.rsqrt(jnp.mean(residual * residual, axis=1, keepdims=True) + eps)
    res_ref[...] = residual
    low_ref[...] = (residual * inv * gain_ref[...]).astype(bf16)


def norm_back(x, gain, grad):
    inv = lax.rsqrt(jnp.mean(x * x, axis=1, keepdims=True) + eps)
    unit = x * inv
    scaled = grad * gain
    out = inv * (scaled - unit * jnp.mean(scaled * unit, axis=1, keepdims=True))
    return out, jnp.sum(grad * unit, axis=0, keepdims=True)


def second_back_kernel(size, z_ref, cot_ref, gain_ref, res_ref, o0, o1, o2, gr_ref, low_ref, gain_out):
    grad, gain_grad = norm_back(res_ref[...], gain_ref[...], sum_pieces((o0, o1, o2)))
    grad = grad + my_rows(z_ref, cot_ref, res_ref.shape[0])
    gr_ref[...] = grad
    low_ref[...] = grad.astype(bf16)
    gain_out[...] = to_abs(z_ref[1], size, gain_grad)


def first_back_kernel(size, z_ref, x_ref, gain_ref, gr_ref, o0, o1, o2, out_ref):
    x = my_rows(z_ref, x_ref, gr_ref.shape[0])
    grad, _ = norm_back(x, gain_ref[...], sum_pieces((o0, o1, o2)))
    out_ref[...] = to_abs(z_ref[1], size, gr_ref[...] + grad).astype(bf16)


def block_out_kernel(size, z_ref, res_ref, o0, o1, o2, out_ref):
    out_ref[...] = to_abs(z_ref[1], size, res_ref[...] + sum_pieces((o0, o1, o2))).astype(bf16)


def ffn_kernel(groups, first, last, *refs):
    refs = list(refs)

    def take(n):
        taken = refs[:n]
        del refs[:n]
        return taken

    (z_ref,) = take(1)
    if first:
        pieces = take(4)
    else:
        s_any, in_grad = take(2)
    (cot_any,) = take(1)
    s_ref, cot_ref, pre_ref, back_ref, w_ref, acc_grad, sems, out_sems = refs[-8:]
    del refs[-8:]
    n_outs = 2 * groups + (4 if last else 1 + first)
    outs = refs[-n_outs:]
    del refs[-n_outs:]
    per = len(refs) // groups
    rows, width = w_ref.shape[1] // 4, back_ref.shape[1]
    copies = []

    def load(src, dst):
        copy = pltpu.make_async_copy(src, dst, sems.at[len(copies)])
        copy.start()
        copies.append(copy)
        return copy

    held = []
    if not first:
        held.append(load(s_any, s_ref))
    held.append(load(cot_any, cot_ref))
    landing = []
    for g in range(groups):
        at, marks = 0, []
        for piece in refs[g * per : (g + 1) * per]:
            marks.append((at, load(piece, w_ref.at[g, pl.ds(at, piece.shape[0])])))
            at += piece.shape[0]
        landing.append(marks)
    if not first:
        sums = load(in_grad, acc_grad)
    if first:
        assemble_kernel(z_ref, *pieces, s_ref)
    for copy in held:
        copy.wait()
    stores = []

    def store(src, dst):
        copy = pltpu.make_async_copy(src, dst, out_sems.at[len(stores)])
        copy.start()
        stores.append(copy)

    if first:
        store(s_ref, outs[2 * groups])
    for g in range(groups):
        ggu_ref, mid_ref = outs[2 * g : 2 * g + 2]
        for i in range(4):
            at = slice(i * rows, (i + 1) * rows)
            await_rows(landing[g], (i + 1) * rows)
            pre = nn(s_ref[:, at], w_ref[g, at, : 2 * width])
            back = nn(cot_ref[:, at], w_ref[g, at, 2 * width :])
            if i == 0:
                pre_ref[...] = pre
                back_ref[...] = back
            else:
                pre_ref[...] += pre
                back_ref[...] += back
        for c in range(0, width, 128):
            gate, up = pre_ref[:, c : c + 128], pre_ref[:, width + c : width + c + 128]
            back = back_ref[:, c : c + 128]
            gelu_gate, slope = gelu_pair(gate)
            mid_ref[:, c : c + 128] = (gelu_gate * up).astype(bf16)
            ggu_ref[:, c : c + 128] = (back * up * slope).astype(bf16)
            ggu_ref[:, width + c : width + c + 128] = (back * gelu_gate).astype(bf16)
        if g == 0 and not first:
            sums.wait()
        for i in range(4):
            at = slice(i * rows, (i + 1) * rows)
            grad = nt(ggu_ref[...], w_ref[g, at, : 2 * width])
            if first and g == 0:
                acc_grad[:, at] = grad
            else:
                acc_grad[:, at] += grad
            if g == groups - 1 and not last:
                cols = pl.ds(i * rows, rows)
                store(acc_grad.at[:, cols], outs[-1].at[:, cols])
    if last:
        split_rows(z_ref, acc_grad, outs[2:6])
    for copy in stores:
        copy.wait()


def ffn_out_kernel(counts, z_ref, *refs):
    groups = len(counts)
    mids, refs = refs[:groups], refs[groups:]
    own, pass_part, both, w_ref, total_ref, sems = refs[-6:]
    pieces, width = list(refs[:-6]), mids[0].shape[1]
    copies, ends = [], []
    for g in range(groups):
        at = 0
        for piece in [pieces.pop(0) for _ in range(counts[g])]:
            copy = pltpu.make_async_copy(
                piece.at[:, pl.ds(2 * width, width)], w_ref.at[g, pl.ds(at, piece.shape[0])],
                sems.at[len(copies)],
            )
            copy.start()
            copies.append(copy)
            at += piece.shape[0]
        ends.append(len(copies))
    rows = w_ref.shape[1] // 4
    for g in range(groups):
        for copy in copies[ends[g] - counts[g] : ends[g]]:
            copy.wait()
        for i in range(4):
            at = slice(i * rows, (i + 1) * rows)
            out = nt(mids[g][...], w_ref[g, at, :])
            total_ref[:, at] = out if g == 0 else total_ref[:, at] + out
    count = own.shape[0]
    split_rows(
        z_ref, total_ref,
        [own, both.at[pl.ds(count, count)], pass_part, both.at[pl.ds(0, count)]],
    )


def grads_out_kernel(sides, *refs):
    lefts, rights, out = refs[:sides], refs[sides : 2 * sides], refs[2 * sides]
    held, sems = refs[2 * sides + 1 :]
    step = held.shape[0] // 2
    stores = []
    for part in range(2):
        rows, at = slice(part * step, (part + 1) * step), 0
        for left, right in zip(lefts, rights):
            width = right.shape[1]
            held[rows, at : at + width] = tn(left[:, rows], right[...]).astype(bf16)
            at += width
        copy = pltpu.make_async_copy(
            held.at[pl.ds(part * step, step)], out.at[pl.ds(part * step, step)], sems.at[part]
        )
        copy.start()
        stores.append(copy)
    for copy in stores:
        copy.wait()


def grads_own_kernel(sides, room, *refs):
    lefts, rights = refs[:sides], refs[sides : 2 * sides]
    got_any, own, x_top, y_bot, send_x, send_y = refs[2 * sides : 2 * sides + 6]
    got, grads, low, sems = refs[2 * sides + 6 :]
    q = x_top.shape[0]
    loads = [
        pltpu.make_async_copy(
            got_any.at[pl.ds(part * 4 * q, 4 * q)], got.at[pl.ds(part * 4 * q, 4 * q)], sems.at[part]
        )
        for part in range(2)
    ]
    for copy in loads:
        copy.start()
    stores = []

    def store(src, row, count, dst, to):
        copy = pltpu.make_async_copy(
            src.at[pl.ds(row * q, count * q)], dst.at[pl.ds(to * q, count * q)],
            sems.at[2 + len(stores)],
        )
        copy.start()
        stores.append(copy)

    for part in range(2):
        rows, at = slice(part * 4 * q, (part + 1) * 4 * q), 0
        loads[part].wait()
        for left, right in zip(lefts, rights):
            cols = slice(at, at + right.shape[1])
            at += right.shape[1]
            grads[rows, cols] = tn(left[:, rows], right[...]) + got[rows, cols].astype(f32)
        if part == 0:
            low[:q, :] = grads[3 * q : 4 * q, :].astype(bf16)
            store(grads, 0, 2, own, 0)
            store(grads, 2, 1, x_top, 0)
            store(low, 0, 1, send_x, room + 1)
        else:
            low[q : 2 * q, :] = grads[4 * q : 5 * q, :].astype(bf16)
            low[2 * q :, :] = grads[6 * q :, :].astype(bf16)
            store(low, 1, 1, send_y, room + 1)
            store(grads, 5, 1, y_bot, 0)
            store(low, 2, 1, send_y, room)
            store(low, 3, 1, send_x, room)
    for copy in stores:
        copy.wait()


def relay_kernel(groups, has_next, *refs):
    refs = list(refs)
    out_x, out_y = refs[-2:]
    at = 0
    for _ in range(groups):
        x_top, y_bot, got_x, got_y = refs[:4]
        del refs[:4]
        q, cols = x_top.shape[0], slice(at, at + x_top.shape[1])
        out_x[:q, cols] = (x_top[...] + got_y[:, cols].astype(f32)).astype(bf16)
        out_y[:q, cols] = (y_bot[...] + got_x[:, cols].astype(f32)).astype(bf16)
        at += x_top.shape[1]
    at = 0
    for _ in range(has_next):
        send_x, send_y = refs[:2]
        del refs[:2]
        cols = slice(at, at + send_x.shape[1])
        out_x[q:, cols] = send_x[...]
        out_y[q:, cols] = send_y[...]
        at += send_x.shape[1]


def joined(own, got_x, got_y, last_x, last_y, at, cols):
    q = last_x.shape[0]
    top = own[:q, at] + got_y[:, cols].astype(f32) + last_x[:, cols].astype(f32)
    bottom = own[q:, at] + got_x[:, cols].astype(f32) + last_y[:, cols].astype(f32)
    return jnp.concatenate([top, bottom], axis=0)


def join_ffn_kernel(*refs):
    gate_ref, up_ref, down_ref = refs[-3:]
    for c in range(chunk_count):
        parts = refs[5 * c : 5 * c + 5]
        width = parts[0].shape[1] // 3
        at = slice(c * width, (c + 1) * width)
        gate, up, down = [slice(k * width, (k + 1) * width) for k in range(3)]
        gate_ref[:, at] = joined(*parts, gate, gate)
        up_ref[:, at] = joined(*parts, up, up)
        down_ref[:, at] = joined(*parts, down, down)


def add_kernel(a_ref, b_ref, out_ref):
    out_ref[...] = (a_ref[...].astype(f32) + b_ref[...].astype(f32)).astype(out_ref.dtype)


def small_kernel(units, sums_ref, by_x, by_y, across, taps_ref, bias_ref, rate_ref, input_ref, decay_ref, one_ref, two_ref):
    total = (sums_ref[...] + by_x[...]) + (by_y[...] + across[...])
    heads, taps, _ = taps_ref.shape
    for h in range(heads):
        cols = slice(h * units, (h + 1) * units)
        taps_ref[h] = total[8 : 8 + taps, cols]
        bias_ref[h : h + 1, :] = total[8 + taps : 9 + taps, cols]
        rate_ref[h : h + 1, :] = total[1:2, cols]
        input_ref[h : h + 1, :] = total[2:3, cols]
        decay_ref[h : h + 1, :] = total[0:1, cols]
    wide = total.shape[1]
    for k in range(4):
        one_ref[k * wide : (k + 1) * wide] = total[16 + k]
        two_ref[k * wide : (k + 1) * wide] = total[20 + k]


def gate_join_kernel(z_ref, mine_ref, other_ref, rate_ref, input_ref):
    pairs, _, units, _ = mine_ref.shape
    core = z_ref[1] % 2
    for src, head in ((mine_ref, core), (other_ref, 1 - core)):
        for p in range(pairs):
            whole = jnp.concatenate([src[p, z_ref[0] ^ owner] for owner in range(4)], axis=0)
            rate_ref[2 * p + head] = whole[:, :units].T
            input_ref[2 * p + head] = whole[:, units:].T


def relay_mixed_kernel(x_top, y_bot, got_x, got_y, send_x, send_y, out_x, out_y):
    q, width = x_top.shape[0], out_x.shape[1]
    for k in range(x_top.shape[1] // width):
        rows, cols = slice(k * q, (k + 1) * q), slice(k * width, (k + 1) * width)
        out_x[rows, :] = (x_top[:, cols] + got_y[:, cols].astype(f32)).astype(bf16)
        out_y[rows, :] = (y_bot[:, cols] + got_x[:, cols].astype(f32)).astype(bf16)
    out_x[(k + 1) * q :, :] = send_x[...]
    out_y[(k + 1) * q :, :] = send_y[...]


def join_yo_kernel(yo_own, yo_got_x, yo_got_y, y_x, y_y, o_x, o_y, y_ref, out_ref):
    width = y_ref.shape[0]
    first, second = slice(0, width), slice(width, 2 * width)
    y_ref[...] = joined(yo_own, yo_got_x[:, first], yo_got_y[:, first], y_x, y_y, first, first).T
    out_ref[...] = joined(
        yo_own, yo_got_x[:, second], yo_got_y[:, second], o_x, o_y, second, first
    ).T


def join_x_kernel(own, got_x, got_y, last_x, last_y, out_ref):
    cols = slice(0, out_ref.shape[0])
    out_ref[...] = joined(own, got_x, got_y, last_x, last_y, cols, cols).T


def exchange(v, axis, size, bit):
    return lax.ppermute(v, axis, [(i, i ^ bit) for i in range(size)])


def tie(*values):
    return lax.optimization_barrier(values)


def along(size, bit, v):
    return exchange(v, "dp", 8, bit) if size == 8 else v


def move(size, send_x, send_y):
    return along(size, 2, send_x), along(size, 4, send_y)


def gather_all(shard, size):
    mine, bit = shard, 2
    while bit < size:
        mine = jnp.concatenate([mine, exchange(mine, "dp", size, bit)], axis=0)
        bit *= 2
    return [mine], [exchange(mine, "dp", size, 1)]


class Scatter:
    def __init__(self, size, lefts, rights, name):
        self.size, self.name = size, name
        self.lefts, self.rights = lefts, rights
        self.model = lefts[0].shape[1]
        self.width = sum(r.shape[1] for r in rights)

    def halves(self, side):
        tokens = self.lefts[0].shape[0]
        return {i: block((tokens, self.model // 2), 0, side) for i in range(len(self.lefts))}

    def sibling(self, run):
        shape = (self.model // 2, self.width)
        return run(
            partial(grads_out_kernel, len(self.lefts)), [like(shape, bf16)],
            *self.lefts, *self.rights, specs=self.halves(1),
            out_specs=[pl.BlockSpec(memory_space=pl.ANY)],
            scratch=[pltpu.VMEM(shape, bf16), pltpu.SemaphoreType.DMA((2,))],
            name="grads_out_" + self.name,
        )[0]

    def swap(self, out):
        return exchange(out, "dp", self.size, 1)

    def own(self, run, got, room=0):
        q, w = self.model // 16, self.width
        sends = [like(((2 + room) * q, w), bf16)] * 2
        anywhere = pl.BlockSpec(memory_space=pl.ANY)
        specs = self.halves(0)
        specs[2 * len(self.lefts)] = anywhere
        return run(
            partial(grads_own_kernel, len(self.lefts), room),
            [like((2 * q, w), f32), like((q, w), f32), like((q, w), f32)] + sends,
            *self.lefts, *self.rights, got, specs=specs, out_specs=[anywhere] * 5,
            scratch=[
                pltpu.VMEM((8 * q, w), bf16), pltpu.VMEM((8 * q, w), f32), pltpu.VMEM((4 * q, w), bf16),
                pltpu.SemaphoreType.DMA((9,)),
            ],
            name="grads_own_" + self.name,
        )

    def join(self, cut):
        own, x_top, y_bot, from_x, from_y = cut
        q = x_top.shape[0]
        from_x, from_y = from_x[-2 * q :], from_y[-2 * q :]
        total = jnp.concatenate(
            [own, x_top, from_x[q:].astype(f32), from_y[q:].astype(f32), y_bot,
             from_y[:q].astype(f32), from_x[:q].astype(f32)],
            axis=0,
        )
        bit = self.size // 2
        while bit > 1:
            half = total.shape[0] // 2
            total = total[:half] + exchange(total[half:].astype(bf16), "dp", self.size, bit).astype(f32)
            bit //= 2
        return total


def relay(run, cuts, got, base, nexts, name):
    q = cuts[0][1].shape[0]
    width = sum(cut[1].shape[1] for cut in cuts)
    ins, specs, options = [], {}, {}
    for cut in cuts:
        ins += [cut[1], cut[2]]
        for v in got:
            specs[len(ins)] = block((q, v.shape[1]), base, 0)
            ins.append(v)
    if len(nexts) == 1:
        options = dict(
            alias={len(ins): 0, len(ins) + 1: 1}, out_specs=[block((q, width), 0, 0)] * 2
        )
        specs[len(ins)] = specs[len(ins) + 1] = pl.BlockSpec(memory_space=pl.ANY)
    for cut in nexts:
        ins += [cut[3], cut[4]]
    return run(
        partial(relay_kernel, len(cuts), 0 if len(nexts) == 1 else len(nexts)),
        [like((3 * q if nexts else q, width), bf16)] * 2, *ins, specs=specs, name=name, **options,
    )


def to_owner(part):
    return exchange(part, "tensor", 4, 1)


def pass_on(part, got):
    return exchange((part + got.astype(f32)).astype(bf16), "tensor", 4, 2)


class Order:
    def __init__(self):
        self.last = None

    def after(self, *values):
        if self.last is not None:
            values, _ = lax.optimization_barrier((values, self.last))
        return values if len(values) > 1 else values[0]

    def wait(self, *values):
        values = self.after(*values)
        self.last = jax.tree.leaves(values)[0]
        return values

    def run(self, kernel, outs, *args, **options):
        results = call(kernel, outs, *self.after(*args), **options)
        self.last = results[0]
        return results


def spread(piece):
    return exchange(piece, "tensor", 4, 2), exchange(piece, "tensor", 4, 1)


def neighbour(v):
    return exchange(v, "tensor", 4, 1)


def sum_over(v, axis, size, first=1, until=None):
    bit = first
    while bit < (until or size):
        v = v + exchange(v, axis, size, bit)
        bit *= 2
    return v


def sum_low(v, axis, size, first=1, until=None):
    bit = first
    while bit < (until or size):
        low = v.astype(bf16)
        v = low.astype(f32) + exchange(low, axis, size, bit).astype(f32)
        bit *= 2
    return v


def body(
    tokens, segments, first_gain, x_weight, y_weight, conv_weight, conv_bias, rate_weight,
    input_weight, rate_bias, input_bias, decay_logit, out_weight, second_gain, gate_weight,
    up_weight, down_weight, cotangent, dp_size,
):
    count, model = tokens.shape
    heads, _, units = rate_weight.shape
    chan = heads * units
    pairs = heads // 2
    taps = conv_weight.shape[0]
    hidden_units = gate_weight.shape[1]
    width = hidden_units // chunk_count
    me = lax.axis_index("dp")
    z = lax.axis_index("tensor").astype(jnp.int32)
    ids = jnp.stack([z, me.astype(jnp.int32)])
    part = model // dp_size
    q = model // 16
    rows = count // 4
    size = dp_size
    order = Order()
    after, wait, run = order.after, order.wait, order.run
    anywhere = pl.BlockSpec(memory_space=pl.ANY)
    lane = pl.BlockSpec((count, 128), lambda p: (0, p))
    line = pl.BlockSpec((1, 128), lambda p: (0, p))
    sums_spec = pl.BlockSpec((8, 128), lambda p: (0, p))
    block_spec = pl.BlockSpec((1, 8 * units, 4 * units), lambda p: (p, 0, 0))
    mask_spec = pl.BlockSpec((taps - 1, count, 128), lambda p: (0, 0, 0))
    pair_grid = dict(
        grid=(pairs,), cost_estimate=hint,
        compiler_params=pltpu.CompilerParams(vmem_limit_bytes=60 * MIB),
    )
    split_shapes = [like((rows, model), t) for t in (f32, bf16, f32, bf16)]
    split_specs = [pl.BlockSpec((rows, model), lambda p: (0, 0))] * 4
    total_scratch = [pltpu.VMEM((count, model), f32)]

    out_block = pl.BlockSpec((model // 4, 128), lambda p: (0, p))

    def weight_block(at):
        return pl.BlockSpec((model // 2, 128), lambda p: (0, at * pairs + p))

    def sibling(v):
        return exchange(v, "dp", size, 1)

    def halves(by_x, by_y):
        half = by_x.shape[0] // 2
        lower, upper = move(size, by_y[half:], by_x[:half])
        return upper, lower

    def pieces_of(shard, *got):
        if size == 8:
            return [shard, *got[: len(got) // 2]], list(got[len(got) // 2 :])
        return gather_all(shard, size)

    def assemble(pieces, dtype, name, specs=None):
        return run(
            assemble_kernel, [like((count, model), dtype)], ids, *pieces, scalars=1, specs=specs,
            name=name,
        )[0]

    x_flat, y_flat = x_weight.reshape(part, chan), y_weight.reshape(part, chan)
    out_shard = out_weight.reshape(chan, part).T
    half = part // 2
    xy_t = jnp.concatenate([x_flat[:half], y_flat[:half]], axis=1)
    xy_b = jnp.concatenate([x_flat[half:], y_flat[half:]], axis=1)
    xt, yt = move(size, xy_t, xy_t)
    xb, yb = move(size, xy_b, xy_b)

    def ffn_shard(c):
        cols = block((part, width), 0, c)
        return run(
            shard_kernel, [like((part, 3 * width), bf16)], gate_weight, up_weight, down_weight.T,
            specs={0: cols, 1: cols, 2: cols}, name="shard",
        )[0]

    x_rel, nf, gain_one, gain_two = run(
        partial(norm_first_kernel, size),
        [like((count, model), bf16)] * 2 + [like((1, model), f32)] * 2,
        ids, tokens, first_gain.reshape(1, model), second_gain.reshape(1, model), scalars=1,
        name="norm_first",
    )
    f0, f1 = ffn_shard(0), ffn_shard(1)
    xt, xb, yt, yb, out_shard = wait(xt, xb, yt, yb, out_shard)

    top, bot = along(size, 4, xt), along(size, 2, yb)
    st, sb, sxt = sibling(xy_t), sibling(xy_b), sibling(xt)
    (cot_rel,) = run(
        partial(to_rel_kernel, size), [like((count, model), bf16)], ids, cotangent, scalars=1,
        name="cotangent",
    )
    segs = after(segments)
    masks = jnp.stack(
        [
            jnp.concatenate([jnp.full((lag,), -1, jnp.int32), segs[:-lag]]) == segs
            for lag in range(1, taps)
        ]
    ).astype(f32)
    masks = jnp.broadcast_to(masks[:, :, None], (taps - 1, count, 128))
    taps_flat = conv_weight.reshape(taps, chan)
    bias_flat = conv_bias.reshape(1, chan)
    rate_flat, input_flat = rate_bias.reshape(1, chan), input_bias.reshape(1, chan)
    decay_flat = decay_logit.reshape(1, chan)
    masks, taps_flat, bias_flat, rate_flat, input_flat, decay_flat, top, bot, st, sb, sxt = wait(
        masks, taps_flat, bias_flat, rate_flat, input_flat, decay_flat, top, bot, st, sb, sxt
    )
    sxb, syt, syb = sibling(after(xb)), sibling(after(yt)), sibling(after(yb))
    s_top, s_bot = sibling(top), sibling(bot)
    sxb, syt, syb, s_top, s_bot = wait(sxb, syt, syb, s_top, s_bot)
    out_x, out_y = move(size, out_shard, out_shard)
    if size == 8:
        own_w = [xy_t, xy_b, xt, xb, yt, yb, top, bot]
        sib_w = [st, sb, sxt, sxb, syt, syb, s_top, s_bot]
    else:
        own_w, sib_w = gather_all(jnp.concatenate([xy_t, xy_b], axis=0), size)
    all_w = own_w + sib_w
    x_branch, y_branch, conv_low = run(
        branches_kernel,
        [like((count, chan), f32), like((count, chan), f32), like((count, chan), bf16)],
        nf, taps_flat, bias_flat, masks, *all_w,
        specs={4 + i: anywhere for i in range(len(all_w))},
        scratch=[
            pltpu.VMEM((count, 2 * chan), f32),
            pltpu.VMEM((model, 2 * chan), bf16),
            pltpu.SemaphoreType.DMA((len(all_w),)),
        ],
        name="branches",
    )
    conv_low, out_x, out_y = wait(conv_low, out_x, out_y)
    conv2, conv1 = spread(conv_low)
    out_far = along(size, 2, out_y)
    f0_x, f0_y = move(size, *after(f0, f0))
    xy0, xy1 = run(
        partial(join_kernel, len(own_w)), [like((model // 2, 2 * chan), bf16)] * 2, *all_w,
        specs={i: anywhere for i in range(len(all_w))},
        scratch=[pltpu.SemaphoreType.DMA((len(all_w),))], name="join_xy",
    )
    (blocks,) = run(
        blocks_kernel, [like((pairs, 8 * units, 4 * units), bf16)], ids,
        rate_weight.transpose(0, 2, 1), input_weight.transpose(0, 2, 1),
        scalars=1, name="gate_blocks",
    )
    conv2, conv1, out_far = wait(conv2, conv1, out_far)
    conv3 = neighbour(conv2)
    if size == 8:
        pieces = [out_shard, out_x, out_y, out_far]
        outs = run(
            partial(join_kernel, 2), [like((model // 4, chan), bf16)] * 2, *pieces,
            specs={i: anywhere for i in range(4)}, scratch=[pltpu.SemaphoreType.DMA((4,))],
            name="join_out",
        )
    else:
        whole_out = gather_all(out_shard, size)[0][0]
        outs = [whole_out[: model // 4], whole_out[model // 4 :]]
    outs = [*outs, *[sibling(v) for v in outs]]
    conv3, f0_x, f0_y, outs = wait(conv3, f0_x, f0_y, outs)
    conv = [conv_low, conv1, conv2, conv3]
    f0_s, f1_s = [sibling(v) for v in after(f0, f1)]
    f1_x, f1_y = move(size, f1, after(f1))
    f0_sx = sibling(f0_x)
    rate, entry, hidden, mixed, *parts = pl.pallas_call(
        forward_scan_kernel,
        in_specs=[smem] + [lane] * 4 + [block_spec] + [line] * 3 + [lane, mask_spec]
        + [anywhere] * 4,
        out_specs=[lane] * 4 + split_specs,
        out_shape=[like((count, chan), t) for t in (f32, f32, f32, bf16)] + split_shapes,
        scratch_shapes=total_scratch
        + [
            pltpu.VMEM((model, chan), bf16),
            pltpu.VMEM((count, chan), bf16),
            pltpu.SemaphoreType.DMA((4,)),
        ],
        name="forward_scan",
        **pair_grid,
    )(ids, *conv, blocks, rate_flat, input_flat, decay_flat, y_branch, masks, *outs)
    order.last = rate
    parts, f0_s, f1_s, f0_sx = wait(tuple(parts), f0_s, f1_s, f0_sx)
    got3 = to_owner(parts[3])
    f0_sy = sibling(after(f0_y))
    got3, f0_sy = wait(got3, f0_sy)
    got2, got1 = pass_on(parts[2], got3), to_owner(after(parts[1]))
    got2, got1, f1_x, f1_y = wait(got2, got1, f1_x, f1_y)
    f0_far, f1_far = along(size, 2, after(f0_y)), along(size, 4, f1_x)
    f1_sx, f1_sy = sibling(f1_x), sibling(f1_y)
    residual, second_rows = run(
        norm_second_kernel, [like((rows, model), f32), like((rows, model), bf16)],
        ids, x_rel, gain_two, parts[0], got1, got2, scalars=1, name="norm_second",
    )
    second_rows, f1_sx, f1_sy = wait(second_rows, f1_sx, f1_sy)
    sec2, sec1 = spread(second_rows)
    f2 = ffn_shard(2)
    sec2, sec1 = wait(sec2, sec1)
    sec3 = neighbour(sec2)
    sec3, f0_far, f1_far = wait(sec3, f0_far, f1_far)
    f2_x, f2_y = move(size, *after(f2, f2))
    f0_sf, f1_sf = sibling(f0_far), sibling(f1_far)
    f0_sf, f1_sf = wait(f0_sf, f1_sf)
    f2_s = sibling(after(f2))

    def ffn(left, groups, sums, first, last, name):
        outs = [like((count, 2 * width), bf16), like((count, width), bf16)] * len(groups)
        out_specs = [full(v) for v in outs]
        if first:
            outs.append(like((count, model), bf16))
            out_specs.append(anywhere)
        if last:
            outs += split_shapes
            out_specs += [full(v) for v in split_shapes]
        else:
            outs.append(like((count, model), f32))
            out_specs.append(anywhere)
        weights = sum([own + sib for own, sib in groups], [])
        scratch = [
            pltpu.VMEM((count, model), bf16),
            pltpu.VMEM((count, model), bf16),
            pltpu.VMEM((count, 2 * width), f32),
            pltpu.VMEM((count, width), f32),
            pltpu.VMEM((len(groups), model, 3 * width), bf16),
            pltpu.VMEM((count, model), f32),
            pltpu.SemaphoreType.DMA((len(weights) + 3,)),
            pltpu.SemaphoreType.DMA((5,)),
        ]
        ins = [ids, *left, *sums, cot_rel, *weights]
        at = 1 + len(left) * first
        return run(
            partial(ffn_kernel, len(groups), first, last), outs, *ins, scalars=1, scratch=scratch,
            specs={i: anywhere for i in range(at, len(ins))}, out_specs=out_specs, name=name,
        )

    groups = [
        pieces_of(f0, f0_x, f0_y, f0_far, f0_s, f0_sx, f0_sy, f0_sf),
        pieces_of(f1, f1_x, f1_y, f1_far, f1_s, f1_sx, f1_sy, f1_sf),
    ]
    a, mid0, c, mid1, second, *sums = ffn(
        [second_rows, sec1, sec2, sec3], groups, [], True, False, "ffn_01"
    )
    b, d = mid0, mid1
    s0 = Scatter(size, [second, cot_rel], [a, b], "ffn_0")
    s1 = Scatter(size, [second, cot_rel], [c, d], "ffn_1")
    s0_out = s0.sibling(run)
    s0_out, f2_s, f2_x, f2_y = wait(s0_out, f2_s, f2_x, f2_y)
    f2_top, f2_bot = halves(f2_x, f2_y)
    f2_sx, f2_sy = sibling(f2_x), sibling(f2_y)
    s0_swap = s0.swap(s0_out)
    s1_out = s1.sibling(run)
    f2_sx, f2_sy, s0_swap = wait(f2_sx, f2_sy, s0_swap)
    s0_cut = s0.own(run, s0_swap)
    f2_top, f2_bot, s0_send = wait(f2_top, f2_bot, tuple(s0_cut[3:]))
    f2_st, f2_sb = sibling(f2_top), sibling(f2_bot)
    f2_st, f2_sb = wait(f2_st, f2_sb)
    s0_got = move(size, *after(*s0_send))
    s1_swap = s1.swap(after(s1_out))
    groups.append(pieces_of(f2, f2_x, f2_y, f2_top, f2_bot, f2_s, f2_sx, f2_sy, f2_st, f2_sb))
    a, b, *grad_parts = ffn([second], groups[2:], sums, False, True, "ffn_2")
    mid2 = b
    s2 = Scatter(size, [second, cot_rel], [a, b], "ffn_2")
    grad_parts, s1_swap = wait(tuple(grad_parts), s1_swap)

    got3, got1 = to_owner(grad_parts[3]), to_owner(grad_parts[1])
    s1_cut = s1.own(run, s1_swap)
    s2_out = s2.sibling(run)
    got3, s0_got, s2_out, s1_send = wait(got3, s0_got, s2_out, tuple(s1_cut[3:]))
    got2 = pass_on(grad_parts[2], got3)
    s1_got = move(size, *s1_send)
    s2_swap = s2.swap(s2_out)
    lists = [own + sib for own, sib in groups]
    ins = [ids, mid0, mid1, mid2, *sum(lists, [])]
    out_parts = run(
        partial(ffn_out_kernel, [len(v) for v in lists]),
        [like((rows, model), f32)] * 2 + [like((2 * rows, model), bf16)], *ins, scalars=1,
        specs={i: anywhere for i in range(4, len(ins))},
        scratch=[
            pltpu.VMEM((chunk_count, model, width), bf16), pltpu.VMEM((count, model), f32),
            pltpu.SemaphoreType.DMA((len(ins),)),
        ],
        name="ffn_out",
    )
    got2, got1, s2_swap = wait(got2, got1, s2_swap)
    grad_res, rec_rows, second_gain = run(
        partial(second_back_kernel, size),
        [like((rows, model), f32), like((rows, model), bf16), like((1, model), f32)],
        ids, cot_rel, gain_two, residual, grad_parts[0], got1, got2, scalars=1, micros=6, name="second_back",
    )
    rec2, rec1 = spread(rec_rows)
    s2_cut = s2.own(run, s2_swap, 1)
    sends = relay(run, [s0_cut], s0_got, 0, [s2_cut], "relay_0")
    rec2, rec1, s1_got, sends = wait(rec2, rec1, s1_got, tuple(sends))
    rec3 = neighbour(rec2)
    slot = move(size, *sends)
    rec3 = wait(rec3)
    out_got = neighbour(after(out_parts[2]))

    whole = pl.BlockSpec((count, model), lambda p: (0, 0))
    piece = pl.BlockSpec((rows, model), lambda p: (0, 0))
    gate_spec = pl.BlockSpec((1, 4, units, 2 * units), lambda p: (p, 0, 0, 0))
    gate_half = like((pairs, 4, units, 2 * units), bf16)
    grad_rec, grad_y, direct, h1, h2, h3, gate_mine, gate_theirs, scan_sums = pl.pallas_call(
        backward_scan_kernel,
        in_specs=[smem] + [piece] * 4 + [out_block] * 4 + [lane] * 4
        + [block_spec, line, lane, mask_spec] + [lane] * 3,
        out_specs=[whole, lane, lane, lane, lane, lane, gate_spec, gate_spec, sums_spec],
        out_shape=[like((count, model), bf16)]
        + [like((count, chan), t) for t in (bf16, f32, bf16, f32, bf16)]
        + [gate_half, gate_half, like((8, chan), f32)],
        name="backward_scan",
        **pair_grid,
    )(
        *after(ids, rec_rows, rec1, rec2, rec3, *outs, *conv, blocks, decay_flat, y_branch, masks),
        rate, entry, hidden,
    )
    order.last = grad_rec
    out_got, h1, h2, h3 = wait(out_got, h1, h2, h3)
    got3 = to_owner(h3)
    gate_got = sibling(gate_theirs)
    syo = Scatter(size, [nf, grad_rec], [grad_y, mixed], "yo")
    syo_out = syo.sibling(run)
    s1_send = relay(run, [s1_cut], s1_got, 0, [], "relay_1")
    got3, syo_out, gate_got, s1_send = wait(got3, syo_out, gate_got, tuple(s1_send))
    got2, got1 = pass_on(h2, got3), to_owner(after(h1))
    (gate_sum,) = run(add_kernel, [gate_half], gate_mine, gate_got, name="gate_add")
    (out_low,) = run(
        add_kernel, [like((rows, model), bf16)], out_parts[1], out_got,
        specs={1: block((rows, model), 0, 0)}, name="out_add",
    )
    got2, got1, slot, out_low = wait(got2, got1, slot, out_low)
    out_got2 = exchange(out_low, "tensor", 4, 2)
    s1_last = move(size, *after(*s1_send))
    syo_swap = syo.swap(after(syo_out))
    gate_got = along(size, 2, after(gate_sum))
    whole_row = pl.BlockSpec((1, model), lambda p: (0, 0))
    grad_x, conv_sums, first_gain, *first_parts = pl.pallas_call(
        partial(conv_back_kernel, size),
        in_specs=[smem] + [lane] * 4 + [pl.BlockSpec((taps, 128), lambda p: (0, p)), mask_spec, lane]
        + [whole] + [anywhere] * 2,
        out_specs=[lane, sums_spec, whole_row] + split_specs,
        out_shape=[like((count, chan), bf16), like((8, chan), f32), like((1, model), f32)]
        + split_shapes,
        scratch_shapes=total_scratch
        + [
            pltpu.VMEM((model, 2 * chan), bf16),
            pltpu.VMEM((count, 2 * chan), bf16),
            pltpu.SemaphoreType.DMA((2,)),
        ],
        name="conv_back",
        **pair_grid,
    )(*after(ids, direct, got1, got2, x_branch, taps_flat, masks, grad_y, x_rel, xy0, xy1))
    order.last = grad_x
    first_parts, syo_swap, out_got2 = wait(tuple(first_parts), syo_swap, out_got2)
    got3 = to_owner(first_parts[3])
    sx = Scatter(size, [nf], [grad_x], "x")
    sx_out = sx.sibling(run)
    syo_cut = syo.own(run, syo_swap)
    s2_send = relay(run, [s2_cut], slot, 1, [], "relay_2")
    got3, sx_out, yo_send, s1_last, gate_got, s2_send = wait(
        got3, sx_out, tuple(syo_cut[3:]), s1_last, gate_got, tuple(s2_send)
    )
    got2, got1 = pass_on(first_parts[2], got3), to_owner(after(first_parts[1]))
    sx_swap = sx.swap(sx_out)
    yo_got = move(size, *yo_send)
    got2, got1, sx_swap, yo_got = wait(got2, got1, sx_swap, yo_got)
    (tokens_rows,) = run(
        partial(first_back_kernel, size), [like((rows, model), bf16)],
        ids, x_rel, gain_one, grad_res, first_parts[0], got1, got2, scalars=1, name="first_back",
    )
    gains = jnp.concatenate([first_gain, second_gain], axis=0)
    tok2, tok1 = spread(tokens_rows)
    gains = sum_over(after(gains), "tensor", 4, 1, 2)
    s2_last = move(size, *after(*s2_send))
    sx_cut = sx.own(run, sx_swap)
    specs = {k: block((q, 2 * chan), 0, 0) for k in (2, 3)}
    mixed_sends = run(
        relay_mixed_kernel, [like((4 * q, chan), bf16)] * 2, syo_cut[1], syo_cut[2], *yo_got,
        *sx_cut[3:], specs=specs, name="relay_3",
    )
    (block_rows,) = run(
        partial(block_out_kernel, size), [like((rows, model), bf16)],
        ids, residual, out_parts[0], out_got, out_got2, scalars=1,
        specs={3: block((rows, model), 1, 0)}, name="block_out",
    )
    (gate_sum,) = run(add_kernel, [gate_half], gate_sum, gate_got, name="gate_add")
    tok2, tok1, s2_last, gains, mixed_sends = wait(tok2, tok1, s2_last, gains, tuple(mixed_sends))
    tok3 = neighbour(tok2)
    slot3 = move(size, *mixed_sends)
    block2 = exchange(after(block_rows), "tensor", 4, 2)
    gains = sum_over(gains, "tensor", 4, 2)
    if size == 8:
        ins, specs = [], {}
        for cut, (got, base), last in (
            (s0_cut, (s0_got, 0), slot), (s1_cut, (s1_got, 0), s1_last), (s2_cut, (slot, 1), s2_last)
        ):
            ins.append(cut[0])
            for v, at in ((got[0], base + 1), (got[1], base + 1), (last[0], 0), (last[1], 0)):
                specs[len(ins)] = block((q, v.shape[1]), at, 0)
                ins.append(v)
        gate_share, up_share, down_share = run(
            join_ffn_kernel,
            [like((part, hidden_units), f32)] * 3,
            *ins, specs=specs, name="join_ffn",
        )
    else:
        shares = [s0.join(s0_cut), s1.join(s1_cut), s2.join(s2_cut)]
        gate_share, up_share, down_share = [
            jnp.concatenate([v[:, k * width : (k + 1) * width] for v in shares], axis=1)
            for k in range(3)
        ]
    tok3, gains, slot3, block2 = wait(tok3, gains, slot3, block2)
    small = jnp.concatenate([scan_sums, conv_sums, gains.reshape(8, chan)], axis=0)
    small = sum_over(small, "dp", size, 1, 2)
    block13 = neighbour(jnp.concatenate([block_rows, block2], axis=0))
    gate_got = along(size, 4, after(gate_sum))
    x_last = move(size, *relay(run, [sx_cut], slot3, 2, [], "relay_4"))
    yo_ins = [syo_cut[0], *yo_got, *slot3, *slot3]
    if size == 8:
        specs = {1: block((q, 2 * chan), 1, 0), 2: block((q, 2 * chan), 1, 0)}
        for k, at in enumerate((0, 0, 1, 1)):
            specs[3 + k] = block((q, chan), at, 0)
        y_share, out_share = run(
            join_yo_kernel, [like((chan, part), f32)] * 2, *yo_ins, specs=specs, name="join_yo"
        )
    tokens_grad = assemble([tokens_rows, tok1, tok2, tok3], f32, "tokens_grad_all")
    (gate_sum,) = run(
        add_kernel, [like(gate_half.shape, f32)], gate_sum, wait(gate_got), name="gate_add"
    )
    x_last, block13, small, gate_sum = wait(x_last, block13, small, gate_sum)
    block_ins = [block_rows, block13, block2, block13]
    block_specs = {2: block((rows, model), 0, 0), 4: block((rows, model), 1, 0)}
    if size == 8:
        by_x, by_y, across = [exchange(small, "dp", size, bit) for bit in (2, 4, 6)]
        gate_got = sibling(gate_sum)
        specs = {k: block((q, chan), 3 if k < 3 else 0, 0) for k in range(1, 5)}
        (x_share,) = run(
            join_x_kernel, [like((chan, part), f32)], sx_cut[0], *slot3, *x_last, specs=specs,
            name="join_x",
        )
        block_out = assemble(block_ins, bf16, "block_out_all", block_specs)
        gate_got = wait(gate_got)
        rate_grad, input_grad = run(
            gate_join_kernel, [like((heads, units, 4 * units), f32)] * 2, ids, gate_sum, gate_got,
            scalars=1, name="gate_join",
        )
        rate_grad, input_grad = rate_grad.transpose(0, 2, 1), input_grad.transpose(0, 2, 1)
        by_x, by_y, across = wait(by_x, by_y, across)
        head_like = like((heads, units), f32)
        taps_grad, bias_grad, rate_b_grad, input_b_grad, decay_grad, one_grad, two_grad = run(
            partial(small_kernel, units),
            [like((heads, taps, units), f32)] + [head_like] * 4 + [like((model,), f32)] * 2,
            small, by_x, by_y, across, name="small",
        )
        taps_grad = taps_grad.transpose(1, 0, 2)
    else:
        block_out = assemble(block_ins, bf16, "block_out_all", block_specs)
        small = sum_over(small, "dp", size, 2)
        taps_grad = small[8 : 8 + taps].reshape(taps, heads, units)
        bias_grad, rate_b_grad, input_b_grad, decay_grad = [
            small[k].reshape(heads, units) for k in (8 + taps, 1, 2, 0)
        ]
        one_grad, two_grad = small[16:20].reshape(model), small[20:].reshape(model)
        yo_share, x_share = syo.join(syo_cut), sx.join(sx_cut)
        x_share, y_share, out_share = x_share.T, yo_share[:, :chan].T, yo_share[:, chan:].T
        mine = sum_low(gate_mine + sibling(gate_theirs), "dp", size, 2)
        other, core = sibling(mine), me % 2
        gate_sum = jnp.stack(
            [jnp.where(core == 0, mine, other), jnp.where(core == 0, other, mine)], axis=1
        ).reshape(heads, 4, units, 2 * units)
        gate_sum = jnp.concatenate(
            [lax.dynamic_index_in_dim(gate_sum, z ^ k, 1, False) for k in range(4)], axis=1
        )
        rate_grad, input_grad = gate_sum[:, :, :units], gate_sum[:, :, units:]
    x_share = x_share.reshape(heads, units, part).transpose(2, 0, 1)
    y_share = y_share.reshape(heads, units, part).transpose(2, 0, 1)
    return (
        block_out,
        tokens_grad,
        one_grad,
        x_share,
        y_share,
        taps_grad,
        bias_grad,
        rate_grad,
        input_grad,
        rate_b_grad,
        input_b_grad,
        decay_grad,
        out_share.reshape(heads, units, part),
        two_grad,
        gate_share,
        up_share,
        down_share.T,
    )


def solution(mesh):
    return jax.shard_map(
        partial(body, dp_size=mesh.shape["dp"]),
        mesh=mesh,
        in_specs=(
            P("dp", None),
            P("dp"),
            P(),
            P("dp", None, "tensor"),
            P("dp", None, "tensor"),
            P(None, None, "tensor"),
            P(None, "tensor"),
            P(None, None, "tensor"),
            P(None, None, "tensor"),
            P(None, "tensor"),
            P(None, "tensor"),
            P(None, "tensor"),
            P(None, "tensor", "dp"),
            P(),
            P("dp", "tensor"),
            P("dp", "tensor"),
            P("tensor", "dp"),
            P("dp", None),
        ),
        out_specs=(
            P("dp", None),
            P("dp", None),
            P(),
            P("dp", None, "tensor"),
            P("dp", None, "tensor"),
            P(None, None, "tensor"),
            P(None, "tensor"),
            P(None, None, "tensor"),
            P(None, None, "tensor"),
            P(None, "tensor"),
            P(None, "tensor"),
            P(None, "tensor"),
            P(None, "tensor", "dp"),
            P(),
            P("dp", "tensor"),
            P("dp", "tensor"),
            P("tensor", "dp"),
        ),
        check_vma=False,
    )
```

```python
from functools import partial

import jax
import jax.numpy as jnp
from jax import lax
from jax.experimental import pallas as pl
from jax.experimental.pallas import tpu as pltpu
from jax.sharding import PartitionSpec as P

eps = 1e-06
f32 = jnp.float32
bf16 = jnp.bfloat16
vmem = pl.BlockSpec(memory_space=pltpu.VMEM)
smem = pl.BlockSpec(memory_space=pltpu.SMEM)
MIB = 1024 * 1024
chunk_count = 3


def nn(a, b):
    return lax.dot_general(a, b, (((1,), (0,)), ((), ())), preferred_element_type=f32)


def nt(a, b):
    return lax.dot_general(a, b, (((1,), (1,)), ((), ())), preferred_element_type=f32)


def tn(a, b):
    return lax.dot_general(a, b, (((0,), (0,)), ((), ())), preferred_element_type=f32)


def full(v):
    zeros = (0,) * len(v.shape)
    return pl.BlockSpec(v.shape, lambda i: zeros, pipeline_mode=pl.Buffered(1))


def block(shape, *index):
    return pl.BlockSpec(shape, lambda i: index)


def hint_of(micros):
    return pl.CostEstimate(
        flops=1, bytes_accessed=max(1, int(micros * 3.0e6)), transcendentals=0
    )


hint = hint_of(0)


def call(kernel, outs, *args, scalars=0, mem=60, specs=None, out_specs=None, alias=None, scratch=(), micros=0, name=None):
    specs = specs or {}
    return pl.pallas_call(
        kernel,
        grid=(1,),
        out_shape=outs,
        in_specs=[smem] * scalars
        + [specs.get(i) or full(a) for i, a in enumerate(args) if i >= scalars],
        out_specs=out_specs or [full(s) for s in outs],
        scratch_shapes=scratch,
        input_output_aliases=alias or {},
        compiler_params=pltpu.CompilerParams(vmem_limit_bytes=mem * MIB),
        cost_estimate=hint_of(micros),
        name=name,
    )(*args)


def like(shape, dtype):
    return jax.ShapeDtypeStruct(shape, dtype)


def gelu_pair(v):
    c = 0.7978845608028654
    sq = v * v
    t = jnp.tanh(c * v * (1.0 + 0.044715 * sq))
    half = 0.5 * (1.0 + t)
    slope = half + 0.5 * v * (1.0 - t * t) * c * (1.0 + 3.0 * 0.044715 * sq)
    return v * half, slope


def one_less_exp(x):
    series = x * (
        1.0
        - x * (1 / 2) * (1.0 - x * (1 / 3) * (1.0 - x * (1 / 4) * (1.0 - x * (1 / 5) * (
            1.0 - x * (1 / 6) * (1.0 - x * (1 / 7) * (1.0 - x * (1 / 8)))))))
    )
    return jnp.where(x < 0.5, series, 1.0 - jnp.exp(-x))


def softplus(v):
    return jnp.maximum(v, 0.0) + jnp.log1p(jnp.exp(-jnp.abs(v)))


def sigmoid(v):
    return 1.0 / (1.0 + jnp.exp(-v))


def row_ids(shape):
    return lax.broadcasted_iota(jnp.int32, shape, 0)


def down_rows(v, steps, fill=0.0):
    return jnp.where(row_ids(v.shape) >= steps, pltpu.roll(v, steps, 0), fill)


def up_rows(v, steps, fill=0.0):
    rows = v.shape[0]
    return jnp.where(row_ids(v.shape) < rows - steps, pltpu.roll(v, rows - steps, 0), fill)


def scan_rows(decay, drive, shift):
    steps = 1
    while steps < decay.shape[0]:
        drive = decay * shift(drive, steps) + drive
        if steps * 2 < decay.shape[0]:
            decay = decay * shift(decay, steps, 1.0)
        steps *= 2
    return drive


def norm_first_kernel(size, z_ref, x_ref, one_ref, two_ref, rel_ref, out_ref, one_out, two_out):
    me = z_ref[1]
    gain = to_rel(me, size, one_ref[...].reshape(1, -1))
    rel = to_rel(me, size, x_ref[...].astype(f32))
    rel_ref[...] = rel.astype(bf16)
    inv = lax.rsqrt(jnp.mean(rel * rel, axis=1, keepdims=True) + eps)
    out_ref[...] = (rel * inv * gain).astype(bf16)
    one_out[...] = gain
    two_out[...] = to_rel(me, size, two_ref[...].reshape(1, -1))


def to_rel_kernel(size, z_ref, x_ref, rel_ref):
    rel_ref[...] = to_rel(z_ref[1], size, x_ref[...].astype(f32)).astype(bf16)


def shard_kernel(gate_ref, up_ref, down_ref, out_ref):
    width = gate_ref.shape[1]
    out_ref[:, :width] = gate_ref[...]
    out_ref[:, width : 2 * width] = up_ref[...]
    out_ref[:, 2 * width :] = down_ref[...]


def blocks_kernel(z_ref, rate_ref, input_ref, out_ref):
    units = rate_ref.shape[1]
    zero = jnp.zeros((units, units), bf16)
    for p in range(out_ref.shape[0]):
        for a in range(2):
            parts = [ref[2 * p + a].T for ref in (rate_ref, input_ref)]
            rows = []
            for k in range(4):
                row = []
                for part in parts:
                    one = jnp.zeros_like(zero)
                    for owner in range(4):
                        one = jnp.where(
                            (z_ref[0] ^ k) == owner, part[owner * units : (owner + 1) * units], one
                        )
                    row += [zero, one] if a else [one, zero]
                at = slice((2 * k + a) * units, (2 * k + a + 1) * units)
                out_ref[p, at, :] = jnp.concatenate(row, axis=1)


def land(pieces, w_ref, sems, first=0):
    copies, at = [], 0
    for n, piece in enumerate(pieces):
        rows = piece.shape[0]
        copy = pltpu.make_async_copy(piece, w_ref.at[pl.ds(at, rows)], sems.at[first + n])
        copy.start()
        copies.append((at, copy))
        at += rows
    return copies


def await_rows(copies, until):
    while copies and copies[0][0] < until:
        copies.pop(0)[1].wait()


def join_kernel(count, *refs):
    pieces, (first, second, sems) = refs[:-3], refs[-3:]
    copies = land(pieces[:count], first, sems) + land(pieces[count:], second, sems, count)
    for _, copy in copies:
        copy.wait()


def branch_kernel(nf_ref, taps_ref, bias_ref, mask_ref, *refs):
    pieces, (x_ref, conv_ref, w_ref, sems) = refs[:-4], refs[-4:]
    step = w_ref.shape[0] // 4
    copies = land(pieces, w_ref, sems)
    for i in range(4):
        rows = slice(i * step, (i + 1) * step)
        await_rows(copies, (i + 1) * step)
        part = nn(nf_ref[:, rows], w_ref[rows, :])
        x_ref[...] = part if i == 0 else x_ref[...] + part
    for c in range(0, x_ref.shape[1], 128):
        cols = slice(c, c + 128)
        x = x_ref[:, cols]
        total = x * taps_ref[0:1, cols] + bias_ref[:, cols]
        for lag in range(1, taps_ref.shape[0]):
            total = total + down_rows(x, lag) * mask_ref[lag - 1] * taps_ref[lag : lag + 1, cols]
        conv_ref[:, cols] = total.astype(bf16)


def mix_kernel(z_ref, nf_ref, hidden_ref, *refs):
    pieces = refs[:-9]
    y_ref, mixed_ref, o0, o1, o2, o3, total_ref, w_ref, sems = refs[-9:]
    width, half = y_ref.shape[1], len(pieces)
    step = w_ref.shape[1] // 4
    gate = land([p.at[:, pl.ds(0, width)] for p in pieces], w_ref.at[0], sems)
    out = land([p.at[:, pl.ds(width, width)] for p in pieces], w_ref.at[1], sems, half)
    for i in range(4):
        rows = slice(i * step, (i + 1) * step)
        await_rows(gate, (i + 1) * step)
        part = nn(nf_ref[:, rows], w_ref[0, rows, :])
        y_ref[...] = part if i == 0 else y_ref[...] + part
    for c in range(0, width, 128):
        cols = slice(c, c + 128)
        mixed_ref[:, cols] = (hidden_ref[:, cols] * gelu_pair(y_ref[:, cols])[0]).astype(bf16)
    for i in range(4):
        rows = slice(i * step, (i + 1) * step)
        await_rows(out, (i + 1) * step)
        total_ref[:, rows] = nt(mixed_ref[...], w_ref[1, rows, :])
    split_rows(z_ref, total_ref, (o0, o1, o2, o3))


def gates_of(rate, decay_logit, start):
    soft = softplus(-decay_logit)
    minus_log = 8.0 * rate * soft
    lost = one_less_exp(2.0 * minus_log)
    mult = jnp.where(start, 1.0, jnp.sqrt(lost))
    carried = jnp.where(start, 0.0, jnp.exp(-minus_log))
    return soft, mult, carried


def forward_scan_kernel(
    c0, c1, c2, c3, block_ref, rb_ref, ib_ref, dl_ref, mask_ref, rate_ref, entry_ref, hidden_ref
):
    start = mask_ref[0] == 0.0
    pre = nn(jnp.concatenate([c0[...], c1[...], c2[...], c3[...]], axis=1), block_ref[0])
    rate = sigmoid(pre[:, :128] + rb_ref[...])
    entry = sigmoid(pre[:, 128:] + ib_ref[...])
    _, mult, carried = gates_of(rate, dl_ref[...], start)
    driven = c0[...].astype(f32) * entry * mult
    rate_ref[...] = rate
    entry_ref[...] = entry
    hidden_ref[...] = scan_rows(carried, driven, down_rows)


def fetch(step, pieces, w_ref, sems):
    copies = []
    for side, group in enumerate(pieces):
        at = 0
        for piece in group:
            rows = piece.shape[0]
            cols = pl.ds(side * piece.shape[1], piece.shape[1])
            copies.append(
                pltpu.make_async_copy(piece, w_ref.at[pl.ds(at, rows), cols], sems.at[len(copies)])
            )
            at += rows

    @pl.when(step == 0)
    def _():
        for copy in copies:
            copy.start()

    return copies


def product(landing, left_ref, w_ref, total_ref):
    for copy in landing:
        copy.wait()
    rows = w_ref.shape[0] // 4
    for i in range(4):
        at = slice(i * rows, (i + 1) * rows)
        total_ref[:, at] = nt(left_ref[...], w_ref[at, :])


def backward_scan_kernel(count, z_ref, p0, p1, p2, p3, *refs):
    weights, refs = refs[:count], refs[count:]
    c0, c1, c2, c3, block_ref, dl_ref, y_ref, mask_ref, rate_ref, entry_ref, hidden_ref = refs[:11]
    g_ref, gy_ref, direct_ref, h1_ref, h2_ref, h3_ref, mine_ref, theirs_ref, sums_ref = refs[11:]

    @pl.when(pl.program_id(0) == 0)
    def _():
        assemble_kernel(z_ref, p0, p1, p2, p3, g_ref)

    start = mask_ref[0] == 0.0
    grad_mixed = nn(g_ref[...], jnp.concatenate([w[...] for w in weights], axis=0))
    hidden, rate, entry = hidden_ref[...], rate_ref[...], entry_ref[...]
    conv = c0[...].astype(f32)
    gelu_y, slope_y = gelu_pair(y_ref[...])
    gy_ref[...] = (grad_mixed * hidden * slope_y).astype(bf16)
    decay_logit = dl_ref[...]
    soft, mult, carried = gates_of(rate, decay_logit, start)
    state = scan_rows(up_rows(carried, 1), grad_mixed * gelu_y, up_rows)
    kept = carried * carried
    grad_log = jnp.where(
        start, 0.0, state * (down_rows(hidden, 1) * carried - conv * entry * kept / mult)
    )
    rate_low = (grad_log * (-8.0 * soft) * rate * (1.0 - rate)).astype(bf16)
    entry_low = (state * conv * mult * entry * (1.0 - entry)).astype(bf16)
    both = jnp.concatenate([rate_low, entry_low], axis=1)
    sums_ref[...] = jnp.concatenate(
        [
            jnp.sum(grad_log * rate, axis=0, keepdims=True) * (8.0 * sigmoid(-decay_logit)),
            jnp.sum(rate_low.astype(f32), axis=0, keepdims=True),
            jnp.sum(entry_low.astype(f32), axis=0, keepdims=True),
            jnp.zeros((5, 128), f32),
        ],
        axis=0,
    )
    heads = nt(both, block_ref[0])
    direct_ref[...] = state * entry * mult + heads[:, :128]
    h1_ref[...] = heads[:, 128:256].astype(bf16)
    h2_ref[...] = heads[:, 256:384]
    h3_ref[...] = heads[:, 384:].astype(bf16)
    units = jnp.concatenate([c0[...], c1[...], c2[...], c3[...]], axis=1)
    grads = tn(units, both)
    first = jnp.concatenate([grads[:, 0:64], grads[:, 128:192]], axis=1)
    second = jnp.concatenate([grads[:, 64:128], grads[:, 192:256]], axis=1)
    for k in range(4):
        even, odd = first[k * 128 : k * 128 + 64], second[k * 128 + 64 : k * 128 + 128]
        own = z_ref[1] % 2 == 0
        mine_ref[0, k] = jnp.where(own, even, odd).astype(bf16)
        theirs_ref[0, k] = jnp.where(own, odd, even).astype(bf16)


def conv_back_kernel(
    size, count, z_ref, direct_ref, r1, r2, x_ref, taps_ref, mask_ref, gy_ref, rel_ref, *refs
):
    weights, refs = refs[: 2 * count], refs[2 * count :]
    gx_ref, sums_ref, gain_ref, o0, o1, o2, o3, total_ref, w_ref, left_ref, sems = refs
    step, width = pl.program_id(0), left_ref.shape[1] // 2
    sides = (weights[:count], [w.at[:, pl.ds(0, width)] for w in weights[count:]])
    landing = fetch(step, sides, w_ref, sems)
    chan = left_ref.shape[1] // 2
    total = direct_ref[...] + r1[...].astype(f32) + r2[...].astype(f32)
    x = x_ref[...]
    grad = total * taps_ref[0:1]
    sums = [jnp.sum(total * x, axis=0, keepdims=True)]
    for lag in range(1, taps_ref.shape[0]):
        kept = total * mask_ref[lag - 1]
        grad = grad + up_rows(kept, lag) * taps_ref[lag : lag + 1]
        sums.append(jnp.sum(kept * down_rows(x, lag), axis=0, keepdims=True))
    low = grad.astype(bf16)
    gx_ref[...] = low
    sums.append(jnp.sum(total, axis=0, keepdims=True))
    sums.append(jnp.zeros((8 - len(sums), x.shape[1]), f32))
    sums_ref[...] = jnp.concatenate(sums, axis=0)
    left_ref[:, pl.ds(pl.multiple_of(step * 128, 128), 128)] = low
    left_ref[:, pl.ds(pl.multiple_of(chan + step * 128, 128), 128)] = gy_ref[...]

    @pl.when(step == pl.num_programs(0) - 1)
    def _():
        product(landing, left_ref, w_ref, total_ref)
        split_rows(z_ref, total_ref, (o0, o1, o2, o3))
        rel = rel_ref[...].astype(f32)
        inv = lax.rsqrt(jnp.mean(rel * rel, axis=1, keepdims=True) + eps)
        gain = jnp.sum(total_ref[...] * (rel * inv), axis=0, keepdims=True)
        gain_ref[...] = to_abs(z_ref[1], size, gain)


def split_rows(z_ref, total_ref, outs):
    rows = outs[0].shape[0]
    for k, out in enumerate(outs):
        at = pl.multiple_of((z_ref[0] ^ k) * rows, rows)
        out[...] = total_ref[pl.ds(at, rows), :].astype(out.dtype)


def assemble_kernel(z_ref, *refs):
    pieces, out_ref = refs[:-1], refs[-1]
    rows = pieces[0].shape[0]
    for k, piece in enumerate(pieces):
        at = pl.multiple_of((z_ref[0] ^ k) * rows, rows)
        out_ref[pl.ds(at, rows), :] = piece[...].astype(out_ref.dtype)


def to_abs(me, size, v):
    part = v.shape[1] // size

    def picked(v, places):
        return jnp.concatenate([v[:, p * part : (p + 1) * part] for p in places], axis=1)

    v = picked(v, [(s % 2) * (size // 2) + s // 2 for s in range(size)])
    bit = 1
    while bit < size:
        v = jnp.where((me // bit) % 2 == 1, picked(v, [s ^ bit for s in range(size)]), v)
        bit *= 2
    return v


def to_rel(me, size, v):
    part = v.shape[1] // size

    def picked(v, places):
        return jnp.concatenate([v[:, p * part : (p + 1) * part] for p in places], axis=1)

    bit = 1
    while bit < size:
        v = jnp.where((me // bit) % 2 == 1, picked(v, [s ^ bit for s in range(size)]), v)
        bit *= 2
    return picked(v, [2 * j + c for c in range(2) for j in range(size // 2)])


def sum_pieces(pieces):
    total = pieces[0][...]
    for piece in pieces[1:]:
        total = total + piece[...].astype(f32)
    return total


def my_rows(z_ref, ref, rows):
    return ref[pl.ds(pl.multiple_of(z_ref[0] * rows, rows), rows), :].astype(f32)


def norm_second_kernel(z_ref, x_ref, gain_ref, o0, o1, o2, res_ref, low_ref):
    residual = my_rows(z_ref, x_ref, res_ref.shape[0]) + sum_pieces((o0, o1, o2))
    inv = lax.rsqrt(jnp.mean(residual * residual, axis=1, keepdims=True) + eps)
    res_ref[...] = residual
    low_ref[...] = (residual * inv * gain_ref[...]).astype(bf16)


def norm_back(x, gain, grad):
    inv = lax.rsqrt(jnp.mean(x * x, axis=1, keepdims=True) + eps)
    unit = x * inv
    scaled = grad * gain
    out = inv * (scaled - unit * jnp.mean(scaled * unit, axis=1, keepdims=True))
    return out, jnp.sum(grad * unit, axis=0, keepdims=True)


def second_back_kernel(size, z_ref, cot_ref, gain_ref, res_ref, o0, o1, o2, gr_ref, low_ref, gain_out):
    grad, gain_grad = norm_back(res_ref[...], gain_ref[...], sum_pieces((o0, o1, o2)))
    grad = grad + my_rows(z_ref, cot_ref, res_ref.shape[0])
    gr_ref[...] = grad
    low_ref[...] = grad.astype(bf16)
    gain_out[...] = to_abs(z_ref[1], size, gain_grad)


def first_back_kernel(size, z_ref, x_ref, gain_ref, gr_ref, o0, o1, o2, out_ref):
    x = my_rows(z_ref, x_ref, gr_ref.shape[0])
    grad, _ = norm_back(x, gain_ref[...], sum_pieces((o0, o1, o2)))
    out_ref[...] = to_abs(z_ref[1], size, gr_ref[...] + grad).astype(bf16)


def block_out_kernel(size, z_ref, res_ref, o0, o1, o2, out_ref):
    out_ref[...] = to_abs(z_ref[1], size, res_ref[...] + sum_pieces((o0, o1, o2))).astype(bf16)


def ffn_kernel(groups, first, last, *refs):
    refs = list(refs)

    def take(n):
        taken = refs[:n]
        del refs[:n]
        return taken

    (z_ref,) = take(1)
    if first:
        pieces = take(4)
    else:
        s_any, in_grad = take(2)
    (cot_any,) = take(1)
    s_ref, cot_ref, pre_ref, back_ref, w_ref, acc_grad, sems, out_sems = refs[-8:]
    del refs[-8:]
    n_outs = 2 * groups + (4 if last else 1 + first)
    outs = refs[-n_outs:]
    del refs[-n_outs:]
    per = len(refs) // groups
    rows, width = w_ref.shape[1] // 4, back_ref.shape[1]
    copies = []

    def load(src, dst):
        copy = pltpu.make_async_copy(src, dst, sems.at[len(copies)])
        copy.start()
        copies.append(copy)
        return copy

    held = []
    if not first:
        held.append(load(s_any, s_ref))
    held.append(load(cot_any, cot_ref))
    landing = []
    for g in range(groups):
        at, marks = 0, []
        for piece in refs[g * per : (g + 1) * per]:
            marks.append((at, load(piece, w_ref.at[g, pl.ds(at, piece.shape[0])])))
            at += piece.shape[0]
        landing.append(marks)
    if not first:
        sums = load(in_grad, acc_grad)
    if first:
        assemble_kernel(z_ref, *pieces, s_ref)
    for copy in held:
        copy.wait()
    stores = []

    def store(src, dst):
        copy = pltpu.make_async_copy(src, dst, out_sems.at[len(stores)])
        copy.start()
        stores.append(copy)

    if first:
        store(s_ref, outs[2 * groups])
    for g in range(groups):
        ggu_ref, mid_ref = outs[2 * g : 2 * g + 2]
        for i in range(4):
            at = slice(i * rows, (i + 1) * rows)
            await_rows(landing[g], (i + 1) * rows)
            pre = nn(s_ref[:, at], w_ref[g, at, : 2 * width])
            back = nn(cot_ref[:, at], w_ref[g, at, 2 * width :])
            if i == 0:
                pre_ref[...] = pre
                back_ref[...] = back
            else:
                pre_ref[...] += pre
                back_ref[...] += back
        for c in range(0, width, 128):
            gate, up = pre_ref[:, c : c + 128], pre_ref[:, width + c : width + c + 128]
            back = back_ref[:, c : c + 128]
            gelu_gate, slope = gelu_pair(gate)
            mid_ref[:, c : c + 128] = (gelu_gate * up).astype(bf16)
            ggu_ref[:, c : c + 128] = (back * up * slope).astype(bf16)
            ggu_ref[:, width + c : width + c + 128] = (back * gelu_gate).astype(bf16)
        if g == 0 and not first:
            sums.wait()
        for i in range(4):
            at = slice(i * rows, (i + 1) * rows)
            grad = nt(ggu_ref[...], w_ref[g, at, : 2 * width])
            if first and g == 0:
                acc_grad[:, at] = grad
            else:
                acc_grad[:, at] += grad
            if g == groups - 1 and not last:
                cols = pl.ds(i * rows, rows)
                store(acc_grad.at[:, cols], outs[-1].at[:, cols])
    if last:
        split_rows(z_ref, acc_grad, outs[2:6])
    for copy in stores:
        copy.wait()


def ffn_out_kernel(counts, z_ref, *refs):
    groups = len(counts)
    mids, refs = refs[:groups], refs[groups:]
    own, pass_part, both, w_ref, total_ref, sems = refs[-6:]
    pieces, width = list(refs[:-6]), mids[0].shape[1]
    copies, ends = [], []
    for g in range(groups):
        at = 0
        for piece in [pieces.pop(0) for _ in range(counts[g])]:
            copy = pltpu.make_async_copy(
                piece.at[:, pl.ds(2 * width, width)], w_ref.at[g, pl.ds(at, piece.shape[0])],
                sems.at[len(copies)],
            )
            copy.start()
            copies.append(copy)
            at += piece.shape[0]
        ends.append(len(copies))
    rows = w_ref.shape[1] // 4
    for g in range(groups):
        for copy in copies[ends[g] - counts[g] : ends[g]]:
            copy.wait()
        for i in range(4):
            at = slice(i * rows, (i + 1) * rows)
            out = nt(mids[g][...], w_ref[g, at, :])
            total_ref[:, at] = out if g == 0 else total_ref[:, at] + out
    count = own.shape[0]
    split_rows(
        z_ref, total_ref,
        [own, both.at[pl.ds(count, count)], pass_part, both.at[pl.ds(0, count)]],
    )


def grads_out_kernel(sides, *refs):
    lefts, rights, out = refs[:sides], refs[sides : 2 * sides], refs[2 * sides]
    held, sems = refs[2 * sides + 1 :]
    step = held.shape[0] // 2
    stores = []
    for part in range(2):
        rows, at = slice(part * step, (part + 1) * step), 0
        for left, right in zip(lefts, rights):
            width = right.shape[1]
            held[rows, at : at + width] = tn(left[:, rows], right[...]).astype(bf16)
            at += width
        copy = pltpu.make_async_copy(
            held.at[pl.ds(part * step, step)], out.at[pl.ds(part * step, step)], sems.at[part]
        )
        copy.start()
        stores.append(copy)
    for copy in stores:
        copy.wait()


def grads_own_kernel(sides, room, *refs):
    lefts, rights = refs[:sides], refs[sides : 2 * sides]
    got_any, own, x_top, y_bot, send_x, send_y = refs[2 * sides : 2 * sides + 6]
    got, grads, low, sems = refs[2 * sides + 6 :]
    q = x_top.shape[0]
    loads = [
        pltpu.make_async_copy(
            got_any.at[pl.ds(part * 4 * q, 4 * q)], got.at[pl.ds(part * 4 * q, 4 * q)], sems.at[part]
        )
        for part in range(2)
    ]
    for copy in loads:
        copy.start()
    stores = []

    def store(src, row, count, dst, to):
        copy = pltpu.make_async_copy(
            src.at[pl.ds(row * q, count * q)], dst.at[pl.ds(to * q, count * q)],
            sems.at[2 + len(stores)],
        )
        copy.start()
        stores.append(copy)

    for part in range(2):
        rows, at = slice(part * 4 * q, (part + 1) * 4 * q), 0
        loads[part].wait()
        for left, right in zip(lefts, rights):
            cols = slice(at, at + right.shape[1])
            at += right.shape[1]
            grads[rows, cols] = tn(left[:, rows], right[...]) + got[rows, cols].astype(f32)
        if part == 0:
            low[:q, :] = grads[3 * q : 4 * q, :].astype(bf16)
            store(grads, 0, 2, own, 0)
            store(grads, 2, 1, x_top, 0)
            store(low, 0, 1, send_x, room + 1)
        else:
            low[q : 2 * q, :] = grads[4 * q : 5 * q, :].astype(bf16)
            low[2 * q :, :] = grads[6 * q :, :].astype(bf16)
            store(low, 1, 1, send_y, room + 1)
            store(grads, 5, 1, y_bot, 0)
            store(low, 2, 1, send_y, room)
            store(low, 3, 1, send_x, room)
    for copy in stores:
        copy.wait()


def relay_kernel(groups, has_next, *refs):
    refs = list(refs)
    out_x, out_y = refs[-2:]
    at = 0
    for _ in range(groups):
        x_top, y_bot, got_x, got_y = refs[:4]
        del refs[:4]
        q, cols = x_top.shape[0], slice(at, at + x_top.shape[1])
        out_x[:q, cols] = (x_top[...] + got_y[:, cols].astype(f32)).astype(bf16)
        out_y[:q, cols] = (y_bot[...] + got_x[:, cols].astype(f32)).astype(bf16)
        at += x_top.shape[1]
    at = 0
    for _ in range(has_next):
        send_x, send_y = refs[:2]
        del refs[:2]
        cols = slice(at, at + send_x.shape[1])
        out_x[q:, cols] = send_x[...]
        out_y[q:, cols] = send_y[...]
        at += send_x.shape[1]


def joined(own, got_x, got_y, last_x, last_y, at, cols):
    q = last_x.shape[0]
    top = own[:q, at] + got_y[:, cols].astype(f32) + last_x[:, cols].astype(f32)
    bottom = own[q:, at] + got_x[:, cols].astype(f32) + last_y[:, cols].astype(f32)
    return jnp.concatenate([top, bottom], axis=0)


def join_ffn_kernel(*refs):
    gate_ref, up_ref, down_ref = refs[-3:]
    for c in range(chunk_count):
        parts = refs[5 * c : 5 * c + 5]
        width = parts[0].shape[1] // 3
        at = slice(c * width, (c + 1) * width)
        gate, up, down = [slice(k * width, (k + 1) * width) for k in range(3)]
        gate_ref[:, at] = joined(*parts, gate, gate)
        up_ref[:, at] = joined(*parts, up, up)
        down_ref[:, at] = joined(*parts, down, down)


def add_kernel(a_ref, b_ref, out_ref):
    out_ref[...] = (a_ref[...].astype(f32) + b_ref[...].astype(f32)).astype(out_ref.dtype)


def small_kernel(units, sums_ref, by_x, by_y, across, taps_ref, bias_ref, rate_ref, input_ref, decay_ref, one_ref, two_ref):
    total = (sums_ref[...] + by_x[...]) + (by_y[...] + across[...])
    heads, taps, _ = taps_ref.shape
    for h in range(heads):
        cols = slice(h * units, (h + 1) * units)
        taps_ref[h] = total[8 : 8 + taps, cols]
        bias_ref[h : h + 1, :] = total[8 + taps : 9 + taps, cols]
        rate_ref[h : h + 1, :] = total[1:2, cols]
        input_ref[h : h + 1, :] = total[2:3, cols]
        decay_ref[h : h + 1, :] = total[0:1, cols]
    wide = total.shape[1]
    for k in range(4):
        one_ref[k * wide : (k + 1) * wide] = total[16 + k]
        two_ref[k * wide : (k + 1) * wide] = total[20 + k]


def last_kernel(units, z_ref, *refs):
    x_ins, block_ins, gate_ins, small_ins = refs[:5], refs[5:9], refs[9:11], refs[11:15]
    x_ref, block_ref, rate_ref, input_ref = refs[15:19]
    join_x_kernel(*x_ins, x_ref)
    assemble_kernel(z_ref, *block_ins, block_ref)
    gate_join_kernel(z_ref, *gate_ins, rate_ref, input_ref)
    small_kernel(units, *small_ins, *refs[19:])


def gate_join_kernel(z_ref, mine_ref, other_ref, rate_ref, input_ref):
    pairs, _, units, _ = mine_ref.shape
    core = z_ref[1] % 2
    for src, head in ((mine_ref, core), (other_ref, 1 - core)):
        for p in range(pairs):
            whole = jnp.concatenate([src[p, z_ref[0] ^ owner] for owner in range(4)], axis=0)
            rate_ref[2 * p + head] = whole[:, :units].T
            input_ref[2 * p + head] = whole[:, units:].T


def relay_mixed_kernel(x_top, y_bot, got_x, got_y, send_x, send_y, out_x, out_y):
    q, width = x_top.shape[0], out_x.shape[1]
    for k in range(x_top.shape[1] // width):
        rows, cols = slice(k * q, (k + 1) * q), slice(k * width, (k + 1) * width)
        out_x[rows, :] = (x_top[:, cols] + got_y[:, cols].astype(f32)).astype(bf16)
        out_y[rows, :] = (y_bot[:, cols] + got_x[:, cols].astype(f32)).astype(bf16)
    out_x[(k + 1) * q :, :] = send_x[...]
    out_y[(k + 1) * q :, :] = send_y[...]


def join_yo_kernel(yo_own, yo_got_x, yo_got_y, y_x, y_y, o_x, o_y, y_ref, out_ref):
    width = y_ref.shape[0]
    first, second = slice(0, width), slice(width, 2 * width)
    y_ref[...] = joined(yo_own, yo_got_x[:, first], yo_got_y[:, first], y_x, y_y, first, first).T
    out_ref[...] = joined(
        yo_own, yo_got_x[:, second], yo_got_y[:, second], o_x, o_y, second, first
    ).T


def join_x_kernel(own, got_x, got_y, last_x, last_y, out_ref):
    cols = slice(0, out_ref.shape[0])
    out_ref[...] = joined(own, got_x, got_y, last_x, last_y, cols, cols).T


def exchange(v, axis, size, bit):
    return lax.ppermute(v, axis, [(i, i ^ bit) for i in range(size)])


def tie(*values):
    return lax.optimization_barrier(values)


def along(size, bit, v):
    return exchange(v, "dp", 8, bit) if size == 8 else v


def move(size, send_x, send_y):
    return along(size, 2, send_x), along(size, 4, send_y)


def gather_all(shard, size):
    mine, bit = shard, 2
    while bit < size:
        mine = jnp.concatenate([mine, exchange(mine, "dp", size, bit)], axis=0)
        bit *= 2
    return [mine], [exchange(mine, "dp", size, 1)]


class Scatter:
    def __init__(self, size, lefts, rights, name):
        self.size, self.name = size, name
        self.lefts, self.rights = lefts, rights
        self.model = lefts[0].shape[1]
        self.width = sum(r.shape[1] for r in rights)

    def halves(self, side):
        tokens = self.lefts[0].shape[0]
        return {i: block((tokens, self.model // 2), 0, side) for i in range(len(self.lefts))}

    def sibling(self, run):
        shape = (self.model // 2, self.width)
        return run(
            partial(grads_out_kernel, len(self.lefts)), [like(shape, bf16)],
            *self.lefts, *self.rights, specs=self.halves(1),
            out_specs=[pl.BlockSpec(memory_space=pl.ANY)],
            scratch=[pltpu.VMEM(shape, bf16), pltpu.SemaphoreType.DMA((2,))],
            name="grads_out_" + self.name,
        )[0]

    def swap(self, out):
        return exchange(out, "dp", self.size, 1)

    def own(self, run, got, room=0):
        q, w = self.model // 16, self.width
        sends = [like(((2 + room) * q, w), bf16)] * 2
        anywhere = pl.BlockSpec(memory_space=pl.ANY)
        specs = self.halves(0)
        specs[2 * len(self.lefts)] = anywhere
        return run(
            partial(grads_own_kernel, len(self.lefts), room),
            [like((2 * q, w), f32), like((q, w), f32), like((q, w), f32)] + sends,
            *self.lefts, *self.rights, got, specs=specs, out_specs=[anywhere] * 5,
            scratch=[
                pltpu.VMEM((8 * q, w), bf16), pltpu.VMEM((8 * q, w), f32), pltpu.VMEM((4 * q, w), bf16),
                pltpu.SemaphoreType.DMA((9,)),
            ],
            name="grads_own_" + self.name,
        )

    def join(self, cut):
        own, x_top, y_bot, from_x, from_y = cut
        q = x_top.shape[0]
        from_x, from_y = from_x[-2 * q :], from_y[-2 * q :]
        total = jnp.concatenate(
            [own, x_top, from_x[q:].astype(f32), from_y[q:].astype(f32), y_bot,
             from_y[:q].astype(f32), from_x[:q].astype(f32)],
            axis=0,
        )
        bit = self.size // 2
        while bit > 1:
            half = total.shape[0] // 2
            total = total[:half] + exchange(total[half:].astype(bf16), "dp", self.size, bit).astype(f32)
            bit //= 2
        return total


def relay(run, cuts, got, base, nexts, name):
    q = cuts[0][1].shape[0]
    width = sum(cut[1].shape[1] for cut in cuts)
    ins, specs, options = [], {}, {}
    for cut in cuts:
        ins += [cut[1], cut[2]]
        for v in got:
            specs[len(ins)] = block((q, v.shape[1]), base, 0)
            ins.append(v)
    if len(nexts) == 1:
        options = dict(
            alias={len(ins): 0, len(ins) + 1: 1}, out_specs=[block((q, width), 0, 0)] * 2
        )
        specs[len(ins)] = specs[len(ins) + 1] = pl.BlockSpec(memory_space=pl.ANY)
    for cut in nexts:
        ins += [cut[3], cut[4]]
    return run(
        partial(relay_kernel, len(cuts), 0 if len(nexts) == 1 else len(nexts)),
        [like((3 * q if nexts else q, width), bf16)] * 2, *ins, specs=specs, name=name, **options,
    )


def to_owner(part):
    return exchange(part, "tensor", 4, 1)


def pass_on(part, got):
    return exchange((part + got.astype(f32)).astype(bf16), "tensor", 4, 2)


class Order:
    def __init__(self):
        self.last = None

    def after(self, *values):
        if self.last is not None:
            values, _ = lax.optimization_barrier((values, self.last))
        return values if len(values) > 1 else values[0]

    def wait(self, *values):
        values = self.after(*values)
        self.last = jax.tree.leaves(values)[0]
        return values

    def run(self, kernel, outs, *args, **options):
        results = call(kernel, outs, *self.after(*args), **options)
        self.last = results[0]
        return results


def spread(piece):
    return exchange(piece, "tensor", 4, 2), exchange(piece, "tensor", 4, 1)


def neighbour(v):
    return exchange(v, "tensor", 4, 1)


def sum_over(v, axis, size, first=1, until=None):
    bit = first
    while bit < (until or size):
        v = v + exchange(v, axis, size, bit)
        bit *= 2
    return v


def sum_low(v, axis, size, first=1, until=None):
    bit = first
    while bit < (until or size):
        low = v.astype(bf16)
        v = low.astype(f32) + exchange(low, axis, size, bit).astype(f32)
        bit *= 2
    return v


def body(
    tokens, segments, first_gain, x_weight, y_weight, conv_weight, conv_bias, rate_weight,
    input_weight, rate_bias, input_bias, decay_logit, out_weight, second_gain, gate_weight,
    up_weight, down_weight, cotangent, dp_size,
):
    count, model = tokens.shape
    heads, _, units = rate_weight.shape
    chan = heads * units
    pairs = heads // 2
    taps = conv_weight.shape[0]
    hidden_units = gate_weight.shape[1]
    width = hidden_units // chunk_count
    me = lax.axis_index("dp")
    z = lax.axis_index("tensor").astype(jnp.int32)
    ids = jnp.stack([z, me.astype(jnp.int32)])
    part = model // dp_size
    q = model // 16
    rows = count // 4
    size = dp_size
    order = Order()
    after, wait, run = order.after, order.wait, order.run
    anywhere = pl.BlockSpec(memory_space=pl.ANY)
    lane = pl.BlockSpec((count, 128), lambda p: (0, p))
    line = pl.BlockSpec((1, 128), lambda p: (0, p))
    sums_spec = pl.BlockSpec((8, 128), lambda p: (0, p))
    block_spec = pl.BlockSpec((1, 8 * units, 4 * units), lambda p: (p, 0, 0))
    mask_spec = pl.BlockSpec((taps - 1, count, 128), lambda p: (0, 0, 0))
    pair_grid = dict(
        grid=(pairs,), cost_estimate=hint,
        compiler_params=pltpu.CompilerParams(vmem_limit_bytes=60 * MIB),
    )
    split_shapes = [like((rows, model), t) for t in (f32, bf16, f32, bf16)]
    split_specs = [pl.BlockSpec((rows, model), lambda p: (0, 0))] * 4
    total_scratch = [pltpu.VMEM((count, model), f32)]

    def sibling(v):
        return exchange(v, "dp", size, 1)

    def halves(by_x, by_y):
        half = by_x.shape[0] // 2
        lower, upper = move(size, by_y[half:], by_x[:half])
        return upper, lower

    def pieces_of(shard, *got):
        if size == 8:
            return [shard, *got[: len(got) // 2]], list(got[len(got) // 2 :])
        return gather_all(shard, size)

    def assemble(pieces, dtype, name, specs=None):
        return run(
            assemble_kernel, [like((count, model), dtype)], ids, *pieces, scalars=1, specs=specs,
            name=name,
        )[0]

    xs = x_weight.reshape(part, chan)
    x_x, x_y = move(size, xs, xs)
    x_s = sibling(xs)

    def ffn_shard(c):
        cols = block((part, width), 0, c)
        return run(
            shard_kernel, [like((part, 3 * width), bf16)], gate_weight, up_weight, down_weight.T,
            specs={0: cols, 1: cols, 2: cols}, name="shard",
        )[0]

    f0 = ffn_shard(0)
    y_after, out_after = after(y_weight, out_weight)
    yo = jnp.concatenate([y_after.reshape(part, chan), out_after.reshape(chan, part).T], axis=1)
    x_x, x_y, x_s, yo = wait(x_x, x_y, x_s, yo)

    x_top, x_bot = halves(x_x, x_y)
    x_sx, x_sy = sibling(x_x), sibling(x_y)
    x_rel, nf, gain_one, gain_two = run(
        partial(norm_first_kernel, size),
        [like((count, model), bf16)] * 2 + [like((1, model), f32)] * 2,
        ids, tokens, first_gain, second_gain, scalars=1,
        name="norm_first",
    )
    segs = after(segments)
    masks = jnp.stack(
        [
            jnp.concatenate([jnp.full((lag,), -1, jnp.int32), segs[:-lag]]) == segs
            for lag in range(1, taps)
        ]
    ).astype(f32)
    masks = jnp.broadcast_to(masks[:, :, None], (taps - 1, count, 128))
    taps_flat = conv_weight.reshape(taps, chan)
    bias_flat = conv_bias.reshape(1, chan)
    rate_flat, input_flat = rate_bias.reshape(1, chan), input_bias.reshape(1, chan)
    decay_flat = decay_logit.reshape(1, chan)
    masks, taps_flat, bias_flat, rate_flat, input_flat, decay_flat, x_top, x_bot, x_sx, x_sy = wait(
        masks, taps_flat, bias_flat, rate_flat, input_flat, decay_flat, x_top, x_bot, x_sx, x_sy
    )
    yo_x, yo_y = move(size, *after(yo, yo))
    x_st, x_sb = sibling(x_top), sibling(x_bot)
    x_st, x_sb = wait(x_st, x_sb)
    own_x, sib_x = pieces_of(xs, x_x, x_y, x_top, x_bot, x_s, x_sx, x_sy, x_st, x_sb)
    all_x = own_x + sib_x
    x_branch, conv_low = run(
        branch_kernel, [like((count, chan), f32), like((count, chan), bf16)],
        nf, taps_flat, bias_flat, masks, *all_x,
        specs={4 + i: anywhere for i in range(len(all_x))},
        scratch=[pltpu.VMEM((model, chan), bf16), pltpu.SemaphoreType.DMA((len(all_x),))],
        name="branch",
    )
    conv2, conv1 = spread(conv_low)
    yo_s = sibling(after(yo))
    f1 = ffn_shard(1)
    (blocks,) = run(
        blocks_kernel, [like((pairs, 8 * units, 4 * units), bf16)], ids,
        rate_weight.transpose(0, 2, 1), input_weight.transpose(0, 2, 1),
        scalars=1, name="gate_blocks",
    )
    conv2, conv1, yo_x, yo_y, yo_s = wait(conv2, conv1, yo_x, yo_y, yo_s)
    conv3 = neighbour(conv2)
    yo_top, yo_bot = halves(yo_x, yo_y)
    yo_sx, yo_sy = sibling(yo_x), sibling(yo_y)
    (cot_rel,) = run(
        partial(to_rel_kernel, size), [like((count, model), bf16)], ids, cotangent, scalars=1,
        name="cotangent",
    )
    conv3, yo_top, yo_bot, yo_sx, yo_sy = wait(conv3, yo_top, yo_bot, yo_sx, yo_sy)
    conv = [conv_low, conv1, conv2, conv3]
    f0_x, f0_y = move(size, *after(f0, f0))
    f0_s = sibling(after(f0))
    yo_st, yo_sb = sibling(yo_top), sibling(yo_bot)
    rate, entry, hidden = pl.pallas_call(
        forward_scan_kernel,
        in_specs=[lane] * 4 + [block_spec] + [line] * 3 + [mask_spec],
        out_specs=[lane] * 3,
        out_shape=[like((count, chan), f32)] * 3,
        name="forward_scan",
        **pair_grid,
    )(*conv, blocks, rate_flat, input_flat, decay_flat, masks)
    order.last = rate
    yo_st, yo_sb, f0_s, hidden = wait(yo_st, yo_sb, f0_s, hidden)
    own_yo, sib_yo = pieces_of(yo, yo_x, yo_y, yo_top, yo_bot, yo_s, yo_sx, yo_sy, yo_st, yo_sb)
    all_yo = own_yo + sib_yo
    y_branch, mixed, *parts = run(
        mix_kernel,
        [like((count, chan), f32), like((count, chan), bf16)] + split_shapes,
        ids, nf, hidden, *all_yo, scalars=1,
        specs={3 + i: anywhere for i in range(len(all_yo))},
        scratch=total_scratch
        + [pltpu.VMEM((2, model, chan), bf16), pltpu.SemaphoreType.DMA((2 * len(all_yo),))],
        name="mix",
    )
    got3 = to_owner(parts[3])
    f1_x, f1_y = move(size, f1, after(f1))
    got3, f0_x, f0_y = wait(got3, f0_x, f0_y)
    (low,) = run(add_kernel, [like((rows, model), bf16)], parts[2], got3, name="first_add")
    got2, got1 = exchange(low, "tensor", 4, 2), to_owner(after(parts[1]))
    f0_sx = sibling(f0_x)
    got2, got1, f1_x, f1_y, f0_sx = wait(got2, got1, f1_x, f1_y, f0_sx)
    f0_far, f1_far = along(size, 2, after(f0_y)), along(size, 4, f1_x)
    f1_sx, f1_sy, f0_sy = sibling(f1_x), sibling(f1_y), sibling(after(f0_y))
    residual, second_rows = run(
        norm_second_kernel, [like((rows, model), f32), like((rows, model), bf16)],
        ids, x_rel, gain_two, parts[0], got1, got2, scalars=1, name="norm_second",
    )
    second_rows, f1_sx, f1_sy, f0_sy = wait(second_rows, f1_sx, f1_sy, f0_sy)
    sec2, sec1 = spread(second_rows)
    f2 = ffn_shard(2)
    sec2, sec1 = wait(sec2, sec1)
    sec3 = neighbour(sec2)
    sec3, f0_far, f1_far = wait(sec3, f0_far, f1_far)
    f2_x, f2_y = move(size, *after(f2, f2))
    f0_sf, f1_sf, f1_s = sibling(f0_far), sibling(f1_far), sibling(after(f1))
    f0_sf, f1_sf, f1_s = wait(f0_sf, f1_sf, f1_s)
    f2_s = sibling(after(f2))

    def ffn(left, groups, sums, first, last, name):
        outs = [like((count, 2 * width), bf16), like((count, width), bf16)] * len(groups)
        out_specs = [full(v) for v in outs]
        if first:
            outs.append(like((count, model), bf16))
            out_specs.append(anywhere)
        if last:
            outs += split_shapes
            out_specs += [full(v) for v in split_shapes]
        else:
            outs.append(like((count, model), f32))
            out_specs.append(anywhere)
        weights = sum([own + sib for own, sib in groups], [])
        scratch = [
            pltpu.VMEM((count, model), bf16),
            pltpu.VMEM((count, model), bf16),
            pltpu.VMEM((count, 2 * width), f32),
            pltpu.VMEM((count, width), f32),
            pltpu.VMEM((len(groups), model, 3 * width), bf16),
            pltpu.VMEM((count, model), f32),
            pltpu.SemaphoreType.DMA((len(weights) + 3,)),
            pltpu.SemaphoreType.DMA((5,)),
        ]
        ins = [ids, *left, *sums, cot_rel, *weights]
        at = 1 + len(left) * first
        return run(
            partial(ffn_kernel, len(groups), first, last), outs, *ins, scalars=1, scratch=scratch,
            specs={i: anywhere for i in range(at, len(ins))}, out_specs=out_specs, name=name,
        )

    groups = [
        pieces_of(f0, f0_x, f0_y, f0_far, f0_s, f0_sx, f0_sy, f0_sf),
        pieces_of(f1, f1_x, f1_y, f1_far, f1_s, f1_sx, f1_sy, f1_sf),
    ]
    a, mid0, c, mid1, second, *sums = ffn(
        [second_rows, sec1, sec2, sec3], groups, [], True, False, "ffn_01"
    )
    b, d = mid0, mid1
    s0 = Scatter(size, [second, cot_rel], [a, b], "ffn_0")
    s1 = Scatter(size, [second, cot_rel], [c, d], "ffn_1")
    s0_out = s0.sibling(run)
    s0_out, f2_s, f2_x, f2_y = wait(s0_out, f2_s, f2_x, f2_y)
    f2_top, f2_bot = halves(f2_x, f2_y)
    f2_sx, f2_sy = sibling(f2_x), sibling(f2_y)
    s0_swap = s0.swap(s0_out)
    s1_out = s1.sibling(run)
    f2_sx, f2_sy, s0_swap = wait(f2_sx, f2_sy, s0_swap)
    s0_cut = s0.own(run, s0_swap)
    f2_top, f2_bot, s0_send = wait(f2_top, f2_bot, tuple(s0_cut[3:]))
    f2_st, f2_sb = sibling(f2_top), sibling(f2_bot)
    f2_st, f2_sb = wait(f2_st, f2_sb)
    s0_got = move(size, *after(*s0_send))
    s1_swap = s1.swap(after(s1_out))
    groups.append(pieces_of(f2, f2_x, f2_y, f2_top, f2_bot, f2_s, f2_sx, f2_sy, f2_st, f2_sb))
    a, b, *grad_parts = ffn([second], groups[2:], sums, False, True, "ffn_2")
    mid2 = b
    s2 = Scatter(size, [second, cot_rel], [a, b], "ffn_2")
    grad_parts, s1_swap = wait(tuple(grad_parts), s1_swap)

    got3, got1 = to_owner(grad_parts[3]), to_owner(grad_parts[1])
    s1_cut = s1.own(run, s1_swap)
    s2_out = s2.sibling(run)
    got3, s0_got, s2_out, s1_send = wait(got3, s0_got, s2_out, tuple(s1_cut[3:]))
    got2 = pass_on(grad_parts[2], got3)
    s1_got = move(size, *s1_send)
    s2_swap = s2.swap(s2_out)
    lists = [own + sib for own, sib in groups]
    ins = [ids, mid0, mid1, mid2, *sum(lists, [])]
    out_parts = run(
        partial(ffn_out_kernel, [len(v) for v in lists]),
        [like((rows, model), f32)] * 2 + [like((2 * rows, model), bf16)], *ins, scalars=1,
        specs={i: anywhere for i in range(4, len(ins))},
        scratch=[
            pltpu.VMEM((chunk_count, model, width), bf16), pltpu.VMEM((count, model), f32),
            pltpu.SemaphoreType.DMA((len(ins),)),
        ],
        name="ffn_out",
    )
    got2, got1, s2_swap = wait(got2, got1, s2_swap)
    grad_res, rec_rows, second_gain = run(
        partial(second_back_kernel, size),
        [like((rows, model), f32), like((rows, model), bf16), like((1, model), f32)],
        ids, cot_rel, gain_two, residual, grad_parts[0], got1, got2, scalars=1, micros=6, name="second_back",
    )
    rec2, rec1 = spread(rec_rows)
    s2_cut = s2.own(run, s2_swap, 1)
    sends = relay(run, [s0_cut], s0_got, 0, [s2_cut], "relay_0")
    rec2, rec1, s1_got, sends = wait(rec2, rec1, s1_got, tuple(sends))
    rec3 = neighbour(rec2)
    slot = move(size, *sends)
    rec3 = wait(rec3)
    out_got = neighbour(after(out_parts[2]))

    whole = pl.BlockSpec((count, model), lambda p: (0, 0))
    piece = pl.BlockSpec((rows, model), lambda p: (0, 0))
    gate_spec = pl.BlockSpec((1, 4, units, 2 * units), lambda p: (p, 0, 0, 0))
    gate_half = like((pairs, 4, units, 2 * units), bf16)
    grad_rec, grad_y, direct, h1, h2, h3, gate_mine, gate_theirs, scan_sums = pl.pallas_call(
        partial(backward_scan_kernel, len(all_yo)),
        in_specs=[smem] + [piece] * 4
        + [pl.BlockSpec((v.shape[0], 128), lambda p: (0, pairs + p)) for v in all_yo] + [lane] * 4
        + [block_spec, line, lane, mask_spec] + [lane] * 3,
        out_specs=[whole, lane, lane, lane, lane, lane, gate_spec, gate_spec, sums_spec],
        out_shape=[like((count, model), bf16)]
        + [like((count, chan), t) for t in (bf16, f32, bf16, f32, bf16)]
        + [gate_half, gate_half, like((8, chan), f32)],
        name="backward_scan",
        **pair_grid,
    )(
        *after(ids, rec_rows, rec1, rec2, rec3, *all_yo, *conv, blocks, decay_flat, y_branch, masks),
        rate, entry, hidden,
    )
    order.last = grad_rec
    out_got, h1, h2, h3 = wait(out_got, h1, h2, h3)
    got3 = to_owner(h3)
    gate_got = sibling(gate_theirs)
    syo = Scatter(size, [nf, grad_rec], [grad_y, mixed], "yo")
    syo_out = syo.sibling(run)
    s1_send = relay(run, [s1_cut], s1_got, 0, [], "relay_1")
    got3, syo_out, gate_got, s1_send = wait(got3, syo_out, gate_got, tuple(s1_send))
    got2, got1 = pass_on(h2, got3), to_owner(after(h1))
    (gate_sum,) = run(add_kernel, [gate_half], gate_mine, gate_got, name="gate_add")
    (out_low,) = run(
        add_kernel, [like((rows, model), bf16)], out_parts[1], out_got,
        specs={1: block((rows, model), 0, 0)}, name="out_add",
    )
    got2, got1, slot, out_low = wait(got2, got1, slot, out_low)
    out_got2 = exchange(out_low, "tensor", 4, 2)
    s1_last = move(size, *after(*s1_send))
    syo_swap = syo.swap(after(syo_out))
    gate_got = along(size, 2, after(gate_sum))
    whole_row = pl.BlockSpec((1, model), lambda p: (0, 0))
    grad_x, conv_sums, first_gain, *first_parts = pl.pallas_call(
        partial(conv_back_kernel, size, len(all_x)),
        in_specs=[smem] + [lane] * 4 + [pl.BlockSpec((taps, 128), lambda p: (0, p)), mask_spec, lane]
        + [whole] + [anywhere] * (2 * len(all_x)),
        out_specs=[lane, sums_spec, whole_row] + split_specs,
        out_shape=[like((count, chan), bf16), like((8, chan), f32), like((1, model), f32)]
        + split_shapes,
        scratch_shapes=total_scratch
        + [
            pltpu.VMEM((model, 2 * chan), bf16),
            pltpu.VMEM((count, 2 * chan), bf16),
            pltpu.SemaphoreType.DMA((2 * len(all_x),)),
        ],
        name="conv_back",
        **pair_grid,
    )(*after(ids, direct, got1, got2, x_branch, taps_flat, masks, grad_y, x_rel, *all_x, *all_yo))
    order.last = grad_x
    first_parts, syo_swap, out_got2 = wait(tuple(first_parts), syo_swap, out_got2)
    got3 = to_owner(first_parts[3])
    sx = Scatter(size, [nf], [grad_x], "x")
    sx_out = sx.sibling(run)
    syo_cut = syo.own(run, syo_swap)
    s2_send = relay(run, [s2_cut], slot, 1, [], "relay_2")
    got3, sx_out, yo_send, s1_last, gate_got, s2_send = wait(
        got3, sx_out, tuple(syo_cut[3:]), s1_last, gate_got, tuple(s2_send)
    )
    got2, got1 = pass_on(first_parts[2], got3), to_owner(after(first_parts[1]))
    sx_swap = sx.swap(sx_out)
    yo_got = move(size, *yo_send)
    got2, got1, sx_swap, yo_got = wait(got2, got1, sx_swap, yo_got)
    (tokens_rows,) = run(
        partial(first_back_kernel, size), [like((rows, model), bf16)],
        ids, x_rel, gain_one, grad_res, first_parts[0], got1, got2, scalars=1, name="first_back",
    )
    gains = jnp.concatenate([first_gain, second_gain], axis=0)
    tok2, tok1 = spread(tokens_rows)
    gains = sum_over(after(gains), "tensor", 4, 1, 2)
    s2_last = move(size, *after(*s2_send))
    sx_cut = sx.own(run, sx_swap)
    specs = {k: block((q, 2 * chan), 0, 0) for k in (2, 3)}
    mixed_sends = run(
        relay_mixed_kernel, [like((4 * q, chan), bf16)] * 2, syo_cut[1], syo_cut[2], *yo_got,
        *sx_cut[3:], specs=specs, name="relay_3",
    )
    (block_rows,) = run(
        partial(block_out_kernel, size), [like((rows, model), bf16)],
        ids, residual, out_parts[0], out_got, out_got2, scalars=1,
        specs={3: block((rows, model), 1, 0)}, name="block_out",
    )
    (gate_sum,) = run(add_kernel, [gate_half], gate_sum, gate_got, name="gate_add")
    tok2, tok1, s2_last, gains, mixed_sends = wait(tok2, tok1, s2_last, gains, tuple(mixed_sends))
    tok3 = neighbour(tok2)
    slot3 = move(size, *mixed_sends)
    block2 = exchange(after(block_rows), "tensor", 4, 2)
    gains = sum_over(gains, "tensor", 4, 2)
    if size == 8:
        ins, specs = [], {}
        for cut, (got, base), last in (
            (s0_cut, (s0_got, 0), slot), (s1_cut, (s1_got, 0), s1_last), (s2_cut, (slot, 1), s2_last)
        ):
            ins.append(cut[0])
            for v, at in ((got[0], base + 1), (got[1], base + 1), (last[0], 0), (last[1], 0)):
                specs[len(ins)] = block((q, v.shape[1]), at, 0)
                ins.append(v)
        gate_share, up_share, down_share = run(
            join_ffn_kernel,
            [like((part, hidden_units), f32)] * 3,
            *ins, specs=specs, name="join_ffn",
        )
    else:
        shares = [s0.join(s0_cut), s1.join(s1_cut), s2.join(s2_cut)]
        gate_share, up_share, down_share = [
            jnp.concatenate([v[:, k * width : (k + 1) * width] for v in shares], axis=1)
            for k in range(3)
        ]
    tok3, gains, slot3, block2 = wait(tok3, gains, slot3, block2)
    small = jnp.concatenate([scan_sums, conv_sums, gains.reshape(8, chan)], axis=0)
    small = sum_over(small, "dp", size, 1, 2)
    block13 = neighbour(jnp.concatenate([block_rows, block2], axis=0))
    gate_got = along(size, 4, after(gate_sum))
    x_last = move(size, *relay(run, [sx_cut], slot3, 2, [], "relay_4"))
    yo_ins = [syo_cut[0], *yo_got, *slot3, *slot3]
    if size == 8:
        specs = {1: block((q, 2 * chan), 1, 0), 2: block((q, 2 * chan), 1, 0)}
        for k, at in enumerate((0, 0, 1, 1)):
            specs[3 + k] = block((q, chan), at, 0)
        y_share, out_share = run(
            join_yo_kernel, [like((chan, part), f32)] * 2, *yo_ins, specs=specs, name="join_yo"
        )
    tokens_grad = assemble([tokens_rows, tok1, tok2, tok3], f32, "tokens_grad_all")
    (gate_sum,) = run(
        add_kernel, [like(gate_half.shape, f32)], gate_sum, wait(gate_got), name="gate_add"
    )
    x_last, block13, small, gate_sum = wait(x_last, block13, small, gate_sum)
    block_ins = [block_rows, block13, block2, block13]
    block_specs = {2: block((rows, model), 0, 0), 4: block((rows, model), 1, 0)}
    if size == 8:
        by_x, by_y, across = [exchange(small, "dp", size, bit) for bit in (2, 4, 6)]
        gate_got = sibling(gate_sum)
        gate_got, by_x, by_y, across = wait(gate_got, by_x, by_y, across)
        ins = [ids, sx_cut[0], *slot3, *x_last, *block_ins, gate_sum, gate_got, small, by_x, by_y, across]
        specs = {k: block((q, chan), 3 if k < 4 else 0, 0) for k in range(2, 6)}
        specs.update({6 + k: v for k, v in ((1, block_specs[2]), (3, block_specs[4]))})
        head_like, gate_like = like((heads, units), f32), like((heads, units, 4 * units), f32)
        (
            x_share, block_out, rate_grad, input_grad, taps_grad, bias_grad, rate_b_grad,
            input_b_grad, decay_grad, one_grad, two_grad,
        ) = run(
            partial(last_kernel, units),
            [like((chan, part), f32), like((count, model), bf16), gate_like, gate_like]
            + [like((heads, taps, units), f32)] + [head_like] * 4 + [like((model,), f32)] * 2,
            *ins, scalars=1, specs=specs, name="last",
        )
        rate_grad, input_grad = rate_grad.transpose(0, 2, 1), input_grad.transpose(0, 2, 1)
        taps_grad = taps_grad.transpose(1, 0, 2)
    else:
        block_out = assemble(block_ins, bf16, "block_out_all", block_specs)
        small = sum_over(small, "dp", size, 2)
        taps_grad = small[8 : 8 + taps].reshape(taps, heads, units)
        bias_grad, rate_b_grad, input_b_grad, decay_grad = [
            small[k].reshape(heads, units) for k in (8 + taps, 1, 2, 0)
        ]
        one_grad, two_grad = small[16:20].reshape(model), small[20:].reshape(model)
        yo_share, x_share = syo.join(syo_cut), sx.join(sx_cut)
        x_share, y_share, out_share = x_share.T, yo_share[:, :chan].T, yo_share[:, chan:].T
        mine = sum_low(gate_mine + sibling(gate_theirs), "dp", size, 2)
        other, core = sibling(mine), me % 2
        gate_sum = jnp.stack(
            [jnp.where(core == 0, mine, other), jnp.where(core == 0, other, mine)], axis=1
        ).reshape(heads, 4, units, 2 * units)
        gate_sum = jnp.concatenate(
            [lax.dynamic_index_in_dim(gate_sum, z ^ k, 1, False) for k in range(4)], axis=1
        )
        rate_grad, input_grad = gate_sum[:, :, :units], gate_sum[:, :, units:]
    x_share = x_share.reshape(heads, units, part).transpose(2, 0, 1)
    y_share = y_share.reshape(heads, units, part).transpose(2, 0, 1)
    return (
        block_out,
        tokens_grad,
        one_grad,
        x_share,
        y_share,
        taps_grad,
        bias_grad,
        rate_grad,
        input_grad,
        rate_b_grad,
        input_b_grad,
        decay_grad,
        out_share.reshape(heads, units, part),
        two_grad,
        gate_share,
        up_share,
        down_share.T,
    )


def solution(mesh):
    return jax.shard_map(
        partial(body, dp_size=mesh.shape["dp"]),
        mesh=mesh,
        in_specs=(
            P("dp", None),
            P("dp"),
            P(),
            P("dp", None, "tensor"),
            P("dp", None, "tensor"),
            P(None, None, "tensor"),
            P(None, "tensor"),
            P(None, None, "tensor"),
            P(None, None, "tensor"),
            P(None, "tensor"),
            P(None, "tensor"),
            P(None, "tensor"),
            P(None, "tensor", "dp"),
            P(),
            P("dp", "tensor"),
            P("dp", "tensor"),
            P("tensor", "dp"),
            P("dp", None),
        ),
        out_specs=(
            P("dp", None),
            P("dp", None),
            P(),
            P("dp", None, "tensor"),
            P("dp", None, "tensor"),
            P(None, None, "tensor"),
            P(None, "tensor"),
            P(None, None, "tensor"),
            P(None, None, "tensor"),
            P(None, "tensor"),
            P(None, "tensor"),
            P(None, "tensor"),
            P(None, "tensor", "dp"),
            P(),
            P("dp", "tensor"),
            P("dp", "tensor"),
            P("tensor", "dp"),
        ),
        check_vma=False,
    )
```

```python
from functools import partial

import jax
import jax.numpy as jnp
from jax import lax
from jax.experimental import pallas as pl
from jax.experimental.pallas import tpu as pltpu
from jax.sharding import PartitionSpec as P

eps = 1e-06
f32 = jnp.float32
bf16 = jnp.bfloat16
vmem = pl.BlockSpec(memory_space=pltpu.VMEM)
smem = pl.BlockSpec(memory_space=pltpu.SMEM)
MIB = 1024 * 1024
chunk_count = 3


def nn(a, b):
    return lax.dot_general(a, b, (((1,), (0,)), ((), ())), preferred_element_type=f32)


def nt(a, b):
    return lax.dot_general(a, b, (((1,), (1,)), ((), ())), preferred_element_type=f32)


def tn(a, b):
    return lax.dot_general(a, b, (((0,), (0,)), ((), ())), preferred_element_type=f32)


def full(v):
    zeros = (0,) * len(v.shape)
    return pl.BlockSpec(v.shape, lambda i: zeros, pipeline_mode=pl.Buffered(1))


def block(shape, *index):
    return pl.BlockSpec(shape, lambda i: index)


def hint_of(micros):
    return pl.CostEstimate(
        flops=1, bytes_accessed=max(1, int(micros * 3.0e6)), transcendentals=0
    )


hint = hint_of(0)


def call(kernel, outs, *args, scalars=0, mem=60, specs=None, out_specs=None, alias=None, scratch=(), micros=0, name=None):
    specs = specs or {}
    return pl.pallas_call(
        kernel,
        grid=(1,),
        out_shape=outs,
        in_specs=[smem] * scalars
        + [specs.get(i) or full(a) for i, a in enumerate(args) if i >= scalars],
        out_specs=out_specs or [full(s) for s in outs],
        scratch_shapes=scratch,
        input_output_aliases=alias or {},
        compiler_params=pltpu.CompilerParams(vmem_limit_bytes=mem * MIB),
        cost_estimate=hint_of(micros),
        name=name,
    )(*args)


def like(shape, dtype):
    return jax.ShapeDtypeStruct(shape, dtype)


def gelu_pair(v):
    c = 0.7978845608028654
    sq = v * v
    t = jnp.tanh(c * v * (1.0 + 0.044715 * sq))
    half = 0.5 * (1.0 + t)
    slope = half + 0.5 * v * (1.0 - t * t) * c * (1.0 + 3.0 * 0.044715 * sq)
    return v * half, slope


def one_less_exp(x):
    series = x * (
        1.0
        - x * (1 / 2) * (1.0 - x * (1 / 3) * (1.0 - x * (1 / 4) * (1.0 - x * (1 / 5) * (
            1.0 - x * (1 / 6) * (1.0 - x * (1 / 7) * (1.0 - x * (1 / 8)))))))
    )
    return jnp.where(x < 0.5, series, 1.0 - jnp.exp(-x))


def softplus(v):
    return jnp.maximum(v, 0.0) + jnp.log1p(jnp.exp(-jnp.abs(v)))


def sigmoid(v):
    return 1.0 / (1.0 + jnp.exp(-v))


def row_ids(shape):
    return lax.broadcasted_iota(jnp.int32, shape, 0)


def down_rows(v, steps, fill=0.0):
    return jnp.where(row_ids(v.shape) >= steps, pltpu.roll(v, steps, 0), fill)


def up_rows(v, steps, fill=0.0):
    rows = v.shape[0]
    return jnp.where(row_ids(v.shape) < rows - steps, pltpu.roll(v, rows - steps, 0), fill)


def scan_rows(decay, drive, shift):
    steps = 1
    while steps < decay.shape[0]:
        drive = decay * shift(drive, steps) + drive
        if steps * 2 < decay.shape[0]:
            decay = decay * shift(decay, steps, 1.0)
        steps *= 2
    return drive


def norm_first_kernel(size, z_ref, x_ref, one_ref, two_ref, rel_ref, out_ref, one_out, two_out):
    me = z_ref[1]
    gain = to_rel(me, size, one_ref[...].reshape(1, -1))
    rel = to_rel(me, size, x_ref[...].astype(f32))
    rel_ref[...] = rel.astype(bf16)
    inv = lax.rsqrt(jnp.mean(rel * rel, axis=1, keepdims=True) + eps)
    out_ref[...] = (rel * inv * gain).astype(bf16)
    one_out[...] = gain
    two_out[...] = to_rel(me, size, two_ref[...].reshape(1, -1))


def to_rel_kernel(size, z_ref, x_ref, rel_ref):
    rel_ref[...] = to_rel(z_ref[1], size, x_ref[...].astype(f32)).astype(bf16)


def shard_kernel(gate_ref, up_ref, down_ref, out_ref):
    width = gate_ref.shape[1]
    out_ref[:, :width] = gate_ref[...]
    out_ref[:, width : 2 * width] = up_ref[...]
    out_ref[:, 2 * width :] = down_ref[...]


def blocks_kernel(z_ref, rate_ref, input_ref, out_ref):
    units = rate_ref.shape[1]
    zero = jnp.zeros((units, units), bf16)
    for p in range(out_ref.shape[0]):
        for a in range(2):
            parts = [ref[2 * p + a].T for ref in (rate_ref, input_ref)]
            rows = []
            for k in range(4):
                row = []
                for part in parts:
                    one = jnp.zeros_like(zero)
                    for owner in range(4):
                        one = jnp.where(
                            (z_ref[0] ^ k) == owner, part[owner * units : (owner + 1) * units], one
                        )
                    row += [zero, one] if a else [one, zero]
                at = slice((2 * k + a) * units, (2 * k + a + 1) * units)
                out_ref[p, at, :] = jnp.concatenate(row, axis=1)


def land(pieces, w_ref, sems, first=0):
    copies, at = [], 0
    for n, piece in enumerate(pieces):
        rows = piece.shape[0]
        copy = pltpu.make_async_copy(piece, w_ref.at[pl.ds(at, rows)], sems.at[first + n])
        copy.start()
        copies.append((at, copy))
        at += rows
    return copies


def await_rows(copies, until):
    while copies and copies[0][0] < until:
        copies.pop(0)[1].wait()


def join_kernel(count, *refs):
    pieces, (first, second, sems) = refs[:-3], refs[-3:]
    copies = land(pieces[:count], first, sems) + land(pieces[count:], second, sems, count)
    for _, copy in copies:
        copy.wait()


def branch_kernel(nf_ref, taps_ref, bias_ref, mask_ref, *refs):
    pieces, (x_ref, conv_ref, w_ref, sems) = refs[:-4], refs[-4:]
    step = w_ref.shape[0] // 4
    copies = land(pieces, w_ref, sems)
    for i in range(4):
        rows = slice(i * step, (i + 1) * step)
        await_rows(copies, (i + 1) * step)
        part = nn(nf_ref[:, rows], w_ref[rows, :])
        x_ref[...] = part if i == 0 else x_ref[...] + part
    for c in range(0, x_ref.shape[1], 128):
        cols = slice(c, c + 128)
        x = x_ref[:, cols]
        total = x * taps_ref[0:1, cols] + bias_ref[:, cols]
        for lag in range(1, taps_ref.shape[0]):
            total = total + down_rows(x, lag) * mask_ref[lag - 1] * taps_ref[lag : lag + 1, cols]
        conv_ref[:, cols] = total.astype(bf16)


def mix_kernel(z_ref, nf_ref, hidden_ref, *refs):
    pieces = refs[:-9]
    y_ref, mixed_ref, o0, o1, o2, o3, total_ref, w_ref, sems = refs[-9:]
    width, half = y_ref.shape[1], len(pieces)
    step = w_ref.shape[1] // 4
    gate = land([p.at[:, pl.ds(0, width)] for p in pieces], w_ref.at[0], sems)
    out = land([p.at[:, pl.ds(width, width)] for p in pieces], w_ref.at[1], sems, half)
    for i in range(4):
        rows = slice(i * step, (i + 1) * step)
        await_rows(gate, (i + 1) * step)
        part = nn(nf_ref[:, rows], w_ref[0, rows, :])
        y_ref[...] = part if i == 0 else y_ref[...] + part
    for c in range(0, width, 128):
        cols = slice(c, c + 128)
        mixed_ref[:, cols] = (hidden_ref[:, cols] * gelu_pair(y_ref[:, cols])[0]).astype(bf16)
    for i in range(4):
        rows = slice(i * step, (i + 1) * step)
        await_rows(out, (i + 1) * step)
        total_ref[:, rows] = nt(mixed_ref[...], w_ref[1, rows, :])
    split_rows(z_ref, total_ref, (o0, o1, o2, o3))


def gates_of(rate, decay_logit, start):
    soft = softplus(-decay_logit)
    minus_log = 8.0 * rate * soft
    lost = one_less_exp(2.0 * minus_log)
    mult = jnp.where(start, 1.0, jnp.sqrt(lost))
    carried = jnp.where(start, 0.0, jnp.exp(-minus_log))
    return soft, mult, carried


def forward_scan_kernel(
    c0, c1, c2, c3, block_ref, rb_ref, ib_ref, dl_ref, mask_ref, rate_ref, entry_ref, hidden_ref
):
    start = mask_ref[0] == 0.0
    pre = nn(jnp.concatenate([c0[...], c1[...], c2[...], c3[...]], axis=1), block_ref[0])
    rate = sigmoid(pre[:, :128] + rb_ref[...])
    entry = sigmoid(pre[:, 128:] + ib_ref[...])
    _, mult, carried = gates_of(rate, dl_ref[...], start)
    driven = c0[...].astype(f32) * entry * mult
    rate_ref[...] = rate
    entry_ref[...] = entry
    hidden_ref[...] = scan_rows(carried, driven, down_rows)


def fetch(step, pieces, w_ref, sems):
    copies = []
    for side, group in enumerate(pieces):
        at = 0
        for piece in group:
            rows = piece.shape[0]
            cols = pl.ds(side * piece.shape[1], piece.shape[1])
            copies.append(
                pltpu.make_async_copy(piece, w_ref.at[pl.ds(at, rows), cols], sems.at[len(copies)])
            )
            at += rows

    @pl.when(step == 0)
    def _():
        for copy in copies:
            copy.start()

    return copies


def product(landing, left_ref, w_ref, total_ref):
    for copy in landing:
        copy.wait()
    rows = w_ref.shape[0] // 4
    for i in range(4):
        at = slice(i * rows, (i + 1) * rows)
        total_ref[:, at] = nt(left_ref[...], w_ref[at, :])


def backward_scan_kernel(count, z_ref, p0, p1, p2, p3, *refs):
    weights, refs = refs[:count], refs[count:]
    c0, c1, c2, c3, block_ref, dl_ref, y_ref, mask_ref, rate_ref, entry_ref, hidden_ref = refs[:11]
    g_ref, gy_ref, direct_ref, h1_ref, h2_ref, h3_ref, mine_ref, theirs_ref, sums_ref = refs[11:]

    @pl.when(pl.program_id(0) == 0)
    def _():
        assemble_kernel(z_ref, p0, p1, p2, p3, g_ref)

    start = mask_ref[0] == 0.0
    grad_mixed = nn(g_ref[...], jnp.concatenate([w[...] for w in weights], axis=0))
    hidden, rate, entry = hidden_ref[...], rate_ref[...], entry_ref[...]
    conv = c0[...].astype(f32)
    gelu_y, slope_y = gelu_pair(y_ref[...])
    gy_ref[...] = (grad_mixed * hidden * slope_y).astype(bf16)
    decay_logit = dl_ref[...]
    soft, mult, carried = gates_of(rate, decay_logit, start)
    state = scan_rows(up_rows(carried, 1), grad_mixed * gelu_y, up_rows)
    kept = carried * carried
    grad_log = jnp.where(
        start, 0.0, state * (down_rows(hidden, 1) * carried - conv * entry * kept / mult)
    )
    rate_low = (grad_log * (-8.0 * soft) * rate * (1.0 - rate)).astype(bf16)
    entry_low = (state * conv * mult * entry * (1.0 - entry)).astype(bf16)
    both = jnp.concatenate([rate_low, entry_low], axis=1)
    sums_ref[...] = jnp.concatenate(
        [
            jnp.sum(grad_log * rate, axis=0, keepdims=True) * (8.0 * sigmoid(-decay_logit)),
            jnp.sum(rate_low.astype(f32), axis=0, keepdims=True),
            jnp.sum(entry_low.astype(f32), axis=0, keepdims=True),
            jnp.zeros((5, 128), f32),
        ],
        axis=0,
    )
    heads = nt(both, block_ref[0])
    direct_ref[...] = state * entry * mult + heads[:, :128]
    h1_ref[...] = heads[:, 128:256].astype(bf16)
    h2_ref[...] = heads[:, 256:384]
    h3_ref[...] = heads[:, 384:].astype(bf16)
    units = jnp.concatenate([c0[...], c1[...], c2[...], c3[...]], axis=1)
    grads = tn(units, both)
    first = jnp.concatenate([grads[:, 0:64], grads[:, 128:192]], axis=1)
    second = jnp.concatenate([grads[:, 64:128], grads[:, 192:256]], axis=1)
    for k in range(4):
        even, odd = first[k * 128 : k * 128 + 64], second[k * 128 + 64 : k * 128 + 128]
        own = z_ref[1] % 2 == 0
        mine_ref[0, k] = jnp.where(own, even, odd).astype(bf16)
        theirs_ref[0, k] = jnp.where(own, odd, even).astype(bf16)


def conv_back_kernel(
    size, count, z_ref, direct_ref, r1, r2, x_ref, taps_ref, mask_ref, gy_ref, rel_ref, *refs
):
    weights, refs = refs[: 2 * count], refs[2 * count :]
    gx_ref, sums_ref, gain_ref, o0, o1, o2, o3, total_ref, w_ref, left_ref, sems = refs
    step, width = pl.program_id(0), left_ref.shape[1] // 2
    sides = (weights[:count], [w.at[:, pl.ds(0, width)] for w in weights[count:]])
    landing = fetch(step, sides, w_ref, sems)
    chan = left_ref.shape[1] // 2
    total = direct_ref[...] + r1[...].astype(f32) + r2[...].astype(f32)
    x = x_ref[...]
    grad = total * taps_ref[0:1]
    sums = [jnp.sum(total * x, axis=0, keepdims=True)]
    for lag in range(1, taps_ref.shape[0]):
        kept = total * mask_ref[lag - 1]
        grad = grad + up_rows(kept, lag) * taps_ref[lag : lag + 1]
        sums.append(jnp.sum(kept * down_rows(x, lag), axis=0, keepdims=True))
    low = grad.astype(bf16)
    gx_ref[...] = low
    sums.append(jnp.sum(total, axis=0, keepdims=True))
    sums.append(jnp.zeros((8 - len(sums), x.shape[1]), f32))
    sums_ref[...] = jnp.concatenate(sums, axis=0)
    left_ref[:, pl.ds(pl.multiple_of(step * 128, 128), 128)] = low
    left_ref[:, pl.ds(pl.multiple_of(chan + step * 128, 128), 128)] = gy_ref[...]

    @pl.when(step == pl.num_programs(0) - 1)
    def _():
        product(landing, left_ref, w_ref, total_ref)
        split_rows(z_ref, total_ref, (o0, o1, o2, o3))
        rel = rel_ref[...].astype(f32)
        inv = lax.rsqrt(jnp.mean(rel * rel, axis=1, keepdims=True) + eps)
        gain = jnp.sum(total_ref[...] * (rel * inv), axis=0, keepdims=True)
        gain_ref[...] = to_abs(z_ref[1], size, gain)


def split_rows(z_ref, total_ref, outs):
    rows = outs[0].shape[0]
    for k, out in enumerate(outs):
        at = pl.multiple_of((z_ref[0] ^ k) * rows, rows)
        out[...] = total_ref[pl.ds(at, rows), :].astype(out.dtype)


def assemble_kernel(z_ref, *refs):
    pieces, out_ref = refs[:-1], refs[-1]
    rows = pieces[0].shape[0]
    for k, piece in enumerate(pieces):
        at = pl.multiple_of((z_ref[0] ^ k) * rows, rows)
        out_ref[pl.ds(at, rows), :] = piece[...].astype(out_ref.dtype)


def to_abs(me, size, v):
    part = v.shape[1] // size

    def picked(v, places):
        return jnp.concatenate([v[:, p * part : (p + 1) * part] for p in places], axis=1)

    v = picked(v, [(s % 2) * (size // 2) + s // 2 for s in range(size)])
    bit = 1
    while bit < size:
        v = jnp.where((me // bit) % 2 == 1, picked(v, [s ^ bit for s in range(size)]), v)
        bit *= 2
    return v


def to_rel(me, size, v):
    part = v.shape[1] // size

    def picked(v, places):
        return jnp.concatenate([v[:, p * part : (p + 1) * part] for p in places], axis=1)

    bit = 1
    while bit < size:
        v = jnp.where((me // bit) % 2 == 1, picked(v, [s ^ bit for s in range(size)]), v)
        bit *= 2
    return picked(v, [2 * j + c for c in range(2) for j in range(size // 2)])


def sum_pieces(pieces):
    total = pieces[0][...]
    for piece in pieces[1:]:
        total = total + piece[...].astype(f32)
    return total


def my_rows(z_ref, ref, rows):
    return ref[pl.ds(pl.multiple_of(z_ref[0] * rows, rows), rows), :].astype(f32)


def norm_second_kernel(z_ref, x_ref, gain_ref, o0, o1, o2, res_ref, low_ref):
    residual = my_rows(z_ref, x_ref, res_ref.shape[0]) + sum_pieces((o0, o1, o2))
    inv = lax.rsqrt(jnp.mean(residual * residual, axis=1, keepdims=True) + eps)
    res_ref[...] = residual
    low_ref[...] = (residual * inv * gain_ref[...]).astype(bf16)


def norm_back(x, gain, grad):
    inv = lax.rsqrt(jnp.mean(x * x, axis=1, keepdims=True) + eps)
    unit = x * inv
    scaled = grad * gain
    out = inv * (scaled - unit * jnp.mean(scaled * unit, axis=1, keepdims=True))
    return out, jnp.sum(grad * unit, axis=0, keepdims=True)


def second_back_kernel(size, z_ref, cot_ref, gain_ref, res_ref, o0, o1, o2, gr_ref, low_ref, gain_out):
    grad, gain_grad = norm_back(res_ref[...], gain_ref[...], sum_pieces((o0, o1, o2)))
    grad = grad + my_rows(z_ref, cot_ref, res_ref.shape[0])
    gr_ref[...] = grad
    low_ref[...] = grad.astype(bf16)
    gain_out[...] = to_abs(z_ref[1], size, gain_grad)


def first_back_kernel(size, z_ref, x_ref, gain_ref, gr_ref, o0, o1, o2, out_ref):
    x = my_rows(z_ref, x_ref, gr_ref.shape[0])
    grad, _ = norm_back(x, gain_ref[...], sum_pieces((o0, o1, o2)))
    out_ref[...] = to_abs(z_ref[1], size, gr_ref[...] + grad).astype(bf16)


def block_out_kernel(size, z_ref, res_ref, o0, o1, o2, out_ref):
    out_ref[...] = to_abs(z_ref[1], size, res_ref[...] + sum_pieces((o0, o1, o2))).astype(bf16)


def ffn_kernel(groups, first, last, *refs):
    refs = list(refs)

    def take(n):
        taken = refs[:n]
        del refs[:n]
        return taken

    (z_ref,) = take(1)
    if first:
        pieces = take(4)
    else:
        s_any, in_grad = take(2)
    (cot_any,) = take(1)
    s_ref, cot_ref, pre_ref, back_ref, w_ref, acc_grad, sems, out_sems = refs[-8:]
    del refs[-8:]
    n_outs = 2 * groups + (4 if last else 1 + first)
    outs = refs[-n_outs:]
    del refs[-n_outs:]
    per = len(refs) // groups
    rows, width = w_ref.shape[1] // 4, back_ref.shape[1]
    copies = []

    def load(src, dst):
        copy = pltpu.make_async_copy(src, dst, sems.at[len(copies)])
        copy.start()
        copies.append(copy)
        return copy

    held = []
    if first:
        for k, piece in enumerate(pieces):
            count = piece.shape[0]
            at = pl.multiple_of((z_ref[0] ^ k) * count, count)
            held.append(load(piece, s_ref.at[pl.ds(at, count)]))
    else:
        held.append(load(s_any, s_ref))
    held.append(load(cot_any, cot_ref))
    landing = []
    for g in range(groups):
        at, marks = 0, []
        for piece in refs[g * per : (g + 1) * per]:
            marks.append((at, load(piece, w_ref.at[g, pl.ds(at, piece.shape[0])])))
            at += piece.shape[0]
        landing.append(marks)
    if not first:
        sums = load(in_grad, acc_grad)
    for copy in held:
        copy.wait()
    stores = []

    def store(src, dst):
        copy = pltpu.make_async_copy(src, dst, out_sems.at[len(stores)])
        copy.start()
        stores.append(copy)

    if first:
        store(s_ref, outs[2 * groups])
    for g in range(groups):
        ggu_ref, mid_ref = outs[2 * g : 2 * g + 2]
        for i in range(4):
            at = slice(i * rows, (i + 1) * rows)
            await_rows(landing[g], (i + 1) * rows)
            pre = nn(s_ref[:, at], w_ref[g, at, : 2 * width])
            back = nn(cot_ref[:, at], w_ref[g, at, 2 * width :])
            if i == 0:
                pre_ref[...] = pre
                back_ref[...] = back
            else:
                pre_ref[...] += pre
                back_ref[...] += back
        for c in range(0, width, 128):
            gate, up = pre_ref[:, c : c + 128], pre_ref[:, width + c : width + c + 128]
            back = back_ref[:, c : c + 128]
            gelu_gate, slope = gelu_pair(gate)
            mid_ref[:, c : c + 128] = (gelu_gate * up).astype(bf16)
            ggu_ref[:, c : c + 128] = (back * up * slope).astype(bf16)
            ggu_ref[:, width + c : width + c + 128] = (back * gelu_gate).astype(bf16)
        if g == 0 and not first:
            sums.wait()
        for i in range(4):
            at = slice(i * rows, (i + 1) * rows)
            grad = nt(ggu_ref[...], w_ref[g, at, : 2 * width])
            if first and g == 0:
                acc_grad[:, at] = grad
            else:
                acc_grad[:, at] += grad
            if g == groups - 1 and not last:
                cols = pl.ds(i * rows, rows)
                store(acc_grad.at[:, cols], outs[-1].at[:, cols])
    if last:
        split_rows(z_ref, acc_grad, outs[2:6])
    for copy in stores:
        copy.wait()


def ffn_out_kernel(counts, z_ref, *refs):
    groups = len(counts)
    mids, refs = refs[:groups], refs[groups:]
    own, pass_part, both, w_ref, total_ref, sems = refs[-6:]
    pieces, width = list(refs[:-6]), mids[0].shape[1]
    copies, ends = [], []
    for g in range(groups):
        at = 0
        for piece in [pieces.pop(0) for _ in range(counts[g])]:
            copy = pltpu.make_async_copy(
                piece.at[:, pl.ds(2 * width, width)], w_ref.at[g, pl.ds(at, piece.shape[0])],
                sems.at[len(copies)],
            )
            copy.start()
            copies.append(copy)
            at += piece.shape[0]
        ends.append(len(copies))
    rows = w_ref.shape[1] // 4
    for g in range(groups):
        for copy in copies[ends[g] - counts[g] : ends[g]]:
            copy.wait()
        for i in range(4):
            at = slice(i * rows, (i + 1) * rows)
            out = nt(mids[g][...], w_ref[g, at, :])
            total_ref[:, at] = out if g == 0 else total_ref[:, at] + out
    count = own.shape[0]
    split_rows(
        z_ref, total_ref,
        [own, both.at[pl.ds(count, count)], pass_part, both.at[pl.ds(0, count)]],
    )


def grads_out_kernel(sides, *refs):
    lefts, rights, out = refs[:sides], refs[sides : 2 * sides], refs[2 * sides]
    held, sems = refs[2 * sides + 1 :]
    step = held.shape[0] // 2
    stores = []
    for part in range(2):
        rows, at = slice(part * step, (part + 1) * step), 0
        for left, right in zip(lefts, rights):
            width = right.shape[1]
            held[rows, at : at + width] = tn(left[:, rows], right[...]).astype(bf16)
            at += width
        copy = pltpu.make_async_copy(
            held.at[pl.ds(part * step, step)], out.at[pl.ds(part * step, step)], sems.at[part]
        )
        copy.start()
        stores.append(copy)
    for copy in stores:
        copy.wait()


def grads_own_kernel(sides, room, *refs):
    lefts, rights = refs[:sides], refs[sides : 2 * sides]
    got_any, own, x_top, y_bot, send_x, send_y = refs[2 * sides : 2 * sides + 6]
    got, grads, low, sems = refs[2 * sides + 6 :]
    q = x_top.shape[0]
    loads = [
        pltpu.make_async_copy(
            got_any.at[pl.ds(part * 4 * q, 4 * q)], got.at[pl.ds(part * 4 * q, 4 * q)], sems.at[part]
        )
        for part in range(2)
    ]
    for copy in loads:
        copy.start()
    stores = []

    def store(src, row, count, dst, to):
        copy = pltpu.make_async_copy(
            src.at[pl.ds(row * q, count * q)], dst.at[pl.ds(to * q, count * q)],
            sems.at[2 + len(stores)],
        )
        copy.start()
        stores.append(copy)

    for part in range(2):
        rows, at = slice(part * 4 * q, (part + 1) * 4 * q), 0
        loads[part].wait()
        for left, right in zip(lefts, rights):
            cols = slice(at, at + right.shape[1])
            at += right.shape[1]
            grads[rows, cols] = tn(left[:, rows], right[...]) + got[rows, cols].astype(f32)
        if part == 0:
            low[:q, :] = grads[3 * q : 4 * q, :].astype(bf16)
            store(grads, 0, 2, own, 0)
            store(grads, 2, 1, x_top, 0)
            store(low, 0, 1, send_x, room + 1)
        else:
            low[q : 2 * q, :] = grads[4 * q : 5 * q, :].astype(bf16)
            low[2 * q :, :] = grads[6 * q :, :].astype(bf16)
            store(low, 1, 1, send_y, room + 1)
            store(grads, 5, 1, y_bot, 0)
            store(low, 2, 1, send_y, room)
            store(low, 3, 1, send_x, room)
    for copy in stores:
        copy.wait()


def relay_kernel(groups, has_next, *refs):
    refs = list(refs)
    out_x, out_y = refs[-2:]
    at = 0
    for _ in range(groups):
        x_top, y_bot, got_x, got_y = refs[:4]
        del refs[:4]
        q, cols = x_top.shape[0], slice(at, at + x_top.shape[1])
        out_x[:q, cols] = (x_top[...] + got_y[:, cols].astype(f32)).astype(bf16)
        out_y[:q, cols] = (y_bot[...] + got_x[:, cols].astype(f32)).astype(bf16)
        at += x_top.shape[1]
    at = 0
    for _ in range(has_next):
        send_x, send_y = refs[:2]
        del refs[:2]
        cols = slice(at, at + send_x.shape[1])
        out_x[q:, cols] = send_x[...]
        out_y[q:, cols] = send_y[...]
        at += send_x.shape[1]


def joined(own, got_x, got_y, last_x, last_y, at, cols):
    q = last_x.shape[0]
    top = own[:q, at] + got_y[:, cols].astype(f32) + last_x[:, cols].astype(f32)
    bottom = own[q:, at] + got_x[:, cols].astype(f32) + last_y[:, cols].astype(f32)
    return jnp.concatenate([top, bottom], axis=0)


def join_ffn_kernel(*refs):
    gate_ref, up_ref, down_ref = refs[-3:]
    for c in range(chunk_count):
        parts = refs[5 * c : 5 * c + 5]
        width = parts[0].shape[1] // 3
        at = slice(c * width, (c + 1) * width)
        gate, up, down = [slice(k * width, (k + 1) * width) for k in range(3)]
        gate_ref[:, at] = joined(*parts, gate, gate)
        up_ref[:, at] = joined(*parts, up, up)
        down_ref[:, at] = joined(*parts, down, down)


def add_kernel(a_ref, b_ref, out_ref):
    out_ref[...] = (a_ref[...].astype(f32) + b_ref[...].astype(f32)).astype(out_ref.dtype)


def small_kernel(units, sums_ref, by_y, taps_ref, bias_ref, rate_ref, input_ref, decay_ref, one_ref, two_ref):
    total = sums_ref[...] + by_y[...]
    heads, taps, _ = taps_ref.shape
    for h in range(heads):
        cols = slice(h * units, (h + 1) * units)
        taps_ref[h] = total[8 : 8 + taps, cols]
        bias_ref[h : h + 1, :] = total[8 + taps : 9 + taps, cols]
        rate_ref[h : h + 1, :] = total[1:2, cols]
        input_ref[h : h + 1, :] = total[2:3, cols]
        decay_ref[h : h + 1, :] = total[0:1, cols]
    wide = total.shape[1]
    for k in range(4):
        one_ref[k * wide : (k + 1) * wide] = total[16 + k]
        two_ref[k * wide : (k + 1) * wide] = total[20 + k]


def last_kernel(units, z_ref, *refs):
    x_ins, block_ins, gate_ins, small_ins, tok_ins = (
        refs[:5], refs[5:9], refs[9:13], refs[13:15], refs[15:19]
    )
    x_ref, block_ref, tok_ref, rate_ref, input_ref = refs[19:24]
    join_x_kernel(*x_ins, x_ref)
    assemble_kernel(z_ref, *block_ins, block_ref)
    assemble_kernel(z_ref, *tok_ins, tok_ref)
    gate_join_kernel(z_ref, *gate_ins, rate_ref, input_ref)
    small_kernel(units, *small_ins, *refs[24:])


def gate_join_kernel(z_ref, mine_ref, mine_got, other_ref, other_got, rate_ref, input_ref):
    pairs, _, units, _ = mine_ref.shape
    core = z_ref[1] % 2
    for src, got, head in ((mine_ref, mine_got, core), (other_ref, other_got, 1 - core)):
        for p in range(pairs):
            parts = [(src[p, z_ref[0] ^ k], got[p, z_ref[0] ^ k]) for k in range(4)]
            whole = jnp.concatenate([a.astype(f32) + b.astype(f32) for a, b in parts], axis=0)
            rate_ref[2 * p + head] = whole[:, :units].T
            input_ref[2 * p + head] = whole[:, units:].T


def relay_mixed_kernel(x_top, y_bot, got_x, got_y, send_x, send_y, out_x, out_y):
    q, width = x_top.shape[0], out_x.shape[1]
    for k in range(x_top.shape[1] // width):
        rows, cols = slice(k * q, (k + 1) * q), slice(k * width, (k + 1) * width)
        out_x[rows, :] = (x_top[:, cols] + got_y[:, cols].astype(f32)).astype(bf16)
        out_y[rows, :] = (y_bot[:, cols] + got_x[:, cols].astype(f32)).astype(bf16)
    out_x[(k + 1) * q :, :] = send_x[...]
    out_y[(k + 1) * q :, :] = send_y[...]


def join_yo_kernel(yo_own, yo_got_x, yo_got_y, y_x, y_y, o_x, o_y, y_ref, out_ref):
    width = y_ref.shape[0]
    first, second = slice(0, width), slice(width, 2 * width)
    y_ref[...] = joined(yo_own, yo_got_x[:, first], yo_got_y[:, first], y_x, y_y, first, first).T
    out_ref[...] = joined(
        yo_own, yo_got_x[:, second], yo_got_y[:, second], o_x, o_y, second, first
    ).T


def join_x_kernel(own, got_x, got_y, last_x, last_y, out_ref):
    cols = slice(0, out_ref.shape[0])
    out_ref[...] = joined(own, got_x, got_y, last_x, last_y, cols, cols).T


def exchange(v, axis, size, bit):
    return lax.ppermute(v, axis, [(i, i ^ bit) for i in range(size)])


def tie(*values):
    return lax.optimization_barrier(values)


def along(size, bit, v):
    return exchange(v, "dp", 8, bit) if size == 8 else v


def move(size, send_x, send_y):
    return along(size, 2, send_x), along(size, 4, send_y)


def gather_all(shard, size):
    mine, bit = shard, 2
    while bit < size:
        mine = jnp.concatenate([mine, exchange(mine, "dp", size, bit)], axis=0)
        bit *= 2
    return [mine], [exchange(mine, "dp", size, 1)]


class Scatter:
    def __init__(self, size, lefts, rights, name):
        self.size, self.name = size, name
        self.lefts, self.rights = lefts, rights
        self.model = lefts[0].shape[1]
        self.width = sum(r.shape[1] for r in rights)

    def halves(self, side):
        tokens = self.lefts[0].shape[0]
        return {i: block((tokens, self.model // 2), 0, side) for i in range(len(self.lefts))}

    def sibling(self, run):
        shape = (self.model // 2, self.width)
        return run(
            partial(grads_out_kernel, len(self.lefts)), [like(shape, bf16)],
            *self.lefts, *self.rights, specs=self.halves(1),
            out_specs=[pl.BlockSpec(memory_space=pl.ANY)],
            scratch=[pltpu.VMEM(shape, bf16), pltpu.SemaphoreType.DMA((2,))],
            name="grads_out_" + self.name,
        )[0]

    def swap(self, out):
        return exchange(out, "dp", self.size, 1)

    def own(self, run, got, room=0):
        q, w = self.model // 16, self.width
        sends = [like(((2 + room) * q, w), bf16)] * 2
        anywhere = pl.BlockSpec(memory_space=pl.ANY)
        specs = self.halves(0)
        specs[2 * len(self.lefts)] = anywhere
        return run(
            partial(grads_own_kernel, len(self.lefts), room),
            [like((2 * q, w), f32), like((q, w), f32), like((q, w), f32)] + sends,
            *self.lefts, *self.rights, got, specs=specs, out_specs=[anywhere] * 5,
            scratch=[
                pltpu.VMEM((8 * q, w), bf16), pltpu.VMEM((8 * q, w), f32), pltpu.VMEM((4 * q, w), bf16),
                pltpu.SemaphoreType.DMA((9,)),
            ],
            name="grads_own_" + self.name,
        )

    def join(self, cut):
        own, x_top, y_bot, from_x, from_y = cut
        q = x_top.shape[0]
        from_x, from_y = from_x[-2 * q :], from_y[-2 * q :]
        total = jnp.concatenate(
            [own, x_top, from_x[q:].astype(f32), from_y[q:].astype(f32), y_bot,
             from_y[:q].astype(f32), from_x[:q].astype(f32)],
            axis=0,
        )
        bit = self.size // 2
        while bit > 1:
            half = total.shape[0] // 2
            total = total[:half] + exchange(total[half:].astype(bf16), "dp", self.size, bit).astype(f32)
            bit //= 2
        return total


def relay(run, cuts, got, base, nexts, name):
    q = cuts[0][1].shape[0]
    width = sum(cut[1].shape[1] for cut in cuts)
    ins, specs, options = [], {}, {}
    for cut in cuts:
        ins += [cut[1], cut[2]]
        for v in got:
            specs[len(ins)] = block((q, v.shape[1]), base, 0)
            ins.append(v)
    if len(nexts) == 1:
        options = dict(
            alias={len(ins): 0, len(ins) + 1: 1}, out_specs=[block((q, width), 0, 0)] * 2
        )
        specs[len(ins)] = specs[len(ins) + 1] = pl.BlockSpec(memory_space=pl.ANY)
    for cut in nexts:
        ins += [cut[3], cut[4]]
    return run(
        partial(relay_kernel, len(cuts), 0 if len(nexts) == 1 else len(nexts)),
        [like((3 * q if nexts else q, width), bf16)] * 2, *ins, specs=specs, name=name, **options,
    )


def to_owner(part):
    return exchange(part, "tensor", 4, 1)


def pass_on(part, got):
    return exchange((part + got.astype(f32)).astype(bf16), "tensor", 4, 2)


class Order:
    def __init__(self):
        self.last = None

    def after(self, *values):
        if self.last is not None:
            values, _ = lax.optimization_barrier((values, self.last))
        return values if len(values) > 1 else values[0]

    def wait(self, *values):
        values = self.after(*values)
        self.last = jax.tree.leaves(values)[0]
        return values

    def run(self, kernel, outs, *args, **options):
        results = call(kernel, outs, *self.after(*args), **options)
        self.last = results[0]
        return results


def spread(piece):
    return exchange(piece, "tensor", 4, 2), exchange(piece, "tensor", 4, 1)


def neighbour(v):
    return exchange(v, "tensor", 4, 1)


def sum_over(v, axis, size, first=1, until=None):
    bit = first
    while bit < (until or size):
        v = v + exchange(v, axis, size, bit)
        bit *= 2
    return v


def sum_low(v, axis, size, first=1, until=None):
    bit = first
    while bit < (until or size):
        low = v.astype(bf16)
        v = low.astype(f32) + exchange(low, axis, size, bit).astype(f32)
        bit *= 2
    return v


def body(
    tokens, segments, first_gain, x_weight, y_weight, conv_weight, conv_bias, rate_weight,
    input_weight, rate_bias, input_bias, decay_logit, out_weight, second_gain, gate_weight,
    up_weight, down_weight, cotangent, dp_size,
):
    count, model = tokens.shape
    heads, _, units = rate_weight.shape
    chan = heads * units
    pairs = heads // 2
    taps = conv_weight.shape[0]
    hidden_units = gate_weight.shape[1]
    width = hidden_units // chunk_count
    me = lax.axis_index("dp")
    z = lax.axis_index("tensor").astype(jnp.int32)
    ids = jnp.stack([z, me.astype(jnp.int32)])
    part = model // dp_size
    q = model // 16
    rows = count // 4
    size = dp_size
    order = Order()
    after, wait, run = order.after, order.wait, order.run
    anywhere = pl.BlockSpec(memory_space=pl.ANY)
    lane = pl.BlockSpec((count, 128), lambda p: (0, p))
    line = pl.BlockSpec((1, 128), lambda p: (0, p))
    sums_spec = pl.BlockSpec((8, 128), lambda p: (0, p))
    block_spec = pl.BlockSpec((1, 8 * units, 4 * units), lambda p: (p, 0, 0))
    mask_spec = pl.BlockSpec((taps - 1, count, 128), lambda p: (0, 0, 0))
    pair_grid = dict(
        grid=(pairs,), cost_estimate=hint,
        compiler_params=pltpu.CompilerParams(vmem_limit_bytes=60 * MIB),
    )
    split_shapes = [like((rows, model), t) for t in (f32, bf16, f32, bf16)]
    split_specs = [pl.BlockSpec((rows, model), lambda p: (0, 0))] * 4
    total_scratch = [pltpu.VMEM((count, model), f32)]

    def sibling(v):
        return exchange(v, "dp", size, 1)

    def halves(by_x, by_y):
        half = by_x.shape[0] // 2
        lower, upper = move(size, by_y[half:], by_x[:half])
        return upper, lower

    def pieces_of(shard, *got):
        if size == 8:
            return [shard, *got[: len(got) // 2]], list(got[len(got) // 2 :])
        return gather_all(shard, size)

    def assemble(pieces, dtype, name, specs=None):
        return run(
            assemble_kernel, [like((count, model), dtype)], ids, *pieces, scalars=1, specs=specs,
            name=name,
        )[0]

    xs = x_weight.reshape(part, chan)
    x_x, x_y = move(size, xs, xs)
    x_s = sibling(xs)

    def ffn_shard(c):
        cols = block((part, width), 0, c)
        return run(
            shard_kernel, [like((part, 3 * width), bf16)], gate_weight, up_weight, down_weight.T,
            specs={0: cols, 1: cols, 2: cols}, name="shard",
        )[0]

    f0 = ffn_shard(0)
    y_after, out_after = after(y_weight, out_weight)
    yo = jnp.concatenate([y_after.reshape(part, chan), out_after.reshape(chan, part).T], axis=1)
    x_x, x_y, x_s, yo = wait(x_x, x_y, x_s, yo)

    x_top, x_bot = halves(x_x, x_y)
    x_sx, x_sy = sibling(x_x), sibling(x_y)
    x_rel, nf, gain_one, gain_two = run(
        partial(norm_first_kernel, size),
        [like((count, model), bf16)] * 2 + [like((1, model), f32)] * 2,
        ids, tokens, first_gain, second_gain, scalars=1,
        name="norm_first",
    )
    segs = after(segments)
    masks = jnp.stack(
        [
            jnp.concatenate([jnp.full((lag,), -1, jnp.int32), segs[:-lag]]) == segs
            for lag in range(1, taps)
        ]
    ).astype(f32)
    masks = jnp.broadcast_to(masks[:, :, None], (taps - 1, count, 128))
    taps_flat = conv_weight.reshape(taps, chan)
    bias_flat = conv_bias.reshape(1, chan)
    rate_flat, input_flat = rate_bias.reshape(1, chan), input_bias.reshape(1, chan)
    decay_flat = decay_logit.reshape(1, chan)
    masks, taps_flat, bias_flat, rate_flat, input_flat, decay_flat, x_top, x_bot, x_sx, x_sy = wait(
        masks, taps_flat, bias_flat, rate_flat, input_flat, decay_flat, x_top, x_bot, x_sx, x_sy
    )
    yo_x, yo_y = move(size, *after(yo, yo))
    x_st, x_sb = sibling(x_top), sibling(x_bot)
    x_st, x_sb = wait(x_st, x_sb)
    own_x, sib_x = pieces_of(xs, x_x, x_y, x_top, x_bot, x_s, x_sx, x_sy, x_st, x_sb)
    all_x = own_x + sib_x
    x_branch, conv_low = run(
        branch_kernel, [like((count, chan), f32), like((count, chan), bf16)],
        nf, taps_flat, bias_flat, masks, *all_x,
        specs={4 + i: anywhere for i in range(len(all_x))},
        scratch=[pltpu.VMEM((model, chan), bf16), pltpu.SemaphoreType.DMA((len(all_x),))],
        name="branch",
    )
    conv2, conv1 = spread(conv_low)
    yo_s = sibling(after(yo))
    f1 = ffn_shard(1)
    (blocks,) = run(
        blocks_kernel, [like((pairs, 8 * units, 4 * units), bf16)], ids,
        rate_weight.transpose(0, 2, 1), input_weight.transpose(0, 2, 1),
        scalars=1, name="gate_blocks",
    )
    conv2, conv1, yo_x, yo_y, yo_s = wait(conv2, conv1, yo_x, yo_y, yo_s)
    conv3 = neighbour(conv2)
    yo_top, yo_bot = halves(yo_x, yo_y)
    yo_sx, yo_sy = sibling(yo_x), sibling(yo_y)
    (cot_rel,) = run(
        partial(to_rel_kernel, size), [like((count, model), bf16)], ids, cotangent, scalars=1,
        name="cotangent",
    )
    conv3, yo_top, yo_bot, yo_sx, yo_sy = wait(conv3, yo_top, yo_bot, yo_sx, yo_sy)
    conv = [conv_low, conv1, conv2, conv3]
    f0_x, f0_y = move(size, *after(f0, f0))
    f0_s = sibling(after(f0))
    yo_st, yo_sb = sibling(yo_top), sibling(yo_bot)
    rate, entry, hidden = pl.pallas_call(
        forward_scan_kernel,
        in_specs=[lane] * 4 + [block_spec] + [line] * 3 + [mask_spec],
        out_specs=[lane] * 3,
        out_shape=[like((count, chan), f32)] * 3,
        name="forward_scan",
        **pair_grid,
    )(*conv, blocks, rate_flat, input_flat, decay_flat, masks)
    order.last = rate
    yo_st, yo_sb, f0_s, hidden = wait(yo_st, yo_sb, f0_s, hidden)
    own_yo, sib_yo = pieces_of(yo, yo_x, yo_y, yo_top, yo_bot, yo_s, yo_sx, yo_sy, yo_st, yo_sb)
    all_yo = own_yo + sib_yo
    y_branch, mixed, *parts = run(
        mix_kernel,
        [like((count, chan), f32), like((count, chan), bf16)] + split_shapes,
        ids, nf, hidden, *all_yo, scalars=1,
        specs={3 + i: anywhere for i in range(len(all_yo))},
        scratch=total_scratch
        + [pltpu.VMEM((2, model, chan), bf16), pltpu.SemaphoreType.DMA((2 * len(all_yo),))],
        name="mix",
    )
    got3 = to_owner(parts[3])
    f1_x, f1_y = move(size, f1, after(f1))
    got3, f0_x, f0_y = wait(got3, f0_x, f0_y)
    (low,) = run(add_kernel, [like((rows, model), bf16)], parts[2], got3, name="first_add")
    got2, got1 = exchange(low, "tensor", 4, 2), to_owner(after(parts[1]))
    f0_sx = sibling(f0_x)
    got2, got1, f1_x, f1_y, f0_sx = wait(got2, got1, f1_x, f1_y, f0_sx)
    f0_far, f1_far = along(size, 2, after(f0_y)), along(size, 4, f1_x)
    f1_sx, f1_sy, f0_sy = sibling(f1_x), sibling(f1_y), sibling(after(f0_y))
    residual, second_rows = run(
        norm_second_kernel, [like((rows, model), f32), like((rows, model), bf16)],
        ids, x_rel, gain_two, parts[0], got1, got2, scalars=1, name="norm_second",
    )
    second_rows, f1_sx, f1_sy, f0_sy = wait(second_rows, f1_sx, f1_sy, f0_sy)
    sec2, sec1 = spread(second_rows)
    f2 = ffn_shard(2)
    sec2, sec1 = wait(sec2, sec1)
    sec3 = neighbour(sec2)
    sec3, f0_far, f1_far = wait(sec3, f0_far, f1_far)
    f2_x, f2_y = move(size, *after(f2, f2))
    f0_sf, f1_sf, f1_s = sibling(f0_far), sibling(f1_far), sibling(after(f1))
    f0_sf, f1_sf, f1_s = wait(f0_sf, f1_sf, f1_s)
    f2_s = sibling(after(f2))

    def ffn(left, groups, sums, first, last, name):
        outs = [like((count, 2 * width), bf16), like((count, width), bf16)] * len(groups)
        out_specs = [full(v) for v in outs]
        if first:
            outs.append(like((count, model), bf16))
            out_specs.append(anywhere)
        if last:
            outs += split_shapes
            out_specs += [full(v) for v in split_shapes]
        else:
            outs.append(like((count, model), f32))
            out_specs.append(anywhere)
        weights = sum([own + sib for own, sib in groups], [])
        scratch = [
            pltpu.VMEM((count, model), bf16),
            pltpu.VMEM((count, model), bf16),
            pltpu.VMEM((count, 2 * width), f32),
            pltpu.VMEM((count, width), f32),
            pltpu.VMEM((len(groups), model, 3 * width), bf16),
            pltpu.VMEM((count, model), f32),
            pltpu.SemaphoreType.DMA((len(weights) + 6,)),
            pltpu.SemaphoreType.DMA((5,)),
        ]
        ins = [ids, *left, *sums, cot_rel, *weights]
        at = 1
        return run(
            partial(ffn_kernel, len(groups), first, last), outs, *ins, scalars=1, scratch=scratch,
            specs={i: anywhere for i in range(at, len(ins))}, out_specs=out_specs, name=name,
        )

    groups = [
        pieces_of(f0, f0_x, f0_y, f0_far, f0_s, f0_sx, f0_sy, f0_sf),
        pieces_of(f1, f1_x, f1_y, f1_far, f1_s, f1_sx, f1_sy, f1_sf),
    ]
    a, mid0, c, mid1, second, *sums = ffn(
        [second_rows, sec1, sec2, sec3], groups, [], True, False, "ffn_01"
    )
    b, d = mid0, mid1
    s0 = Scatter(size, [second, cot_rel], [a, b], "ffn_0")
    s1 = Scatter(size, [second, cot_rel], [c, d], "ffn_1")
    s0_out = s0.sibling(run)
    s0_out, f2_s, f2_x, f2_y = wait(s0_out, f2_s, f2_x, f2_y)
    f2_top, f2_bot = halves(f2_x, f2_y)
    f2_sx, f2_sy = sibling(f2_x), sibling(f2_y)
    s0_swap = s0.swap(s0_out)
    s1_out = s1.sibling(run)
    f2_sx, f2_sy, s0_swap = wait(f2_sx, f2_sy, s0_swap)
    s0_cut = s0.own(run, s0_swap)
    f2_top, f2_bot, s0_send = wait(f2_top, f2_bot, tuple(s0_cut[3:]))
    f2_st, f2_sb = sibling(f2_top), sibling(f2_bot)
    f2_st, f2_sb = wait(f2_st, f2_sb)
    s0_got = move(size, *after(*s0_send))
    s1_swap = s1.swap(after(s1_out))
    groups.append(pieces_of(f2, f2_x, f2_y, f2_top, f2_bot, f2_s, f2_sx, f2_sy, f2_st, f2_sb))
    a, b, *grad_parts = ffn([second], groups[2:], sums, False, True, "ffn_2")
    mid2 = b
    s2 = Scatter(size, [second, cot_rel], [a, b], "ffn_2")
    grad_parts, s1_swap = wait(tuple(grad_parts), s1_swap)

    got3, got1 = to_owner(grad_parts[3]), to_owner(grad_parts[1])
    s1_cut = s1.own(run, s1_swap)
    s2_out = s2.sibling(run)
    got3, s0_got, s2_out, s1_send = wait(got3, s0_got, s2_out, tuple(s1_cut[3:]))
    got2 = pass_on(grad_parts[2], got3)
    s1_got = move(size, *s1_send)
    s2_swap = s2.swap(s2_out)
    lists = [own + sib for own, sib in groups]
    ins = [ids, mid0, mid1, mid2, *sum(lists, [])]
    out_parts = run(
        partial(ffn_out_kernel, [len(v) for v in lists]),
        [like((rows, model), f32)] * 2 + [like((2 * rows, model), bf16)], *ins, scalars=1,
        specs={i: anywhere for i in range(4, len(ins))},
        scratch=[
            pltpu.VMEM((chunk_count, model, width), bf16), pltpu.VMEM((count, model), f32),
            pltpu.SemaphoreType.DMA((len(ins),)),
        ],
        name="ffn_out",
    )
    got2, got1, s2_swap = wait(got2, got1, s2_swap)
    grad_res, rec_rows, second_gain = run(
        partial(second_back_kernel, size),
        [like((rows, model), f32), like((rows, model), bf16), like((1, model), f32)],
        ids, cot_rel, gain_two, residual, grad_parts[0], got1, got2, scalars=1, micros=6, name="second_back",
    )
    rec2, rec1 = spread(rec_rows)
    s2_cut = s2.own(run, s2_swap, 1)
    sends = relay(run, [s0_cut], s0_got, 0, [s2_cut], "relay_0")
    rec2, rec1, s1_got, sends = wait(rec2, rec1, s1_got, tuple(sends))
    rec3 = neighbour(rec2)
    slot = move(size, *sends)
    rec3 = wait(rec3)
    out_got = neighbour(after(out_parts[2]))

    whole = pl.BlockSpec((count, model), lambda p: (0, 0))
    piece = pl.BlockSpec((rows, model), lambda p: (0, 0))
    gate_spec = pl.BlockSpec((1, 4, units, 2 * units), lambda p: (p, 0, 0, 0))
    gate_half = like((pairs, 4, units, 2 * units), bf16)
    grad_rec, grad_y, direct, h1, h2, h3, gate_mine, gate_theirs, scan_sums = pl.pallas_call(
        partial(backward_scan_kernel, len(all_yo)),
        in_specs=[smem] + [piece] * 4
        + [pl.BlockSpec((v.shape[0], 128), lambda p: (0, pairs + p)) for v in all_yo] + [lane] * 4
        + [block_spec, line, lane, mask_spec] + [lane] * 3,
        out_specs=[whole, lane, lane, lane, lane, lane, gate_spec, gate_spec, sums_spec],
        out_shape=[like((count, model), bf16)]
        + [like((count, chan), t) for t in (bf16, f32, bf16, f32, bf16)]
        + [gate_half, gate_half, like((8, chan), f32)],
        name="backward_scan",
        **pair_grid,
    )(
        *after(ids, rec_rows, rec1, rec2, rec3, *all_yo, *conv, blocks, decay_flat, y_branch, masks),
        rate, entry, hidden,
    )
    order.last = grad_rec
    out_got, h1, h2, h3 = wait(out_got, h1, h2, h3)
    got3 = to_owner(h3)
    gate_got = sibling(gate_theirs)
    syo = Scatter(size, [nf, grad_rec], [grad_y, mixed], "yo")
    syo_out = syo.sibling(run)
    s1_send = relay(run, [s1_cut], s1_got, 0, [], "relay_1")
    got3, syo_out, gate_got, s1_send = wait(got3, syo_out, gate_got, tuple(s1_send))
    got2, got1 = pass_on(h2, got3), to_owner(after(h1))
    (gate_sum,) = run(add_kernel, [gate_half], gate_mine, gate_got, name="gate_add")
    (out_low,) = run(
        add_kernel, [like((rows, model), bf16)], out_parts[1], out_got,
        specs={1: block((rows, model), 0, 0)}, name="out_add",
    )
    got2, got1, slot, out_low = wait(got2, got1, slot, out_low)
    out_got2 = exchange(out_low, "tensor", 4, 2)
    s1_last = move(size, *after(*s1_send))
    syo_swap = syo.swap(after(syo_out))
    gate_got = along(size, 2, after(gate_sum))
    whole_row = pl.BlockSpec((1, model), lambda p: (0, 0))
    grad_x, conv_sums, first_gain, *first_parts = pl.pallas_call(
        partial(conv_back_kernel, size, len(all_x)),
        in_specs=[smem] + [lane] * 4 + [pl.BlockSpec((taps, 128), lambda p: (0, p)), mask_spec, lane]
        + [whole] + [anywhere] * (2 * len(all_x)),
        out_specs=[lane, sums_spec, whole_row] + split_specs,
        out_shape=[like((count, chan), bf16), like((8, chan), f32), like((1, model), f32)]
        + split_shapes,
        scratch_shapes=total_scratch
        + [
            pltpu.VMEM((model, 2 * chan), bf16),
            pltpu.VMEM((count, 2 * chan), bf16),
            pltpu.SemaphoreType.DMA((2 * len(all_x),)),
        ],
        name="conv_back",
        **pair_grid,
    )(*after(ids, direct, got1, got2, x_branch, taps_flat, masks, grad_y, x_rel, *all_x, *all_yo))
    order.last = grad_x
    first_parts, syo_swap, out_got2 = wait(tuple(first_parts), syo_swap, out_got2)
    got3 = to_owner(first_parts[3])
    sx = Scatter(size, [nf], [grad_x], "x")
    sx_out = sx.sibling(run)
    syo_cut = syo.own(run, syo_swap)
    s2_send = relay(run, [s2_cut], slot, 1, [], "relay_2")
    got3, sx_out, yo_send, s1_last, gate_got, s2_send = wait(
        got3, sx_out, tuple(syo_cut[3:]), s1_last, gate_got, tuple(s2_send)
    )
    got2, got1 = pass_on(first_parts[2], got3), to_owner(after(first_parts[1]))
    sx_swap = sx.swap(sx_out)
    yo_got = move(size, *yo_send)
    got2, got1, sx_swap, yo_got = wait(got2, got1, sx_swap, yo_got)
    (tokens_rows,) = run(
        partial(first_back_kernel, size), [like((rows, model), bf16)],
        ids, x_rel, gain_one, grad_res, first_parts[0], got1, got2, scalars=1, name="first_back",
    )
    gains = jnp.concatenate([first_gain, second_gain], axis=0)
    tok2, tok1 = spread(tokens_rows)
    gains = sum_over(after(gains), "tensor", 4, 1, 2)
    s2_last = move(size, *after(*s2_send))
    sx_cut = sx.own(run, sx_swap)
    specs = {k: block((q, 2 * chan), 0, 0) for k in (2, 3)}
    mixed_sends = run(
        relay_mixed_kernel, [like((4 * q, chan), bf16)] * 2, syo_cut[1], syo_cut[2], *yo_got,
        *sx_cut[3:], specs=specs, name="relay_3",
    )
    (block_rows,) = run(
        partial(block_out_kernel, size), [like((rows, model), bf16)],
        ids, residual, out_parts[0], out_got, out_got2, scalars=1,
        specs={3: block((rows, model), 1, 0)}, name="block_out",
    )
    (gate_sum,) = run(add_kernel, [gate_half], gate_sum, gate_got, name="gate_add")
    tok2, tok1, s2_last, gains, mixed_sends = wait(tok2, tok1, s2_last, gains, tuple(mixed_sends))
    tok3 = neighbour(tok2)
    slot3 = move(size, *mixed_sends)
    block2 = exchange(after(block_rows), "tensor", 4, 2)
    gains = sum_over(gains, "tensor", 4, 2)
    if size == 8:
        ins, specs = [], {}
        for cut, (got, base), last in (
            (s0_cut, (s0_got, 0), slot), (s1_cut, (s1_got, 0), s1_last), (s2_cut, (slot, 1), s2_last)
        ):
            ins.append(cut[0])
            for v, at in ((got[0], base + 1), (got[1], base + 1), (last[0], 0), (last[1], 0)):
                specs[len(ins)] = block((q, v.shape[1]), at, 0)
                ins.append(v)
        gate_share, up_share, down_share = run(
            join_ffn_kernel,
            [like((part, hidden_units), f32)] * 3,
            *ins, specs=specs, name="join_ffn",
        )
    else:
        shares = [s0.join(s0_cut), s1.join(s1_cut), s2.join(s2_cut)]
        gate_share, up_share, down_share = [
            jnp.concatenate([v[:, k * width : (k + 1) * width] for v in shares], axis=1)
            for k in range(3)
        ]
    tok3, gains, slot3, block2 = wait(tok3, gains, slot3, block2)
    small = jnp.concatenate([scan_sums, conv_sums, gains.reshape(8, chan)], axis=0)
    small = sum_over(small, "dp", size, 1, 4)
    block13 = neighbour(jnp.concatenate([block_rows, block2], axis=0))
    gate_got = along(size, 4, after(gate_sum))
    x_last = move(size, *relay(run, [sx_cut], slot3, 2, [], "relay_4"))
    yo_ins = [syo_cut[0], *yo_got, *slot3, *slot3]
    if size == 8:
        specs = {1: block((q, 2 * chan), 1, 0), 2: block((q, 2 * chan), 1, 0)}
        for k, at in enumerate((0, 0, 1, 1)):
            specs[3 + k] = block((q, chan), at, 0)
        y_share, out_share = run(
            join_yo_kernel, [like((chan, part), f32)] * 2, *yo_ins, specs=specs, name="join_yo"
        )
    x_last, block13, small, gate_got = wait(x_last, block13, small, gate_got)
    block_ins = [block_rows, block13, block2, block13]
    block_specs = {2: block((rows, model), 0, 0), 4: block((rows, model), 1, 0)}
    if size == 8:
        by_y = exchange(small, "dp", size, 4)
        gate_other, got_other = sibling(gate_sum), sibling(gate_got)
        gate_other, got_other, by_y = wait(gate_other, got_other, by_y)
        ins = [ids, sx_cut[0], *slot3, *x_last, *block_ins, gate_sum, gate_got, gate_other, got_other]
        ins += [small, by_y, tokens_rows, tok1, tok2, tok3]
        specs = {k: block((q, chan), 3 if k < 4 else 0, 0) for k in range(2, 6)}
        specs.update({6 + k: v for k, v in ((1, block_specs[2]), (3, block_specs[4]))})
        head_like, gate_like = like((heads, units), f32), like((heads, units, 4 * units), f32)
        (
            x_share, block_out, tokens_grad, rate_grad, input_grad, taps_grad, bias_grad, rate_b_grad,
            input_b_grad, decay_grad, one_grad, two_grad,
        ) = run(
            partial(last_kernel, units),
            [like((chan, part), f32), like((count, model), bf16), like((count, model), f32)]
            + [gate_like, gate_like]
            + [like((heads, taps, units), f32)] + [head_like] * 4 + [like((model,), f32)] * 2,
            *ins, scalars=1, specs=specs, name="last",
        )
        rate_grad, input_grad = rate_grad.transpose(0, 2, 1), input_grad.transpose(0, 2, 1)
        taps_grad = taps_grad.transpose(1, 0, 2)
    else:
        block_out = assemble(block_ins, bf16, "block_out_all", block_specs)
        tokens_grad = assemble([tokens_rows, tok1, tok2, tok3], f32, "tokens_grad_all")
        small = sum_over(small, "dp", size, 4)
        taps_grad = small[8 : 8 + taps].reshape(taps, heads, units)
        bias_grad, rate_b_grad, input_b_grad, decay_grad = [
            small[k].reshape(heads, units) for k in (8 + taps, 1, 2, 0)
        ]
        one_grad, two_grad = small[16:20].reshape(model), small[20:].reshape(model)
        yo_share, x_share = syo.join(syo_cut), sx.join(sx_cut)
        x_share, y_share, out_share = x_share.T, yo_share[:, :chan].T, yo_share[:, chan:].T
        mine = sum_low(gate_mine + sibling(gate_theirs), "dp", size, 2)
        other, core = sibling(mine), me % 2
        gate_sum = jnp.stack(
            [jnp.where(core == 0, mine, other), jnp.where(core == 0, other, mine)], axis=1
        ).reshape(heads, 4, units, 2 * units)
        gate_sum = jnp.concatenate(
            [lax.dynamic_index_in_dim(gate_sum, z ^ k, 1, False) for k in range(4)], axis=1
        )
        rate_grad, input_grad = gate_sum[:, :, :units], gate_sum[:, :, units:]
    x_share = x_share.reshape(heads, units, part).transpose(2, 0, 1)
    y_share = y_share.reshape(heads, units, part).transpose(2, 0, 1)
    return (
        block_out,
        tokens_grad,
        one_grad,
        x_share,
        y_share,
        taps_grad,
        bias_grad,
        rate_grad,
        input_grad,
        rate_b_grad,
        input_b_grad,
        decay_grad,
        out_share.reshape(heads, units, part),
        two_grad,
        gate_share,
        up_share,
        down_share.T,
    )


def solution(mesh):
    return jax.shard_map(
        partial(body, dp_size=mesh.shape["dp"]),
        mesh=mesh,
        in_specs=(
            P("dp", None),
            P("dp"),
            P(),
            P("dp", None, "tensor"),
            P("dp", None, "tensor"),
            P(None, None, "tensor"),
            P(None, "tensor"),
            P(None, None, "tensor"),
            P(None, None, "tensor"),
            P(None, "tensor"),
            P(None, "tensor"),
            P(None, "tensor"),
            P(None, "tensor", "dp"),
            P(),
            P("dp", "tensor"),
            P("dp", "tensor"),
            P("tensor", "dp"),
            P("dp", None),
        ),
        out_specs=(
            P("dp", None),
            P("dp", None),
            P(),
            P("dp", None, "tensor"),
            P("dp", None, "tensor"),
            P(None, None, "tensor"),
            P(None, "tensor"),
            P(None, None, "tensor"),
            P(None, None, "tensor"),
            P(None, "tensor"),
            P(None, "tensor"),
            P(None, "tensor"),
            P(None, "tensor", "dp"),
            P(),
            P("dp", "tensor"),
            P("dp", "tensor"),
            P("tensor", "dp"),
        ),
        check_vma=False,
    )
```
